256 devices in a mesh: row: 8 (over y, z_lo), col: 32 (over x, z_hi, core).
Axes of the slice: x: 4, y: 4, z: 8 (z_hi: 4, z_lo: 2; z = z_hi * 2 + z_lo), core: 2. Of those that a mesh axis runs over, the one named last changes fastest.
Arguments:
- atoms: bfloat16 [393216, 128], P(('row', 'col')), may hold values from -48 to 48
- window_offsets: int32 [12288], P(('row', 'col')), may hold values from -64 to -32
- atom_token: int32 [393216], P(('row', 'col')), may hold values from 0 to 32767, as said below
- w_query: bfloat16 [128, 128], replicated, may hold values from -0.5 to 0.5
- w_key: bfloat16 [128, 128], replicated, may hold values from -0.5 to 0.5
- w_value: bfloat16 [128, 128], replicated, may hold values from -0.5 to 0.5
- w_out: bfloat16 [128, 128], replicated, may hold values from -0.5 to 0.5
- w_token: bfloat16 [128, 384], replicated, may hold values from -0.5 to 0.5
- gain_token: bfloat16 [384], replicated, may hold values from 0.099609375 to 1.8984375
- w_pair: bfloat16 [384, 320], replicated, may hold values from -0.3125 to 0.3125
- w_outer: bfloat16 [1024, 128], replicated, may hold values from -0.1875 to 0.1875
Outputs:
- pair_slab: bfloat16 [64, 32768, 128], P('row', 'col')
The draws below stay inside these ranges and needn't reach their ends.
Inputs may be any that keep to these rules, and one draw needn't show every extreme that they name: `atom_token`: Non-decreasing; token t's first atom lies between t*12 and t*12 + 11, and for t a positive multiple of 128 strictly after t*12; every token has at least one atom.
All inputs are finite; a program needn't handle non-finite values.
Results may differ from the reference program's by a relative error of at most 0.017.
Values may be sent and summed in bfloat16 or wider, within the bound.
A program may use at most 128 MiB of HBM per device.

```python
import jax
import jax.numpy as jnp
from jax import lax

AW = 128
HEADS = 4
TW = 384
CZ = 128
CO = 32
QB = 32
KW = 128
RIM = 64
APT = 12
TOK_DEV = 128
ATOMS = 393216
TOKENS = 32768
NBLK = 12288
SLAB = 64


def draw_atoms(key, part):
    key = jax.random.fold_in(key, 11)
    first_key = jax.random.fold_in(key, 0)
    result = jax.random.normal(first_key, (ATOMS, AW), jnp.float32)
    return jnp.clip(result, -48.0, 48.0).astype(jnp.bfloat16)


def draw_atom_token(key, part):
    key = jax.random.fold_in(key, 23)
    first_key, second_key = jax.random.split(key)
    tokens = jnp.arange(TOKENS, dtype=jnp.int32)
    jitter = jax.random.randint(first_key, (TOKENS,), 0, APT, dtype=jnp.int32)
    boundary_jitter = jax.random.randint(second_key, (TOKENS,), 1, APT, dtype=jnp.int32)
    boundary = (tokens % TOK_DEV == 0) & (tokens > 0)
    jitter = jnp.where(boundary, boundary_jitter, jitter)
    jitter = jnp.where(tokens == 0, 0, jitter)
    starts = tokens * APT + jitter
    marks = jnp.zeros((ATOMS,), jnp.int32).at[starts].add(1)
    return (jnp.cumsum(marks) - 1).astype(jnp.int32)


def with_ends(entries, rng, smallest, high):
    spot = [jax.random.randint(jax.random.fold_in(rng, axis), (), 0, length) for axis, length in enumerate(entries.shape)]
    widest = entries.shape.index(max(entries.shape))
    neighbour = spot[:widest] + [(spot[widest] + 1) % entries.shape[widest]] + spot[widest + 1:]
    return entries.at[tuple(spot)].set(smallest).at[tuple(neighbour)].set(high)


def gaussian(key, shape, scale, most, kind=jnp.bfloat16):
    return jnp.clip(scale * jax.random.normal(key, shape, jnp.float32), -most, most).astype(kind)


def setup_inputs(seed: int = 0) -> dict:
    arg_keys = jax.random.split(jax.random.key(seed), 12)
    atoms = draw_atoms(jax.random.fold_in(arg_keys[11], 71), 0)
    window_offsets = with_ends(jax.random.randint(arg_keys[1], (NBLK,), 0 - RIM, 1 - QB), jax.random.fold_in(arg_keys[1], 1), 0 - RIM, (1 - QB) - 1).astype(jnp.int32)
    atom_token = draw_atom_token(jax.random.fold_in(arg_keys[11], 71), 0)
    w_query = gaussian(arg_keys[3], (AW, AW), AW ** -0.5, 0.5)
    w_key = gaussian(arg_keys[4], (AW, AW), AW ** -0.5, 0.5)
    w_value = gaussian(arg_keys[5], (AW, AW), AW ** -0.5, 0.5)
    w_out = gaussian(arg_keys[6], (AW, AW), AW ** -0.5, 0.5)
    w_token = gaussian(arg_keys[7], (AW, TW), AW ** -0.5, 0.5)
    gain_token = jnp.clip(1.0 + 0.18 * jax.random.normal(arg_keys[8], (TW,), jnp.float32), 0.099609375, 1.8984375).astype(jnp.bfloat16)
    w_pair = gaussian(arg_keys[9], (TW, 2 * CZ + 2 * CO), TW ** -0.5, 0.3125)
    w_outer = gaussian(arg_keys[10], (CO * CO, CZ), (CO * CO) ** -0.5, 0.1875)
    return {"atoms": atoms, "window_offsets": window_offsets, "atom_token": atom_token, "w_query": w_query, "w_key": w_key, "w_value": w_value, "w_out": w_out, "w_token": w_token, "gain_token": gain_token, "w_pair": w_pair, "w_outer": w_outer}


def window_attend(queries, blocks, inside):
    features = queries.shape[-1]
    head_size = features // HEADS
    block_count = queries.shape[0] // QB
    query_heads = queries.reshape(block_count, QB, HEADS, head_size).astype(jnp.float32)
    key_heads = blocks[:, :, :features].reshape(block_count, KW, HEADS, head_size).astype(jnp.float32)
    value_heads = blocks[:, :, features:].reshape(block_count, KW, HEADS, head_size).astype(jnp.float32)
    scores = jnp.einsum('bqhd,bkhd->bhqk', query_heads, key_heads) * head_size ** (-0.5)
    scores = jnp.where(inside[:, None, None, :], scores, -1e+30)
    row_max = lax.optimization_barrier(jnp.max(scores, axis=-1, keepdims=True))
    lifted = jnp.exp(scores - row_max)
    weights = (lifted / lax.optimization_barrier(jnp.sum(lifted, axis=-1, keepdims=True))).astype(jnp.bfloat16)
    mixed_heads = jnp.einsum('bhqk,bkhd->bqhd', weights.astype(jnp.float32), value_heads)
    return mixed_heads.astype(jnp.bfloat16).reshape(block_count * QB, features)

def normalize(single, gain_token):
    centre = single - lax.optimization_barrier(jnp.mean(single, axis=1, keepdims=True))
    variance = lax.optimization_barrier(jnp.mean(centre * centre, axis=1, keepdims=True))
    return (centre * lax.rsqrt(variance + 1e-05) * gain_token.astype(jnp.float32)).astype(jnp.bfloat16)

def outer_pairs(left_rows, right_rows, w_outer):
    mixing = jnp.dot(left_rows[:, CZ:], w_outer.reshape(CO, CO * CZ), preferred_element_type=jnp.float32)
    mixing = mixing.astype(jnp.bfloat16).reshape(-1, CO, CZ)
    right_linear = right_rows[:, :CZ].astype(jnp.float32)
    right_outer = right_rows[:, CZ:].astype(jnp.float32)
    groups = left_rows.shape[0] // 8

    def row_group(pieces):
        mix_group, linear_group = pieces
        pair_grid = jnp.einsum('jn,inc->ijc', right_outer, mix_group.astype(jnp.float32))
        return (pair_grid + linear_group.astype(jnp.float32)[:, None, :] + right_linear[None]).astype(jnp.bfloat16)
    result = lax.map(row_group, (mixing.reshape(groups, 8, CO, CZ), left_rows[:, :CZ].reshape(groups, 8, CZ)))
    return result.reshape(left_rows.shape[0], right_rows.shape[0], CZ)

def reference(atoms, window_offsets, atom_token, w_query, w_key, w_value, w_out, w_token, gain_token, w_pair, w_outer):
    queries = jnp.dot(atoms, w_query, preferred_element_type=jnp.float32).astype(jnp.bfloat16)
    joined = jnp.concatenate([w_key, w_value], axis=1)
    key_values = jnp.dot(atoms, joined, preferred_element_type=jnp.float32).astype(jnp.bfloat16)
    padded = jnp.pad(key_values, ((RIM, RIM), (0, 0)))
    block_count = ATOMS // QB
    starts = jnp.arange(block_count, dtype=jnp.int32) * QB + window_offsets.astype(jnp.int32) + RIM
    window_index = starts[:, None] + jnp.arange(KW, dtype=jnp.int32)[None, :]
    blocks = padded[window_index]
    positions = window_index - RIM
    inside = (positions >= 0) & (positions < ATOMS)
    attended = window_attend(queries, blocks, inside)
    update = (atoms.astype(jnp.float32) + jnp.dot(attended, w_out, preferred_element_type=jnp.float32)).astype(jnp.bfloat16)
    hidden = jax.nn.relu(jnp.dot(update, w_token, preferred_element_type=jnp.float32)).astype(jnp.bfloat16)
    totals = jax.ops.segment_sum(hidden.astype(jnp.float32), atom_token, num_segments=TOKENS)
    counts = jax.ops.segment_sum(jnp.ones((ATOMS,), jnp.float32), atom_token, num_segments=TOKENS)
    token_norm = normalize(totals / counts[:, None], gain_token)
    projected = jnp.dot(token_norm, w_pair, preferred_element_type=jnp.float32).astype(jnp.bfloat16)
    left_rows = projected[:SLAB, :CZ + CO]
    right_rows = projected[:, CZ + CO:]
    return outer_pairs(left_rows, right_rows, w_outer)
```

```python
import jax
import jax.numpy as jnp
from jax import lax
from jax.experimental import pallas as pl
from jax.experimental.pallas import tpu as pltpu
from jax.sharding import PartitionSpec as P

AW = 128
HEADS = 4
TW = 384
CZ = 128
CO = 32
QB = 32
RIM = 64
ROWS = 8
COLS = 32
DEVICES = ROWS * COLS
ATOMS_DEV = 1536
TOK_DEV = 128
EXT = ATOMS_DEV + 2 * RIM
GROUP = 128
GROUPS = ATOMS_DEV // GROUP
KEYS = GROUP + 2 * RIM
HALF = 64
BLK = HALF + HALF // 4
WIDE = TW + 128
EXP_SCALE = float(32 ** -0.5 * 1.4426950408889634)
MESH = pl.DeviceIdType.MESH
NT = (((1,), (1,)), ((), ()))


def dot(a, b):
    return jnp.dot(a, b, preferred_element_type=jnp.float32)


def place(device):
    return (lax.div(device, COLS), lax.rem(device, COLS))


def attend_group(g, edge_low, edge_high, off, keys, queries, values, att):
    k = keys[GROUP * g : GROUP * g + KEYS, :]
    q = queries[:, GROUP * g : GROUP * g + GROUP]
    lane = lax.broadcasted_iota(jnp.int32, (1, GROUP), 1)
    start = jnp.zeros((1, GROUP), jnp.int32)
    for b in range(GROUP // QB):
        start = jnp.where(lane // QB == b, QB * b + RIM + off[GROUP // QB * g + b], start)
    key = lax.broadcasted_iota(jnp.int32, (KEYS, GROUP), 0)
    inside = (key >= start) & (key < start + 128)
    if g == 0:
        inside &= key >= edge_low
    if g == GROUPS - 1:
        inside &= key < edge_high
    bias = jnp.where(inside, 0.0, -1e30)
    zero = jnp.zeros((AW // HEADS, GROUP), jnp.bfloat16)
    outs = []
    for pair in range(2):
        sides = []
        for h in (2 * pair, 2 * pair + 1):
            head = [zero] * HEADS
            head[h] = q[32 * h : 32 * h + 32, :]
            sides.append(jnp.concatenate(head, axis=0))
        scores = dot(k, jnp.concatenate(sides, axis=1))
        scores = scores + jnp.concatenate([bias, bias], axis=1)
        top = jnp.max(scores, axis=0, keepdims=True)
        lifted = jnp.exp2((scores - top) * EXP_SCALE).astype(jnp.bfloat16)
        mixed = dot(values[pair, :, GROUP * g : GROUP * g + KEYS], lifted)
        scaled = mixed[:64] * (1.0 / mixed[64:65])
        outs += [scaled[:32, :GROUP], scaled[32:, GROUP:]]
    att[GROUP * g : GROUP * g + GROUP, :] = jnp.concatenate(outs, axis=0).T.astype(jnp.bfloat16)


def hidden_rows(lo, hi, ext, att, w_out, w_token, hid):
    mixed = dot(att[lo:hi, :], w_out[...])
    update = (ext[RIM + lo : RIM + hi, :].astype(jnp.float32) + mixed).astype(jnp.bfloat16)
    hid[lo:hi, :TW] = jnp.maximum(dot(update, w_token[...]), 0.0).astype(jnp.bfloat16)


def pooled_rows(first, count, lo, hi, device, token, hid):
    slot = token[:, lo:hi] - device * TOK_DEV
    rows = lax.broadcasted_iota(jnp.int32, (count, hi - lo), 0) + first
    one_hot = jnp.where(rows == slot, 1.0, 0.0).astype(jnp.bfloat16)
    return dot(one_hot, hid[lo:hi, :])


def token_normed(pooled, gain):
    count = pooled[:, TW:]
    single = pooled[:, :TW] / jnp.concatenate([count] * 3, axis=1)
    centre = single - jnp.mean(single, axis=1, keepdims=True)
    variance = jnp.mean(centre * centre, axis=1, keepdims=True)
    return (centre * lax.rsqrt(variance + 1e-05) * gain).astype(jnp.bfloat16)


def embed_kernel(
    atoms, off, token, wq, wk, wv, w_out, w_token_hbm, gain, w_pair_hbm,
    gathered, left_rows,
    ext, keys, queries, values, att, hid, w_token, w_pair, w_right,
    spill_out, spill_in, block, left_all, left_in,
    own_sem, load_sem, halo_send, halo_recv, spill_send, spill_recv,
    gather_send, gather_recv, left_send, left_recv, out_sem,
):
    row = lax.axis_index("row")
    col = lax.axis_index("col")
    me = row * COLS + col
    before = lax.rem(me + DEVICES - 1, DEVICES)
    after = lax.rem(me + 1, DEVICES)
    group_col = lax.div(me, ROWS)
    slot = lax.rem(me, ROWS)
    keeps = jnp.where(group_col == col, 1, 0)

    def signal(device):
        pl.semaphore_signal(barrier, inc=1, device_id=place(device), device_id_type=MESH)

    barrier = pltpu.get_barrier_semaphore()
    signal(before)
    signal(after)
    for k in range(ROWS):
        @pl.when(ROWS * col + k != me)
        def _():
            signal(ROWS * col + k)

    @pl.when(col != 0)
    def _():
        signal(row * COLS)

    @pl.when((col == 0) & (row != 0))
    def _():
        signal(0)

    own = pltpu.make_async_copy(atoms, ext.at[pl.ds(RIM, ATOMS_DEV)], own_sem)
    own.start()
    loads = [
        pltpu.make_async_copy(w_token_hbm, w_token, load_sem.at[0]),
        pltpu.make_async_copy(w_pair_hbm, w_pair, load_sem.at[1]),
    ]
    for load in loads:
        load.start()

    both = jnp.concatenate([wq[...], wv[...]], axis=1).astype(jnp.float32).T.astype(jnp.bfloat16)
    hid[:, TW:] = jnp.ones((ATOMS_DEV, WIDE - TW), jnp.bfloat16)
    for pair in range(2):
        values[pair, 64:, :] = jnp.ones((16, EXT), jnp.bfloat16)
    own.wait()
    for lo in range(0, ATOMS_DEV, 512):
        x = ext[RIM + lo : RIM + lo + 512, :]
        keys[RIM + lo : RIM + lo + 512, :] = dot(x, wk[...]).astype(jnp.bfloat16)
    for lo in range(128, ATOMS_DEV, 256):
        hi = min(lo + 256, ATOMS_DEV)
        x = ext[lo:hi, :]
        vt = lax.dot_general(both[AW:], x, NT, preferred_element_type=jnp.float32).astype(jnp.bfloat16)
        values[0, :64, lo:hi] = vt[:64]
        values[1, :64, lo:hi] = vt[64:]
    for lo in range(0, ATOMS_DEV, 512):
        x = ext[RIM + lo : RIM + lo + 512, :]
        queries[:, lo : lo + 512] = lax.dot_general(
            both[:AW], x, NT, preferred_element_type=jnp.float32
        ).astype(jnp.bfloat16)

    is_leader = jnp.where(col == 0, 1, 0)
    is_first = jnp.where(me == 0, 1, 0)
    pl.semaphore_wait(barrier, 2 + ROWS - keeps + (COLS - 1) * is_leader + (ROWS - 1) * is_first)

    halo = [
        pltpu.make_async_remote_copy(
            src_ref=atoms.at[pl.ds(ATOMS_DEV - RIM, RIM)], dst_ref=ext.at[pl.ds(0, RIM)],
            send_sem=halo_send.at[0], recv_sem=halo_recv.at[0],
            device_id=place(after), device_id_type=MESH,
        ),
        pltpu.make_async_remote_copy(
            src_ref=atoms.at[pl.ds(0, RIM)], dst_ref=ext.at[pl.ds(EXT - RIM, RIM)],
            send_sem=halo_send.at[1], recv_sem=halo_recv.at[1],
            device_id=place(before), device_id_type=MESH,
        ),
    ]
    for copy in halo:
        copy.start()

    edge_low = jnp.where(me == 0, RIM, 0)
    edge_high = jnp.where(me == DEVICES - 1, KEYS - RIM, KEYS)

    def attend(g):
        attend_group(g, edge_low, edge_high, off, keys, queries, values, att)

    for load in loads:
        load.wait()
    w_right[:, :CZ] = w_pair[:, CZ + CO : 2 * CZ + CO]
    w_right[:, CZ:] = jnp.concatenate([w_pair[:, 2 * CZ + CO :]] * 4, axis=1)

    for g in range(1, 6):
        attend(g)

    for copy in halo:
        copy.wait()
    for lo in (0, EXT - RIM):
        keys[lo : lo + RIM, :] = dot(ext[lo : lo + RIM, :], wk[...]).astype(jnp.bfloat16)
    for lo in (0, EXT - 128):
        vt = lax.dot_general(
            both[AW:], ext[lo : lo + 128, :], NT, preferred_element_type=jnp.float32
        ).astype(jnp.bfloat16)
        values[0, :64, lo : lo + 128] = vt[:64]
        values[1, :64, lo : lo + 128] = vt[64:]
    attend(0)
    attend(6)

    lane = lax.broadcasted_iota(jnp.int32, (16, CZ), 1)
    sends = []

    def finish(half, pooled):
        normed = token_normed(pooled, gain[...].astype(jnp.float32))
        right = dot(normed, w_right[...])
        packed = right[:16, CZ:]
        for m in range(1, 4):
            packed = jnp.where(lane // CO == m, right[16 * m : 16 * m + 16, CZ:], packed)
        block[half, :HALF, :] = right[:, :CZ].astype(jnp.bfloat16)
        block[half, HALF:, :] = packed.astype(jnp.bfloat16)
        for i in range(ROWS):
            to_row = lax.rem(slot + i, ROWS)
            copy = pltpu.make_async_remote_copy(
                src_ref=block.at[half], dst_ref=gathered.at[slot, half],
                send_sem=gather_send.at[half, i], recv_sem=gather_recv.at[half, slot],
                device_id=(to_row, group_col), device_id_type=MESH,
            )
            mine = (to_row == row) & (group_col == col)

            @pl.when(jnp.logical_not(mine))
            def _():
                copy.start()

            @pl.when(mine)
            def _():
                pltpu.make_async_copy(
                    block.at[half], gathered.at[slot, half], gather_send.at[half, i]
                ).start()

            sends.append((copy, mine, half, i))
        return normed

    hidden_rows(0, 896, ext, att, w_out, w_token, hid)
    pooled = pooled_rows(-16, 80, 0, 896, me, token, hid)
    spill_out[...] = pooled[8:16]
    spill = pltpu.make_async_remote_copy(
        src_ref=spill_out, dst_ref=spill_in, send_sem=spill_send, recv_sem=spill_recv,
        device_id=place(before), device_id_type=MESH,
    )
    spill.start()
    normed = finish(0, pooled[16:])

    def left_copy(source, to, index):
        return pltpu.make_async_remote_copy(
            src_ref=source, dst_ref=left_in, send_sem=left_send.at[index], recv_sem=left_recv,
            device_id=to, device_id_type=MESH,
        )

    @pl.when(me == 0)
    def _():
        left = dot(normed, w_pair[:, : 2 * CZ])
        for r in range(ROWS):
            rows = left[8 * r : 8 * r + 8]
            left_all[r] = jnp.concatenate([rows[:, :CZ], rows[:, CZ:]], axis=0).astype(jnp.bfloat16)
        left_in[...] = left_all[0]
        for r in range(1, ROWS):
            left_copy(left_all.at[r], (r, 0), r).start()

    for g in range(7, 12):
        attend(g)
    hidden_rows(896, ATOMS_DEV, ext, att, w_out, w_token, hid)
    pooled = pooled_rows(HALF, HALF, 768, ATOMS_DEV, me, token, hid)
    spill.wait()
    pooled = jnp.concatenate([pooled[:56], pooled[56:] + spill_in[...]], axis=0)
    finish(1, pooled)

    @pl.when(me == 0)
    def _():
        for r in range(1, ROWS):
            left_copy(left_all.at[r], (r, 0), r).wait_send()

    @pl.when(me != 0)
    def _():
        left_copy(left_in, (row, 0), 0).wait_recv()

    @pl.when(col == 0)
    def _():
        for c in range(1, COLS):
            left_copy(left_in, (row, c), c).start()
        for c in range(1, COLS):
            left_copy(left_in, (row, c), c).wait_send()

    result = pltpu.make_async_copy(left_in, left_rows, out_sem)
    result.start()
    for half in range(2):
        for k in range(ROWS):
            source = ROWS * col + k

            @pl.when(source != me)
            def _():
                pltpu.make_async_remote_copy(
                    src_ref=block.at[half], dst_ref=gathered.at[k, half],
                    send_sem=gather_send.at[half, 0], recv_sem=gather_recv.at[half, k],
                    device_id=place(source), device_id_type=MESH,
                ).wait_recv()

    for copy, mine, half, i in sends:
        @pl.when(jnp.logical_not(mine))
        def _():
            copy.wait_send()

        @pl.when(mine)
        def _():
            pltpu.make_async_copy(
                block.at[half], gathered.at[slot, half], gather_send.at[half, i]
            ).wait()
    result.wait()


def pair_kernel(gathered, left_rows, w_outer, out, base, result, sems):
    left = left_rows[:8, :]
    outer = left_rows[8:, :CO]
    spread = lax.broadcasted_iota(jnp.int32, (CO, CO * CO), 1) // CO
    spread = jnp.where(spread == lax.broadcasted_iota(jnp.int32, (CO, CO * CO), 0), 1.0, 0.0)
    wide = dot(outer, spread.astype(jnp.bfloat16))
    n = lax.broadcasted_iota(jnp.int32, (CO, CO * CO), 0)
    mine = lax.rem(lax.broadcasted_iota(jnp.int32, (CO, CO * CO), 1), CO) == n
    expanded = [jnp.where(mine, wide[i : i + 1], 0.0).astype(jnp.bfloat16) for i in range(8)]
    mixing = dot(jnp.concatenate(expanded, axis=0), w_outer[...]).astype(jnp.bfloat16)
    eye = jnp.where(
        lax.broadcasted_iota(jnp.int32, (CZ, CZ), 0) == lax.broadcasted_iota(jnp.int32, (CZ, CZ), 1), 1.0, 0.0
    ).astype(jnp.bfloat16)
    for i in range(8):
        base[:CZ, CZ * i : CZ * i + CZ] = eye
        for k in range(4):
            base[CZ + CO * k : CZ + CO * k + CO, CZ * i : CZ * i + CZ] = mixing[CO * i : CO * i + CO]
    left = left.astype(jnp.float32)
    lane = lax.broadcasted_iota(jnp.int32, (16, CZ), 1)
    copies = []
    for k in range(ROWS):
        parts = []
        for half in range(2):
            packed = gathered[k, half, HALF:, :].astype(jnp.float32)
            outer_rows = [jnp.where(lane // CO == m, packed, 0.0) for m in range(4)]
            outer_rows = jnp.concatenate(outer_rows, axis=0).astype(jnp.bfloat16)
            parts.append(jnp.concatenate([gathered[k, half, :HALF, :], outer_rows], axis=1))
        rows = jnp.concatenate(parts, axis=0)
        for i in range(0, 8, 2):
            grid = dot(rows, base[:, CZ * i : CZ * i + 2 * CZ])
            for j in range(2):
                total = grid[:, CZ * j : CZ * j + CZ] + left[i + j : i + j + 1]
                result[i + j, TOK_DEV * k : TOK_DEV * k + TOK_DEV, :] = total.astype(jnp.bfloat16)
        copy = pltpu.make_async_copy(
            result.at[:, pl.ds(TOK_DEV * k, TOK_DEV)], out.at[:, pl.ds(TOK_DEV * k, TOK_DEV)], sems.at[k]
        )
        copy.start()
        copies.append(copy)
    for copy in copies:
        copy.wait()


def body(
    atoms, window_offsets, atom_token, w_query, w_key, w_value, w_out, w_token, gain_token, w_pair, w_outer
):
    vmem = pl.BlockSpec(memory_space=pltpu.VMEM)
    smem = pl.BlockSpec(memory_space=pltpu.SMEM)
    anywhere = pl.BlockSpec(memory_space=pl.ANY)
    dma = pltpu.SemaphoreType.DMA
    bf16, f32 = jnp.bfloat16, jnp.float32
    gathered, left_rows = pl.pallas_call(
        embed_kernel,
        out_shape=[
            jax.ShapeDtypeStruct((ROWS, 2, BLK, CZ), bf16),
            jax.ShapeDtypeStruct((16, CZ), bf16),
        ],
        in_specs=[anywhere, smem, vmem, vmem, vmem, vmem, vmem, anywhere, vmem, anywhere],
        out_specs=[anywhere, anywhere],
        scratch_shapes=[
            pltpu.VMEM((EXT, AW), bf16),
            pltpu.VMEM((EXT, AW), bf16),
            pltpu.VMEM((AW, ATOMS_DEV), bf16),
            pltpu.VMEM((2, 80, EXT), bf16),
            pltpu.VMEM((ATOMS_DEV, AW), bf16),
            pltpu.VMEM((ATOMS_DEV, WIDE), bf16),
            pltpu.VMEM((AW, TW), bf16),
            pltpu.VMEM((TW, 2 * CZ + 2 * CO), bf16),
            pltpu.VMEM((TW, 2 * CZ), bf16),
            pltpu.VMEM((8, WIDE), f32),
            pltpu.VMEM((8, WIDE), f32),
            pltpu.VMEM((2, BLK, CZ), bf16),
            pltpu.VMEM((ROWS, 16, CZ), bf16),
            pltpu.VMEM((16, CZ), bf16),
            dma, dma((2,)), dma((2,)), dma((2,)), dma, dma,
            dma((2, ROWS)), dma((2, ROWS)), dma((COLS,)), dma, dma,
        ],
        compiler_params=pltpu.CompilerParams(
            collective_id=0, has_side_effects=True, vmem_limit_bytes=32 * 1024 * 1024
        ),
        name="embed",
    )(
        atoms, window_offsets, atom_token.reshape(1, -1), w_query, w_key, w_value, w_out, w_token,
        gain_token.reshape(1, -1), w_pair,
    )
    return pl.pallas_call(
        pair_kernel,
        out_shape=jax.ShapeDtypeStruct((8, ROWS * TOK_DEV, CZ), bf16),
        in_specs=[vmem, vmem, vmem],
        out_specs=anywhere,
        scratch_shapes=[
            pltpu.VMEM((2 * CZ, 8 * CZ), bf16),
            pltpu.VMEM((8, ROWS * TOK_DEV, CZ), bf16),
            dma((ROWS,)),
        ],
        compiler_params=pltpu.CompilerParams(vmem_limit_bytes=32 * 1024 * 1024),
        name="pair",
    )(gathered, left_rows, w_outer)


def solution(mesh):
    split = P(("row", "col"))
    placed = (P(("row", "col"), None), split, split) + (P(),) * 8
    return jax.shard_map(
        body, mesh=mesh, in_specs=placed, out_specs=P("row", "col", None), check_vma=False
    )
```

```python
import jax
import jax.numpy as jnp
from jax import lax
from jax.experimental import pallas as pl
from jax.experimental.pallas import tpu as pltpu
from jax.sharding import PartitionSpec as P

AW = 128
HEADS = 4
TW = 384
CZ = 128
CO = 32
QB = 32
RIM = 64
ROWS = 8
COLS = 32
DEVICES = ROWS * COLS
ATOMS_DEV = 1536
TOK_DEV = 128
EXT = ATOMS_DEV + 2 * RIM
GROUP = 128
GROUPS = ATOMS_DEV // GROUP
KEYS = GROUP + 2 * RIM
HALF = 64
BLK = HALF + HALF // 4
WIDE = TW + 128
EXP_SCALE = float(32 ** -0.5 * 1.4426950408889634)
MESH = pl.DeviceIdType.MESH
NT = (((1,), (1,)), ((), ()))


def dot(a, b):
    return jnp.dot(a, b, preferred_element_type=jnp.float32)


def place(device):
    return (lax.div(device, COLS), lax.rem(device, COLS))


def attend_group(g, edge_low, edge_high, off, keys, queries, values, att):
    k = keys[GROUP * g : GROUP * g + KEYS, :]
    q = queries[:, GROUP * g : GROUP * g + GROUP]
    lane = lax.broadcasted_iota(jnp.int32, (1, GROUP), 1)
    start = jnp.zeros((1, GROUP), jnp.int32)
    for b in range(GROUP // QB):
        start = jnp.where(lane // QB == b, QB * b + RIM + off[GROUP // QB * g + b], start)
    key = lax.broadcasted_iota(jnp.int32, (KEYS, GROUP), 0)
    inside = (key >= start) & (key < start + 128)
    if g == 0:
        inside &= key >= edge_low
    if g == GROUPS - 1:
        inside &= key < edge_high
    bias = jnp.where(inside, 0.0, -1e30)
    zero = jnp.zeros((AW // HEADS, GROUP), jnp.bfloat16)
    outs = []
    for pair in range(2):
        sides = []
        for h in (2 * pair, 2 * pair + 1):
            head = [zero] * HEADS
            head[h] = q[32 * h : 32 * h + 32, :]
            sides.append(jnp.concatenate(head, axis=0))
        scores = dot(k, jnp.concatenate(sides, axis=1))
        scores = scores + jnp.concatenate([bias, bias], axis=1)
        top = jnp.max(scores, axis=0, keepdims=True)
        lifted = jnp.exp2((scores - top) * EXP_SCALE).astype(jnp.bfloat16)
        mixed = dot(values[pair, :, GROUP * g : GROUP * g + KEYS], lifted)
        scaled = mixed[:64] * (1.0 / mixed[64:65])
        outs += [scaled[:32, :GROUP], scaled[32:, GROUP:]]
    att[GROUP * g : GROUP * g + GROUP, :] = jnp.concatenate(outs, axis=0).T.astype(jnp.bfloat16)


def hidden_rows(lo, hi, ext, att, w_out, w_token, hid):
    mixed = dot(att[lo:hi, :], w_out[...])
    update = (ext[RIM + lo : RIM + hi, :].astype(jnp.float32) + mixed).astype(jnp.bfloat16)
    hid[lo:hi, :TW] = jnp.maximum(dot(update, w_token[...]), 0.0).astype(jnp.bfloat16)


def pooled_rows(first, count, lo, hi, device, token, hid):
    slot = token[...].reshape(1, ATOMS_DEV)[:, lo:hi] - device * TOK_DEV
    rows = lax.broadcasted_iota(jnp.int32, (count, hi - lo), 0) + first
    one_hot = jnp.where(rows == slot, 1.0, 0.0).astype(jnp.bfloat16)
    return dot(one_hot, hid[lo:hi, :])


def token_normed(pooled, gain):
    count = pooled[:, TW:]
    single = pooled[:, :TW] / jnp.concatenate([count] * 3, axis=1)
    centre = single - jnp.mean(single, axis=1, keepdims=True)
    variance = jnp.mean(centre * centre, axis=1, keepdims=True)
    return (centre * lax.rsqrt(variance + 1e-05) * gain).astype(jnp.bfloat16)


def embed_kernel(
    atoms, off_hbm, token_hbm, wq_hbm, wk_hbm, wv_hbm, w_out_hbm, w_token_hbm, gain_hbm, w_pair_hbm,
    gathered, left_rows,
    off, token, wq, wk, wv, w_out, w_token, gain, w_pair,
    ext, keys, queries, values, att, hid, w_right,
    spill_out, spill_in, block, left_all, left_in,
    own_sem, load_sem, halo_send, halo_recv, spill_send, spill_recv,
    first_send, first_recv, local_sem, pass_send, pass_recv, left_send, left_recv, out_sem,
):
    row = lax.axis_index("row")
    col = lax.axis_index("col")
    me = row * COLS + col
    before = lax.rem(me + DEVICES - 1, DEVICES)
    after = lax.rem(me + 1, DEVICES)
    group_col = lax.div(me, ROWS)
    slot = lax.rem(me, ROWS)
    my_y, my_z = lax.div(row, 2), lax.rem(row, 2)
    relay_y = lax.rem(lax.div(col, 8) + lax.div(slot, 2), 4)
    held = 2 * lax.rem(my_y + 4 - lax.rem(col, 4), 4)
    keeps = jnp.where((group_col == col) & (relay_y == my_y), 1, 0)

    def signal(device):
        pl.semaphore_signal(barrier, inc=1, device_id=place(device), device_id_type=MESH)

    barrier = pltpu.get_barrier_semaphore()
    signal(before)
    signal(after)
    for k in range(2):
        @pl.when(ROWS * col + held + k != me)
        def _():
            signal(ROWS * col + held + k)
    for i in range(1, 4):
        signal((2 * lax.rem(my_y + i, 4) + my_z) * COLS + col)

    @pl.when(lax.rem(col, 8) != 0)
    def _():
        signal(me - lax.rem(col, 8))

    @pl.when((lax.rem(col, 8) == 0) & (col != 0))
    def _():
        signal(row * COLS)

    @pl.when((col == 0) & (row != 0))
    def _():
        signal(0)

    own = pltpu.make_async_copy(atoms, ext.at[pl.ds(RIM, ATOMS_DEV)], own_sem)
    own.start()
    pieces = [
        (wq_hbm, wq), (wk_hbm, wk), (wv_hbm, wv), (off_hbm, off), (w_out_hbm, w_out),
        (token_hbm, token), (w_token_hbm, w_token), (gain_hbm, gain), (w_pair_hbm, w_pair),
    ]
    loads = [pltpu.make_async_copy(a, b, load_sem.at[i]) for i, (a, b) in enumerate(pieces)]
    for load in loads:
        load.start()
    for load in loads[:3]:
        load.wait()

    both = jnp.concatenate([wq[...], wv[...]], axis=1).astype(jnp.float32).T.astype(jnp.bfloat16)
    hid[:, TW:] = jnp.ones((ATOMS_DEV, WIDE - TW), jnp.bfloat16)
    for pair in range(2):
        values[pair, 64:, :] = jnp.ones((16, EXT), jnp.bfloat16)
    own.wait()
    for lo in range(0, ATOMS_DEV, 512):
        x = ext[RIM + lo : RIM + lo + 512, :]
        keys[RIM + lo : RIM + lo + 512, :] = dot(x, wk[...]).astype(jnp.bfloat16)
    for lo in range(128, ATOMS_DEV, 256):
        hi = min(lo + 256, ATOMS_DEV)
        x = ext[lo:hi, :]
        vt = lax.dot_general(both[AW:], x, NT, preferred_element_type=jnp.float32).astype(jnp.bfloat16)
        values[0, :64, lo:hi] = vt[:64]
        values[1, :64, lo:hi] = vt[64:]
    for lo in range(0, ATOMS_DEV, 512):
        x = ext[RIM + lo : RIM + lo + 512, :]
        queries[:, lo : lo + 512] = lax.dot_general(
            both[:AW], x, NT, preferred_element_type=jnp.float32
        ).astype(jnp.bfloat16)

    is_head = jnp.where(lax.rem(col, 8) == 0, 1, 0)
    is_leader = jnp.where(col == 0, 1, 0)
    is_first = jnp.where(me == 0, 1, 0)
    pl.semaphore_wait(barrier, 2 + 2 - keeps + 3 + 7 * is_head + 3 * is_leader + 7 * is_first)

    halo = [
        pltpu.make_async_remote_copy(
            src_ref=atoms.at[pl.ds(ATOMS_DEV - RIM, RIM)], dst_ref=ext.at[pl.ds(0, RIM)],
            send_sem=halo_send.at[0], recv_sem=halo_recv.at[0],
            device_id=place(after), device_id_type=MESH,
        ),
        pltpu.make_async_remote_copy(
            src_ref=atoms.at[pl.ds(0, RIM)], dst_ref=ext.at[pl.ds(EXT - RIM, RIM)],
            send_sem=halo_send.at[1], recv_sem=halo_recv.at[1],
            device_id=place(before), device_id_type=MESH,
        ),
    ]
    for copy in halo:
        copy.start()

    edge_low = jnp.where(me == 0, RIM, 0)
    edge_high = jnp.where(me == DEVICES - 1, KEYS - RIM, KEYS)

    def attend(g):
        attend_group(g, edge_low, edge_high, off, keys, queries, values, att)

    for load in loads[3:]:
        load.wait()
    w_right[:CZ, :] = w_pair[CZ + CO : 2 * CZ + CO, :]
    for m in range(4):
        w_right[CZ + CO * m : CZ + CO * m + CO, :] = w_pair[2 * CZ + CO :, :]

    for g in range(1, 6):
        attend(g)

    for copy in halo:
        copy.wait()
    for lo in (0, EXT - RIM):
        keys[lo : lo + RIM, :] = dot(ext[lo : lo + RIM, :], wk[...]).astype(jnp.bfloat16)
    for lo in (0, EXT - 128):
        vt = lax.dot_general(
            both[AW:], ext[lo : lo + 128, :], NT, preferred_element_type=jnp.float32
        ).astype(jnp.bfloat16)
        values[0, :64, lo : lo + 128] = vt[:64]
        values[1, :64, lo : lo + 128] = vt[64:]
    attend(0)
    attend(6)

    lane = lax.broadcasted_iota(jnp.int32, (16, CZ), 1)

    def first_copy(half, i):
        return pltpu.make_async_remote_copy(
            src_ref=block.at[half], dst_ref=gathered.at[half, slot],
            send_sem=first_send.at[half, i], recv_sem=first_recv.at[half, lax.rem(slot, 2)],
            device_id=(2 * relay_y + i, group_col), device_id_type=MESH,
        )

    def local_copy(half):
        return pltpu.make_async_copy(block.at[half], gathered.at[half, slot], local_sem.at[half])

    def pass_copy(half, i, start):
        return pltpu.make_async_remote_copy(
            src_ref=gathered.at[half, pl.ds(start, 2)], dst_ref=gathered.at[half, pl.ds(start, 2)],
            send_sem=pass_send.at[half, i], recv_sem=pass_recv.at[half, i],
            device_id=(2 * lax.rem(my_y + i, 4) + my_z, col), device_id_type=MESH,
        )

    def pass_on(half):
        for k in range(2):
            @pl.when(ROWS * col + held + k != me)
            def _():
                pltpu.make_async_remote_copy(
                    src_ref=block.at[half], dst_ref=gathered.at[half, held + k],
                    send_sem=first_send.at[half, 0], recv_sem=first_recv.at[half, k],
                    device_id=place(ROWS * col + held + k), device_id_type=MESH,
                ).wait_recv()

        @pl.when(keeps == 1)
        def _():
            local_copy(half).wait()

        for i in range(1, 4):
            pass_copy(half, i, held).start()

    def finish(half, pooled):
        normed = token_normed(pooled, gain[...].reshape(1, TW).astype(jnp.float32))
        right = lax.dot_general(normed, w_right[...], NT, preferred_element_type=jnp.float32)
        packed = right[:16, CZ:]
        for m in range(1, 4):
            packed = jnp.where(lane // CO == m, right[16 * m : 16 * m + 16, CZ:], packed)
        block[half, :HALF, :] = right[:, :CZ].astype(jnp.bfloat16)
        block[half, HALF:, :] = packed.astype(jnp.bfloat16)
        for i in range(2):
            copy = first_copy(half, i)
            mine = (keeps == 1) & (my_z == i)

            @pl.when(jnp.logical_not(mine))
            def _():
                copy.start()

            @pl.when(mine)
            def _():
                local_copy(half).start()

        return normed

    hidden_rows(0, 896, ext, att, w_out, w_token, hid)
    pooled = pooled_rows(-16, 80, 0, 896, me, token, hid)
    spill_out[...] = pooled[8:16]
    spill = pltpu.make_async_remote_copy(
        src_ref=spill_out, dst_ref=spill_in, send_sem=spill_send, recv_sem=spill_recv,
        device_id=place(before), device_id_type=MESH,
    )
    spill.start()
    normed = finish(0, pooled[16:])

    def left_copy(source, to, index):
        return pltpu.make_async_remote_copy(
            src_ref=source, dst_ref=left_in, send_sem=left_send.at[index], recv_sem=left_recv,
            device_id=to, device_id_type=MESH,
        )

    @pl.when(me == 0)
    def _():
        left = lax.dot_general(normed, w_pair[: 2 * CZ, :], NT, preferred_element_type=jnp.float32)
        for r in range(ROWS):
            rows = left[8 * r : 8 * r + 8]
            left_all[r] = jnp.concatenate([rows[:, :CZ], rows[:, CZ:]], axis=0).astype(jnp.bfloat16)
        left_in[...] = left_all[0]
        for r in range(1, ROWS):
            left_copy(left_all.at[r], (r, 0), r).start()

    for g in range(7, 12):
        attend(g)
    hidden_rows(896, ATOMS_DEV, ext, att, w_out, w_token, hid)
    pooled = pooled_rows(HALF, HALF, 768, ATOMS_DEV, me, token, hid)
    spill.wait()
    pooled = jnp.concatenate([pooled[:56], pooled[56:] + spill_in[...]], axis=0)
    finish(1, pooled)

    @pl.when(me == 0)
    def _():
        for r in range(1, ROWS):
            left_copy(left_all.at[r], (r, 0), r).wait_send()

    @pl.when(me != 0)
    def _():
        left_copy(left_in, (row, 0), 0).wait_recv()

    @pl.when(col == 0)
    def _():
        for x in range(1, 4):
            left_copy(left_in, (row, 8 * x), 8 + x).start()

    @pl.when(lax.rem(col, 8) == 0)
    def _():
        for c in range(1, 8):
            left_copy(left_in, (row, col + c), 16 + c).start()

    result = pltpu.make_async_copy(left_in, left_rows, out_sem)
    result.start()
    for half in range(2):
        pass_on(half)

    for half in range(2):
        for i in range(1, 4):
            theirs = 2 * lax.rem(my_y + 4 - i + 4 - lax.rem(col, 4), 4)
            pass_copy(half, i, theirs).wait_recv()
            pass_copy(half, i, held).wait_send()
        for i in range(2):
            @pl.when(jnp.logical_not((keeps == 1) & (my_z == i)))
            def _():
                first_copy(half, i).wait_send()

    @pl.when(col == 0)
    def _():
        for x in range(1, 4):
            left_copy(left_in, (row, 8 * x), 8 + x).wait_send()

    @pl.when(lax.rem(col, 8) == 0)
    def _():
        for c in range(1, 8):
            left_copy(left_in, (row, col + c), 16 + c).wait_send()

    result.wait()


def pair_kernel(gathered, left_rows, w_outer, out, base, result, sems):
    left = left_rows[:8, :]
    outer = left_rows[8:, :CO]
    spread = lax.broadcasted_iota(jnp.int32, (CO, CO * CO), 1) // CO
    spread = jnp.where(spread == lax.broadcasted_iota(jnp.int32, (CO, CO * CO), 0), 1.0, 0.0)
    wide = dot(outer, spread.astype(jnp.bfloat16))
    n = lax.broadcasted_iota(jnp.int32, (CO, CO * CO), 0)
    mine = lax.rem(lax.broadcasted_iota(jnp.int32, (CO, CO * CO), 1), CO) == n
    expanded = [jnp.where(mine, wide[i : i + 1], 0.0).astype(jnp.bfloat16) for i in range(8)]
    mixing = dot(jnp.concatenate(expanded, axis=0), w_outer[...]).astype(jnp.bfloat16)
    eye = jnp.where(
        lax.broadcasted_iota(jnp.int32, (CZ, CZ), 0) == lax.broadcasted_iota(jnp.int32, (CZ, CZ), 1), 1.0, 0.0
    ).astype(jnp.bfloat16)
    for i in range(8):
        base[:CZ, CZ * i : CZ * i + CZ] = eye
        for k in range(4):
            base[CZ + CO * k : CZ + CO * k + CO, CZ * i : CZ * i + CZ] = mixing[CO * i : CO * i + CO]
    left = left.astype(jnp.float32)
    lane = lax.broadcasted_iota(jnp.int32, (16, CZ), 1)
    copies = []
    for k in range(ROWS):
        parts = []
        for half in range(2):
            packed = gathered[half, k, HALF:, :].astype(jnp.float32)
            outer_rows = [jnp.where(lane // CO == m, packed, 0.0) for m in range(4)]
            outer_rows = jnp.concatenate(outer_rows, axis=0).astype(jnp.bfloat16)
            parts.append(jnp.concatenate([gathered[half, k, :HALF, :], outer_rows], axis=1))
        rows = jnp.concatenate(parts, axis=0)
        for i in range(0, 8, 2):
            grid = dot(rows, base[:, CZ * i : CZ * i + 2 * CZ])
            for j in range(2):
                total = grid[:, CZ * j : CZ * j + CZ] + left[i + j : i + j + 1]
                result[i + j, TOK_DEV * k : TOK_DEV * k + TOK_DEV, :] = total.astype(jnp.bfloat16)
        copy = pltpu.make_async_copy(
            result.at[:, pl.ds(TOK_DEV * k, TOK_DEV)], out.at[:, pl.ds(TOK_DEV * k, TOK_DEV)], sems.at[k]
        )
        copy.start()
        copies.append(copy)
    for copy in copies:
        copy.wait()


def body(
    atoms, window_offsets, atom_token, w_query, w_key, w_value, w_out, w_token, gain_token, w_pair, w_outer
):
    vmem = pl.BlockSpec(memory_space=pltpu.VMEM)
    hbm = pl.BlockSpec(memory_space=pltpu.HBM)
    anywhere = pl.BlockSpec(memory_space=pl.ANY)
    dma = pltpu.SemaphoreType.DMA
    bf16, f32 = jnp.bfloat16, jnp.float32
    gathered, left_rows = pl.pallas_call(
        embed_kernel,
        out_shape=[
            jax.ShapeDtypeStruct((2, ROWS, BLK, CZ), bf16),
            jax.ShapeDtypeStruct((16, CZ), bf16),
        ],
        in_specs=[hbm] * 10,
        out_specs=[anywhere, anywhere],
        scratch_shapes=[
            pltpu.SMEM((ATOMS_DEV // QB,), jnp.int32),
            pltpu.VMEM((ATOMS_DEV,), jnp.int32),
            pltpu.VMEM((AW, AW), bf16),
            pltpu.VMEM((AW, AW), bf16),
            pltpu.VMEM((AW, AW), bf16),
            pltpu.VMEM((AW, AW), bf16),
            pltpu.VMEM((AW, TW), bf16),
            pltpu.VMEM((TW,), bf16),
            pltpu.VMEM((2 * CZ + 2 * CO, TW), bf16),
            pltpu.VMEM((EXT, AW), bf16),
            pltpu.VMEM((EXT, AW), bf16),
            pltpu.VMEM((AW, ATOMS_DEV), bf16),
            pltpu.VMEM((2, 80, EXT), bf16),
            pltpu.VMEM((ATOMS_DEV, AW), bf16),
            pltpu.VMEM((ATOMS_DEV, WIDE), bf16),
            pltpu.VMEM((2 * CZ, TW), bf16),
            pltpu.VMEM((8, WIDE), f32),
            pltpu.VMEM((8, WIDE), f32),
            pltpu.VMEM((2, BLK, CZ), bf16),
            pltpu.VMEM((ROWS, 16, CZ), bf16),
            pltpu.VMEM((16, CZ), bf16),
            dma, dma((9,)), dma((2,)), dma((2,)), dma, dma,
            dma((2, 2)), dma((2, 2)), dma((2,)), dma((2, 4)), dma((2, 4)), dma((COLS,)), dma, dma,
        ],
        compiler_params=pltpu.CompilerParams(
            collective_id=0, has_side_effects=True, vmem_limit_bytes=60 * 1024 * 1024
        ),
        name="embed",
    )(
        atoms, window_offsets, atom_token, w_query, w_key, w_value, w_out, w_token, gain_token, w_pair.T,
    )
    return pl.pallas_call(
        pair_kernel,
        out_shape=jax.ShapeDtypeStruct((8, ROWS * TOK_DEV, CZ), bf16),
        in_specs=[vmem, vmem, vmem],
        out_specs=anywhere,
        scratch_shapes=[
            pltpu.VMEM((2 * CZ, 8 * CZ), bf16),
            pltpu.VMEM((8, ROWS * TOK_DEV, CZ), bf16),
            dma((ROWS,)),
        ],
        compiler_params=pltpu.CompilerParams(vmem_limit_bytes=60 * 1024 * 1024),
        name="pair",
    )(gathered, left_rows, w_outer)


def solution(mesh):
    split = P(("row", "col"))
    placed = (P(("row", "col"), None), split, split) + (P(),) * 8
    return jax.shard_map(
        body, mesh=mesh, in_specs=placed, out_specs=P("row", "col", None), check_vma=False
    )
```

```python
import jax
import jax.numpy as jnp
from jax import lax
from jax.experimental import pallas as pl
from jax.experimental.pallas import tpu as pltpu
from jax.sharding import PartitionSpec as P

AW = 128
HEADS = 4
TW = 384
CZ = 128
CO = 32
QB = 32
RIM = 64
ROWS = 8
COLS = 32
DEVICES = ROWS * COLS
ATOMS_DEV = 1536
TOK_DEV = 128
EXT = ATOMS_DEV + 2 * RIM
GROUP = 128
GROUPS = ATOMS_DEV // GROUP
KEYS = GROUP + 2 * RIM
HALF = 64
BLK = HALF + HALF // 4
WIDE = TW + 128
EXP_SCALE = float(32 ** -0.5 * 1.4426950408889634)
MESH = pl.DeviceIdType.MESH
NT = (((1,), (1,)), ((), ()))


def dot(a, b):
    return jnp.dot(a, b, preferred_element_type=jnp.float32)


def place(device):
    return (lax.div(device, COLS), lax.rem(device, COLS))


def attend_group(g, edge_low, edge_high, off, keys, queries, values, att):
    k = keys[GROUP * g : GROUP * g + KEYS, :]
    q = queries[:, GROUP * g : GROUP * g + GROUP]
    lane = lax.broadcasted_iota(jnp.int32, (1, GROUP), 1)
    start = jnp.zeros((1, GROUP), jnp.int32)
    for b in range(GROUP // QB):
        start = jnp.where(lane // QB == b, QB * b + RIM + off[GROUP // QB * g + b], start)
    key = lax.broadcasted_iota(jnp.int32, (KEYS, GROUP), 0)
    inside = (key >= start) & (key < start + 128)
    if g == 0:
        inside &= key >= edge_low
    if g == GROUPS - 1:
        inside &= key < edge_high
    bias = jnp.where(inside, 0.0, -1e30)
    zero = jnp.zeros((AW // HEADS, GROUP), jnp.bfloat16)
    outs = []
    for pair in range(2):
        sides = []
        for h in (2 * pair, 2 * pair + 1):
            head = [zero] * HEADS
            head[h] = q[32 * h : 32 * h + 32, :]
            sides.append(jnp.concatenate(head, axis=0))
        scores = dot(k, jnp.concatenate(sides, axis=1))
        scores = scores + jnp.concatenate([bias, bias], axis=1)
        top = jnp.max(scores, axis=0, keepdims=True)
        lifted = jnp.exp2((scores - top) * EXP_SCALE).astype(jnp.bfloat16)
        mixed = dot(values[pair, :, GROUP * g : GROUP * g + KEYS], lifted)
        scaled = mixed[:64] * (1.0 / mixed[64:65])
        outs += [scaled[:32, :GROUP], scaled[32:, GROUP:]]
    att[GROUP * g : GROUP * g + GROUP, :] = jnp.concatenate(outs, axis=0).T.astype(jnp.bfloat16)


def hidden_rows(lo, hi, ext, att, w_out, w_token, hid):
    mixed = dot(att[lo:hi, :], w_out[...])
    update = (ext[RIM + lo : RIM + hi, :].astype(jnp.float32) + mixed).astype(jnp.bfloat16)
    hid[lo:hi, :TW] = jnp.maximum(dot(update, w_token[...]), 0.0).astype(jnp.bfloat16)


def pooled_rows(first, count, lo, hi, device, token, hid):
    slot = token[...].reshape(1, ATOMS_DEV)[:, lo:hi] - device * TOK_DEV
    rows = lax.broadcasted_iota(jnp.int32, (count, hi - lo), 0) + first
    one_hot = jnp.where(rows == slot, 1.0, 0.0).astype(jnp.bfloat16)
    return dot(one_hot, hid[lo:hi, :])


def token_normed(pooled, gain):
    count = pooled[:, TW:]
    single = pooled[:, :TW] / jnp.concatenate([count] * 3, axis=1)
    centre = single - jnp.mean(single, axis=1, keepdims=True)
    variance = jnp.mean(centre * centre, axis=1, keepdims=True)
    return (centre * lax.rsqrt(variance + 1e-05) * gain).astype(jnp.bfloat16)


def embed_kernel(
    atoms, off_hbm, token_hbm, wq_hbm, wk_hbm, wv_hbm, w_out_hbm, w_token_hbm, gain_hbm, w_pair_hbm, w_outer_hbm,
    result,
    off, token, wq, wk, wv, w_out, w_token, gain, w_pair, w_outer,
    gathered, base,
    ext, keys, queries, values, att, hid, w_right,
    spill_out, spill_in, block, left_all, left_in,
    own_sem, load_sem, halo_send, halo_recv, spill_send, spill_recv,
    first_send, first_recv, local_sem, pass_send, pass_recv, left_send, left_recv,
):
    row = lax.axis_index("row")
    col = lax.axis_index("col")
    me = row * COLS + col
    before = lax.rem(me + DEVICES - 1, DEVICES)
    after = lax.rem(me + 1, DEVICES)
    group_col = lax.div(me, ROWS)
    slot = lax.rem(me, ROWS)
    my_y, my_z = lax.div(row, 2), lax.rem(row, 2)
    relay_y = lax.rem(lax.div(col, 8) + lax.div(slot, 2), 4)
    held = 2 * lax.rem(my_y + 4 - lax.rem(col, 4), 4)
    keeps = jnp.where((group_col == col) & (relay_y == my_y), 1, 0)

    def signal(device):
        pl.semaphore_signal(barrier, inc=1, device_id=place(device), device_id_type=MESH)

    barrier = pltpu.get_barrier_semaphore()
    signal(before)
    signal(after)
    for k in range(2):
        @pl.when(ROWS * col + held + k != me)
        def _():
            signal(ROWS * col + held + k)
    for i in range(1, 4):
        signal((2 * lax.rem(my_y + i, 4) + my_z) * COLS + col)

    @pl.when(lax.rem(col, 8) != 0)
    def _():
        signal(me - lax.rem(col, 8))

    @pl.when((lax.rem(col, 8) == 0) & (col != 0))
    def _():
        signal(row * COLS)

    @pl.when((col == 0) & (row != 0))
    def _():
        signal(0)

    own = pltpu.make_async_copy(atoms, ext.at[pl.ds(RIM, ATOMS_DEV)], own_sem)
    own.start()
    pieces = [
        (wq_hbm, wq), (wk_hbm, wk), (wv_hbm, wv), (off_hbm, off), (w_out_hbm, w_out),
        (token_hbm, token), (w_token_hbm, w_token), (gain_hbm, gain), (w_pair_hbm, w_pair),
        (w_outer_hbm, w_outer),
    ]
    loads = [pltpu.make_async_copy(a, b, load_sem.at[i]) for i, (a, b) in enumerate(pieces)]
    for load in loads:
        load.start()
    for load in loads[:3]:
        load.wait()

    both = jnp.concatenate([wq[...], wv[...]], axis=1).astype(jnp.float32).T.astype(jnp.bfloat16)
    hid[:, TW:] = jnp.ones((ATOMS_DEV, WIDE - TW), jnp.bfloat16)
    for pair in range(2):
        values[pair, 64:, :] = jnp.ones((16, EXT), jnp.bfloat16)
    own.wait()
    for lo in range(0, ATOMS_DEV, 512):
        x = ext[RIM + lo : RIM + lo + 512, :]
        keys[RIM + lo : RIM + lo + 512, :] = dot(x, wk[...]).astype(jnp.bfloat16)
    for lo in range(128, ATOMS_DEV, 256):
        hi = min(lo + 256, ATOMS_DEV)
        x = ext[lo:hi, :]
        vt = lax.dot_general(both[AW:], x, NT, preferred_element_type=jnp.float32).astype(jnp.bfloat16)
        values[0, :64, lo:hi] = vt[:64]
        values[1, :64, lo:hi] = vt[64:]
    for lo in range(0, ATOMS_DEV, 512):
        x = ext[RIM + lo : RIM + lo + 512, :]
        queries[:, lo : lo + 512] = lax.dot_general(
            both[:AW], x, NT, preferred_element_type=jnp.float32
        ).astype(jnp.bfloat16)

    is_head = jnp.where(lax.rem(col, 8) == 0, 1, 0)
    is_leader = jnp.where(col == 0, 1, 0)
    is_first = jnp.where(me == 0, 1, 0)
    pl.semaphore_wait(barrier, 2 + 2 - keeps + 3 + 7 * is_head + 3 * is_leader + 7 * is_first)

    halo = [
        pltpu.make_async_remote_copy(
            src_ref=atoms.at[pl.ds(ATOMS_DEV - RIM, RIM)], dst_ref=ext.at[pl.ds(0, RIM)],
            send_sem=halo_send.at[0], recv_sem=halo_recv.at[0],
            device_id=place(after), device_id_type=MESH,
        ),
        pltpu.make_async_remote_copy(
            src_ref=atoms.at[pl.ds(0, RIM)], dst_ref=ext.at[pl.ds(EXT - RIM, RIM)],
            send_sem=halo_send.at[1], recv_sem=halo_recv.at[1],
            device_id=place(before), device_id_type=MESH,
        ),
    ]
    for copy in halo:
        copy.start()

    edge_low = jnp.where(me == 0, RIM, 0)
    edge_high = jnp.where(me == DEVICES - 1, KEYS - RIM, KEYS)

    def attend(g):
        attend_group(g, edge_low, edge_high, off, keys, queries, values, att)

    for load in loads[3:]:
        load.wait()
    eye = lax.broadcasted_iota(jnp.int32, (CZ, CZ), 0) == lax.broadcasted_iota(jnp.int32, (CZ, CZ), 1)
    for i in range(8):
        base[:CZ, CZ * i : CZ * i + CZ] = jnp.where(eye, 1.0, 0.0).astype(jnp.bfloat16)
    w_right[:CZ, :] = w_pair[CZ + CO : 2 * CZ + CO, :]
    for m in range(4):
        w_right[CZ + CO * m : CZ + CO * m + CO, :] = w_pair[2 * CZ + CO :, :]

    for g in range(1, 6):
        attend(g)

    for copy in halo:
        copy.wait()
    for lo in (0, EXT - RIM):
        keys[lo : lo + RIM, :] = dot(ext[lo : lo + RIM, :], wk[...]).astype(jnp.bfloat16)
    for lo in (0, EXT - 128):
        vt = lax.dot_general(
            both[AW:], ext[lo : lo + 128, :], NT, preferred_element_type=jnp.float32
        ).astype(jnp.bfloat16)
        values[0, :64, lo : lo + 128] = vt[:64]
        values[1, :64, lo : lo + 128] = vt[64:]
    attend(0)
    attend(6)

    lane = lax.broadcasted_iota(jnp.int32, (16, CZ), 1)

    def first_copy(half, i):
        return pltpu.make_async_remote_copy(
            src_ref=block.at[half], dst_ref=gathered.at[half, slot],
            send_sem=first_send.at[half, i], recv_sem=first_recv.at[half, lax.rem(slot, 2)],
            device_id=(2 * relay_y + i, group_col), device_id_type=MESH,
        )

    def local_copy(half):
        return pltpu.make_async_copy(block.at[half], gathered.at[half, slot], local_sem.at[half])

    def pass_copy(half, i, start):
        return pltpu.make_async_remote_copy(
            src_ref=gathered.at[half, pl.ds(start, 2)], dst_ref=gathered.at[half, pl.ds(start, 2)],
            send_sem=pass_send.at[half, i], recv_sem=pass_recv.at[half, i],
            device_id=(2 * lax.rem(my_y + i, 4) + my_z, col), device_id_type=MESH,
        )

    def pass_on(half):
        for k in range(2):
            @pl.when(ROWS * col + held + k != me)
            def _():
                pltpu.make_async_remote_copy(
                    src_ref=block.at[half], dst_ref=gathered.at[half, held + k],
                    send_sem=first_send.at[half, 0], recv_sem=first_recv.at[half, k],
                    device_id=place(ROWS * col + held + k), device_id_type=MESH,
                ).wait_recv()

        @pl.when(keeps == 1)
        def _():
            local_copy(half).wait()

        for i in range(1, 4):
            pass_copy(half, i, held).start()

    def finish(half, pooled):
        normed = token_normed(pooled, gain[...].reshape(1, TW).astype(jnp.float32))
        right = lax.dot_general(normed, w_right[...], NT, preferred_element_type=jnp.float32)
        packed = right[:16, CZ:]
        for m in range(1, 4):
            packed = jnp.where(lane // CO == m, right[16 * m : 16 * m + 16, CZ:], packed)
        block[half, :HALF, :] = right[:, :CZ].astype(jnp.bfloat16)
        block[half, HALF:, :] = packed.astype(jnp.bfloat16)
        for i in range(2):
            copy = first_copy(half, i)
            mine = (keeps == 1) & (my_z == i)

            @pl.when(jnp.logical_not(mine))
            def _():
                copy.start()

            @pl.when(mine)
            def _():
                local_copy(half).start()

        return normed

    hidden_rows(0, 896, ext, att, w_out, w_token, hid)
    pooled = pooled_rows(-16, 80, 0, 896, me, token, hid)
    spill_out[...] = pooled[8:16]
    spill = pltpu.make_async_remote_copy(
        src_ref=spill_out, dst_ref=spill_in, send_sem=spill_send, recv_sem=spill_recv,
        device_id=place(before), device_id_type=MESH,
    )
    spill.start()
    normed = finish(0, pooled[16:])

    def left_copy(source, to, index):
        return pltpu.make_async_remote_copy(
            src_ref=source, dst_ref=left_in, send_sem=left_send.at[index], recv_sem=left_recv,
            device_id=to, device_id_type=MESH,
        )

    @pl.when(me == 0)
    def _():
        left = lax.dot_general(normed, w_pair[: 2 * CZ, :], NT, preferred_element_type=jnp.float32)
        for r in range(ROWS):
            rows = left[8 * r : 8 * r + 8]
            left_all[r] = jnp.concatenate([rows[:, :CZ], rows[:, CZ:]], axis=0).astype(jnp.bfloat16)
        left_in[...] = left_all[0]
        for r in range(1, ROWS):
            left_copy(left_all.at[r], (r, 0), r).start()

    for g in range(7, 11):
        attend(g)

    attend(11)
    hidden_rows(896, ATOMS_DEV, ext, att, w_out, w_token, hid)
    pooled = pooled_rows(HALF, HALF, 768, ATOMS_DEV, me, token, hid)
    spill.wait()
    pooled = jnp.concatenate([pooled[:56], pooled[56:] + spill_in[...]], axis=0)
    finish(1, pooled)

    @pl.when((col == 0) & (me != 0))
    def _():
        left_copy(left_in, (row, 0), 0).wait_recv()

    @pl.when(col == 0)
    def _():
        for x in range(1, 4):
            left_copy(left_in, (row, 8 * x), 8 + x).start()
        for c in range(1, 8):
            left_copy(left_in, (row, c), 16 + c).start()

    pass_on(0)

    @pl.when((lax.rem(col, 8) == 0) & (col != 0))
    def _():
        left_copy(left_in, (row, 0), 0).wait_recv()

    @pl.when((lax.rem(col, 8) == 0) & (col != 0))
    def _():
        for c in range(1, 8):
            left_copy(left_in, (row, col + c), 16 + c).start()

    pass_on(1)

    @pl.when(lax.rem(col, 8) != 0)
    def _():
        left_copy(left_in, (row, 0), 0).wait_recv()

    mix_left(left_in, w_outer, base)
    left = left_in[:8, :].astype(jnp.float32)

    def pair_rows(half, start):
        pair_block(gathered, half, start, base, left, result)

    def arrived(half):
        for i in range(1, 4):
            theirs = 2 * lax.rem(my_y + 4 - i + 4 - lax.rem(col, 4), 4)
            pass_copy(half, i, theirs).wait_recv()
            pair_rows(half, theirs)

    pair_rows(0, held)
    arrived(0)
    pair_rows(1, held)
    arrived(1)

    @pl.when(me == 0)
    def _():
        for r in range(1, ROWS):
            left_copy(left_all.at[r], (r, 0), r).wait_send()

    @pl.when(col == 0)
    def _():
        for x in range(1, 4):
            left_copy(left_in, (row, 8 * x), 8 + x).wait_send()

    @pl.when(lax.rem(col, 8) == 0)
    def _():
        for c in range(1, 8):
            left_copy(left_in, (row, col + c), 16 + c).wait_send()

    for half in range(2):
        for i in range(1, 4):
            pass_copy(half, i, held).wait_send()
        for i in range(2):
            @pl.when(jnp.logical_not((keeps == 1) & (my_z == i)))
            def _():
                first_copy(half, i).wait_send()


def mix_left(left_in, w_outer, base):
    outer = left_in[8:, :CO]
    spread = lax.broadcasted_iota(jnp.int32, (CO, CO * CO), 1) // CO
    spread = jnp.where(spread == lax.broadcasted_iota(jnp.int32, (CO, CO * CO), 0), 1.0, 0.0)
    wide = dot(outer, spread.astype(jnp.bfloat16))
    n = lax.broadcasted_iota(jnp.int32, (CO, CO * CO), 0)
    mine = lax.rem(lax.broadcasted_iota(jnp.int32, (CO, CO * CO), 1), CO) == n
    expanded = [jnp.where(mine, wide[i : i + 1], 0.0).astype(jnp.bfloat16) for i in range(8)]
    mixing = dot(jnp.concatenate(expanded, axis=0), w_outer[...]).astype(jnp.bfloat16)
    for i in range(8):
        for k in range(4):
            base[CZ + CO * k : CZ + CO * k + CO, CZ * i : CZ * i + CZ] = mixing[CO * i : CO * i + CO]


def pair_block(gathered, half, start, base, left, result):
    lane = lax.broadcasted_iota(jnp.int32, (16, CZ), 1)
    parts = []
    for k in range(2):
        packed = gathered[half, start + k, HALF:, :].astype(jnp.float32)
        outer = [jnp.where(lane // CO == m, packed, 0.0) for m in range(4)]
        outer = jnp.concatenate(outer, axis=0).astype(jnp.bfloat16)
        parts.append(jnp.concatenate([gathered[half, start + k, :HALF, :], outer], axis=1))
    rows = jnp.concatenate(parts, axis=0)
    for i in range(0, 8, 2):
        grid = dot(rows, base[:, CZ * i : CZ * i + 2 * CZ])
        for j in range(2):
            total = (grid[:, CZ * j : CZ * j + CZ] + left[i + j : i + j + 1]).astype(jnp.bfloat16)
            for k in range(2):
                first = pl.multiple_of(TOK_DEV * (start + k) + HALF * half, HALF)
                result[i + j, pl.ds(first, HALF), :] = total[HALF * k : HALF * k + HALF]


def body(
    atoms, window_offsets, atom_token, w_query, w_key, w_value, w_out, w_token, gain_token, w_pair, w_outer
):
    hbm = pl.BlockSpec(memory_space=pltpu.HBM)
    dma = pltpu.SemaphoreType.DMA
    bf16, f32 = jnp.bfloat16, jnp.float32
    return pl.pallas_call(
        embed_kernel,
        out_shape=pltpu.VMEM((8, ROWS * TOK_DEV, CZ), bf16),
        in_specs=[hbm] * 11,
        out_specs=pl.BlockSpec(memory_space=pltpu.VMEM),
        scratch_shapes=[
            pltpu.SMEM((ATOMS_DEV // QB,), jnp.int32),
            pltpu.VMEM((ATOMS_DEV,), jnp.int32),
            pltpu.VMEM((AW, AW), bf16),
            pltpu.VMEM((AW, AW), bf16),
            pltpu.VMEM((AW, AW), bf16),
            pltpu.VMEM((AW, AW), bf16),
            pltpu.VMEM((AW, TW), bf16),
            pltpu.VMEM((TW,), bf16),
            pltpu.VMEM((2 * CZ + 2 * CO, TW), bf16),
            pltpu.VMEM((CO * CO, CZ), bf16),
            pltpu.VMEM((2, ROWS, BLK, CZ), bf16),
            pltpu.VMEM((2 * CZ, 8 * CZ), bf16),
            pltpu.VMEM((EXT, AW), bf16),
            pltpu.VMEM((EXT, AW), bf16),
            pltpu.VMEM((AW, ATOMS_DEV), bf16),
            pltpu.VMEM((2, 80, EXT), bf16),
            pltpu.VMEM((ATOMS_DEV, AW), bf16),
            pltpu.VMEM((ATOMS_DEV, WIDE), bf16),
            pltpu.VMEM((2 * CZ, TW), bf16),
            pltpu.VMEM((8, WIDE), f32),
            pltpu.VMEM((8, WIDE), f32),
            pltpu.VMEM((2, BLK, CZ), bf16),
            pltpu.VMEM((ROWS, 16, CZ), bf16),
            pltpu.VMEM((16, CZ), bf16),
            dma, dma((10,)), dma((2,)), dma((2,)), dma, dma,
            dma((2, 2)), dma((2, 2)), dma((2,)), dma((2, 4)), dma((2, 4)), dma((COLS,)), dma,
        ],
        compiler_params=pltpu.CompilerParams(
            collective_id=0, has_side_effects=True, vmem_limit_bytes=60 * 1024 * 1024
        ),
        name="embed",
    )(
        atoms, window_offsets, atom_token, w_query, w_key, w_value, w_out, w_token, gain_token, w_pair.T,
        w_outer,
    )


def solution(mesh):
    split = P(("row", "col"))
    placed = (P(("row", "col"), None), split, split) + (P(),) * 8
    return jax.shard_map(
        body, mesh=mesh, in_specs=placed, out_specs=P("row", "col", None), check_vma=False
    )
```

```python
import jax
import jax.numpy as jnp
from jax import lax
from jax.experimental import pallas as pl
from jax.experimental.pallas import tpu as pltpu
from jax.sharding import PartitionSpec as P

AW = 128
HEADS = 4
TW = 384
CZ = 128
CO = 32
QB = 32
RIM = 64
ROWS = 8
COLS = 32
DEVICES = ROWS * COLS
ATOMS_DEV = 1536
TOK_DEV = 128
EXT = ATOMS_DEV + 2 * RIM
GROUP = 128
GROUPS = ATOMS_DEV // GROUP
UNITS = 2 * GROUPS
AHEAD = 3
BEHIND = 2
HALF = 64
BLK = HALF + HALF // 4
WIDE = TW + 128
EXP_SCALE = float(32 ** -0.5 * 1.4426950408889634)
MESH = pl.DeviceIdType.MESH
NT = (((1,), (1,)), ((), ()))


def dot(a, b):
    return jnp.dot(a, b, preferred_element_type=jnp.float32)


def place(device):
    return (lax.div(device, COLS), lax.rem(device, COLS))


def dot_nt(a, b):
    return lax.dot_general(a, b, NT, preferred_element_type=jnp.float32)


def turned(w):
    return w[...].astype(jnp.float32).T.astype(jnp.bfloat16)


def unit_scores(unit, keys, queries):
    g, j = unit // 2, unit % 2
    q = queries[:, GROUP * g : GROUP * g + GROUP]
    side = (lax.broadcasted_iota(jnp.int32, (HALF, GROUP), 0) // 32 == j) == (
        lax.broadcasted_iota(jnp.int32, (HALF, GROUP), 1) < HALF
    )
    none = jnp.zeros((HALF, GROUP), jnp.bfloat16)
    heads = [jnp.where(side, q[HALF * t : HALF * t + HALF], none) for t in range(2)]
    operand = jnp.concatenate(
        [jnp.concatenate([heads[0], none], axis=1), jnp.concatenate([none, heads[1]], axis=1)], axis=0
    )
    return dot(keys[HALF * unit : HALF * unit + 192, :], operand)


def unit_softmax(unit, scores, me, off):
    lane = lax.broadcasted_iota(jnp.int32, (1, GROUP), 1)
    second = lax.rem(lane // QB, 2) == 1
    start = jnp.where(second, off[2 * unit + 1] + RIM + QB, off[2 * unit] + RIM)
    low, high = start, start + 128
    if unit == 0:
        low = jnp.maximum(low, jnp.where(me == 0, RIM, 0))
    if unit == UNITS - 1:
        high = jnp.minimum(high, jnp.where(me == DEVICES - 1, 128, 192))
    row = lax.broadcasted_iota(jnp.int32, (HALF, GROUP), 0)
    enters, stays = row >= low, row + 128 < high
    parts = []
    for t in range(2):
        tile = scores[:, GROUP * t : GROUP * t + GROUP]
        tile = jnp.concatenate(
            [jnp.where(enters, tile[:64], -1e30), tile[64:128], jnp.where(stays, tile[128:], -1e30)], axis=0
        )
        top = jnp.max(tile, axis=0, keepdims=True)
        parts.append(jnp.exp2((tile - top) * EXP_SCALE).astype(jnp.bfloat16))
    return jnp.concatenate(
        [jnp.concatenate(parts, axis=1), jnp.zeros((HALF, 2 * GROUP), jnp.bfloat16)], axis=0
    )


def group_store(g, mixed, att):
    left = lax.broadcasted_iota(jnp.int32, (1, GROUP), 1) < HALF
    for h in range(HEADS):
        lanes = slice(GROUP * (h // 2), GROUP * (h // 2) + GROUP)
        a, b = mixed if h % 2 == 0 else mixed[::-1]
        total = jnp.where(left, a[AW : AW + 1, lanes], b[AW : AW + 1, lanes])
        value = jnp.where(left, a[32 * h : 32 * h + 32, lanes], b[32 * h : 32 * h + 32, lanes]) * (1.0 / total)
        if h % 2 == 1:
            value = pltpu.roll(value, HALF, 1)
        att[32 * h : 32 * h + 32, GROUP * g : GROUP * g + GROUP] = value.astype(jnp.bfloat16)


def attend(groups, me, off, keys, queries, values, att):
    units = [2 * g + j for g in groups for j in range(2)]
    scores, lifted, mixed = {}, {}, {}
    for i in range(len(units) + AHEAD + BEHIND):
        if i < len(units):
            scores[i] = unit_scores(units[i], keys, queries)
        k = i - AHEAD
        if 0 <= k < len(units):
            lifted[k] = unit_softmax(units[k], scores.pop(k), me, off)
        k = i - AHEAD - BEHIND
        if 0 <= k < len(units):
            g, j = units[k] // 2, units[k] % 2
            mixed[j] = dot(values[j, :, GROUP * g : GROUP * g + 2 * GROUP], lifted.pop(k))
            if j == 1:
                group_store(g, [mixed[0], mixed[1]], att)


def hidden_rows(lo, hi, turned_atoms, att, w_out_t, w_token_t, hid):
    mixed = dot(w_out_t[...], att[:, lo:hi])
    update = (turned_atoms[:, lo:hi].astype(jnp.float32) + mixed).astype(jnp.bfloat16)
    hid[:TW, lo:hi] = jnp.maximum(dot(w_token_t[...], update), 0.0).astype(jnp.bfloat16)


def pooled_rows(first, count, lo, hi, device, token, hid):
    slot = token[...].reshape(1, ATOMS_DEV)[:, lo:hi] - device * TOK_DEV
    rows = lax.broadcasted_iota(jnp.int32, (count, hi - lo), 0) + first
    one_hot = jnp.where(rows == slot, 1.0, 0.0).astype(jnp.bfloat16)
    return dot_nt(one_hot, hid[:, lo:hi])


def token_normed(pooled, gain):
    count = pooled[:, TW:]
    single = pooled[:, :TW] / jnp.concatenate([count] * 3, axis=1)
    centre = single - jnp.mean(single, axis=1, keepdims=True)
    variance = jnp.mean(centre * centre, axis=1, keepdims=True)
    return (centre * lax.rsqrt(variance + 1e-05) * gain).astype(jnp.bfloat16)


def embed_kernel(
    atoms, off_hbm, token_hbm, wq_hbm, wk_hbm, wv_hbm, w_out_hbm, w_token_hbm, gain_hbm, w_pair_hbm, w_outer_hbm,
    result,
    off, token, wq, wk, wv, w_out, w_token, gain, w_pair, w_outer,
    gathered, base,
    ext, keys, queries, values, att, hid, turned_atoms, w_out_t, w_token_t, w_right,
    spill_out, spill_in, block, left_all, left_in,
    own_sem, load_sem, halo_send, halo_recv, spill_send, spill_recv,
    first_send, first_recv, local_sem, pass_send, pass_recv, left_send, left_recv,
):
    row = lax.axis_index("row")
    col = lax.axis_index("col")
    me = row * COLS + col
    before = lax.rem(me + DEVICES - 1, DEVICES)
    after = lax.rem(me + 1, DEVICES)
    group_col = lax.div(me, ROWS)
    slot = lax.rem(me, ROWS)
    my_y, my_z = lax.div(row, 2), lax.rem(row, 2)
    relay_y = lax.rem(lax.div(col, 8) + lax.div(slot, 2), 4)
    held = 2 * lax.rem(my_y + 4 - lax.rem(col, 4), 4)
    keeps = jnp.where((group_col == col) & (relay_y == my_y), 1, 0)

    def signal(device):
        pl.semaphore_signal(barrier, inc=1, device_id=place(device), device_id_type=MESH)

    barrier = pltpu.get_barrier_semaphore()
    signal(before)
    signal(after)
    for k in range(2):
        @pl.when(ROWS * col + held + k != me)
        def _():
            signal(ROWS * col + held + k)
    for i in range(1, 4):
        signal((2 * lax.rem(my_y + i, 4) + my_z) * COLS + col)

    @pl.when(lax.rem(col, 8) != 0)
    def _():
        signal(me - lax.rem(col, 8))

    @pl.when((lax.rem(col, 8) == 0) & (col != 0))
    def _():
        signal(row * COLS)

    @pl.when((col == 0) & (row != 0))
    def _():
        signal(0)

    own = pltpu.make_async_copy(atoms, ext.at[pl.ds(RIM, ATOMS_DEV)], own_sem)
    own.start()
    pieces = [
        (wq_hbm, wq), (wk_hbm, wk), (wv_hbm, wv), (off_hbm, off), (w_out_hbm, w_out),
        (token_hbm, token), (w_token_hbm, w_token), (gain_hbm, gain), (w_pair_hbm, w_pair),
        (w_outer_hbm, w_outer),
    ]
    loads = [pltpu.make_async_copy(a, b, load_sem.at[i]) for i, (a, b) in enumerate(pieces)]
    for load in loads:
        load.start()
    for load in loads[:3]:
        load.wait()

    one = lax.broadcasted_iota(jnp.int32, (CZ, CZ), 0) == lax.broadcasted_iota(jnp.int32, (CZ, CZ), 1)
    eye = jnp.where(one, 1.0, 0.0).astype(jnp.bfloat16)
    value_t = turned(wv)
    left_side = jnp.concatenate([turned(wq), value_t, eye], axis=0)
    hid[TW:, :] = jnp.ones((WIDE - TW, ATOMS_DEV), jnp.bfloat16)
    for j in range(2):
        values[j, AW:, :] = jnp.ones((16, EXT), jnp.bfloat16)
    own.wait()
    for lo in range(0, ATOMS_DEV, 512):
        x = ext[RIM + lo : RIM + lo + 512, :]
        keys[RIM + lo : RIM + lo + 512, :] = dot(x, wk[...]).astype(jnp.bfloat16)
    for lo in range(0, ATOMS_DEV, 256):
        product = dot_nt(left_side, ext[RIM + lo : RIM + lo + 256, :])
        for h in range(HEADS):
            rows = slice(32 * h, 32 * h + 32)
            for part in range(0, 256, GROUP):
                q = product[rows, part : part + GROUP]
                if h % 2 == 1:
                    q = pltpu.roll(q, HALF, 1)
                queries[rows, lo + part : lo + part + GROUP] = q.astype(jnp.bfloat16)
        values[1, :AW, lo : lo + 256] = product[AW : 2 * AW].astype(jnp.bfloat16)
        turned_atoms[:, lo : lo + 256] = product[2 * AW :].astype(jnp.bfloat16)
    for lo in range(128, ATOMS_DEV, 256):
        hi = min(lo + 256, ATOMS_DEV)
        values[0, :AW, lo:hi] = dot_nt(value_t, ext[lo:hi, :]).astype(jnp.bfloat16)
    pad = jnp.zeros((RIM, AW), jnp.bfloat16)
    rest = jnp.concatenate([ext[ATOMS_DEV : ATOMS_DEV + RIM, :], pad], axis=0)
    values[0, :AW, ATOMS_DEV:] = dot_nt(value_t, rest).astype(jnp.bfloat16)

    is_head = jnp.where(lax.rem(col, 8) == 0, 1, 0)
    is_leader = jnp.where(col == 0, 1, 0)
    is_first = jnp.where(me == 0, 1, 0)
    pl.semaphore_wait(barrier, 2 + 2 - keeps + 3 + 7 * is_head + 3 * is_leader + 7 * is_first)

    halo = [
        pltpu.make_async_remote_copy(
            src_ref=atoms.at[pl.ds(ATOMS_DEV - RIM, RIM)], dst_ref=ext.at[pl.ds(0, RIM)],
            send_sem=halo_send.at[0], recv_sem=halo_recv.at[0],
            device_id=place(after), device_id_type=MESH,
        ),
        pltpu.make_async_remote_copy(
            src_ref=atoms.at[pl.ds(0, RIM)], dst_ref=ext.at[pl.ds(EXT - RIM, RIM)],
            send_sem=halo_send.at[1], recv_sem=halo_recv.at[1],
            device_id=place(before), device_id_type=MESH,
        ),
    ]
    for copy in halo:
        copy.start()

    for load in loads[3:]:
        load.wait()
    for i in range(8):
        base[:CZ, CZ * i : CZ * i + CZ] = eye
    w_out_t[...] = turned(w_out)
    w_token_t[...] = turned(w_token)
    w_right[:CZ, :] = w_pair[CZ + CO : 2 * CZ + CO, :]
    for m in range(4):
        w_right[CZ + CO * m : CZ + CO * m + CO, :] = w_pair[2 * CZ + CO :, :]

    attend(range(1, 7), me, off, keys, queries, values, att)

    for copy in halo:
        copy.wait()
    for lo in (0, EXT - RIM):
        keys[lo : lo + RIM, :] = dot(ext[lo : lo + RIM, :], wk[...]).astype(jnp.bfloat16)
    values[0, :AW, :GROUP] = dot_nt(value_t, ext[:GROUP, :]).astype(jnp.bfloat16)
    rest = jnp.concatenate([ext[EXT - RIM :, :], pad], axis=0)
    values[1, :AW, ATOMS_DEV:] = dot_nt(value_t, rest).astype(jnp.bfloat16)
    attend([0], me, off, keys, queries, values, att)

    lane = lax.broadcasted_iota(jnp.int32, (16, CZ), 1)

    def first_copy(half, i):
        return pltpu.make_async_remote_copy(
            src_ref=block.at[half], dst_ref=gathered.at[half, slot],
            send_sem=first_send.at[half, i], recv_sem=first_recv.at[half, lax.rem(slot, 2)],
            device_id=(2 * relay_y + i, group_col), device_id_type=MESH,
        )

    def local_copy(half):
        return pltpu.make_async_copy(block.at[half], gathered.at[half, slot], local_sem.at[half])

    def pass_copy(half, i, start):
        return pltpu.make_async_remote_copy(
            src_ref=gathered.at[half, pl.ds(start, 2)], dst_ref=gathered.at[half, pl.ds(start, 2)],
            send_sem=pass_send.at[half, i], recv_sem=pass_recv.at[half, i],
            device_id=(2 * lax.rem(my_y + i, 4) + my_z, col), device_id_type=MESH,
        )

    def pass_on(half):
        for k in range(2):
            @pl.when(ROWS * col + held + k != me)
            def _():
                pltpu.make_async_remote_copy(
                    src_ref=block.at[half], dst_ref=gathered.at[half, held + k],
                    send_sem=first_send.at[half, 0], recv_sem=first_recv.at[half, k],
                    device_id=place(ROWS * col + held + k), device_id_type=MESH,
                ).wait_recv()

        @pl.when(keeps == 1)
        def _():
            local_copy(half).wait()

        for i in range(1, 4):
            pass_copy(half, i, held).start()

    def finish(half, pooled):
        normed = token_normed(pooled, gain[...].reshape(1, TW).astype(jnp.float32))
        right = lax.dot_general(normed, w_right[...], NT, preferred_element_type=jnp.float32)
        packed = right[:16, CZ:]
        for m in range(1, 4):
            packed = jnp.where(lane // CO == m, right[16 * m : 16 * m + 16, CZ:], packed)
        block[half, :HALF, :] = right[:, :CZ].astype(jnp.bfloat16)
        block[half, HALF:, :] = packed.astype(jnp.bfloat16)
        for i in range(2):
            copy = first_copy(half, i)
            mine = (keeps == 1) & (my_z == i)

            @pl.when(jnp.logical_not(mine))
            def _():
                copy.start()

            @pl.when(mine)
            def _():
                local_copy(half).start()

        return normed

    hidden_rows(0, 896, turned_atoms, att, w_out_t, w_token_t, hid)
    pooled = pooled_rows(-16, 80, 0, 896, me, token, hid)
    spill_out[...] = pooled[8:16]
    spill = pltpu.make_async_remote_copy(
        src_ref=spill_out, dst_ref=spill_in, send_sem=spill_send, recv_sem=spill_recv,
        device_id=place(before), device_id_type=MESH,
    )
    spill.start()
    normed = finish(0, pooled[16:])

    def left_copy(source, to, index):
        return pltpu.make_async_remote_copy(
            src_ref=source, dst_ref=left_in, send_sem=left_send.at[index], recv_sem=left_recv,
            device_id=to, device_id_type=MESH,
        )

    @pl.when(me == 0)
    def _():
        left = lax.dot_general(normed, w_pair[: 2 * CZ, :], NT, preferred_element_type=jnp.float32)
        for r in range(ROWS):
            rows = left[8 * r : 8 * r + 8]
            left_all[r] = jnp.concatenate([rows[:, :CZ], rows[:, CZ:]], axis=0).astype(jnp.bfloat16)
        left_in[...] = left_all[0]
        for r in range(1, ROWS):
            left_copy(left_all.at[r], (r, 0), r).start()

    attend(range(7, 12), me, off, keys, queries, values, att)

    hidden_rows(896, ATOMS_DEV, turned_atoms, att, w_out_t, w_token_t, hid)
    pooled = pooled_rows(HALF, HALF, 768, ATOMS_DEV, me, token, hid)
    spill.wait()
    pooled = jnp.concatenate([pooled[:56], pooled[56:] + spill_in[...]], axis=0)
    finish(1, pooled)

    @pl.when((col == 0) & (me != 0))
    def _():
        left_copy(left_in, (row, 0), 0).wait_recv()

    @pl.when(col == 0)
    def _():
        for x in range(1, 4):
            left_copy(left_in, (row, 8 * x), 8 + x).start()
        for c in range(1, 8):
            left_copy(left_in, (row, c), 16 + c).start()

    pass_on(0)

    @pl.when((lax.rem(col, 8) == 0) & (col != 0))
    def _():
        left_copy(left_in, (row, 0), 0).wait_recv()

    @pl.when((lax.rem(col, 8) == 0) & (col != 0))
    def _():
        for c in range(1, 8):
            left_copy(left_in, (row, col + c), 16 + c).start()

    pass_on(1)

    @pl.when(lax.rem(col, 8) != 0)
    def _():
        left_copy(left_in, (row, 0), 0).wait_recv()

    mix_left(left_in, w_outer, base)
    left = left_in[:8, :].astype(jnp.float32)

    def pair_rows(half, start):
        pair_block(gathered, half, start, base, left, result)

    def arrived(half):
        for i in range(1, 4):
            theirs = 2 * lax.rem(my_y + 4 - i + 4 - lax.rem(col, 4), 4)
            pass_copy(half, i, theirs).wait_recv()
            pair_rows(half, theirs)

    pair_rows(0, held)
    arrived(0)
    pair_rows(1, held)
    arrived(1)

    @pl.when(me == 0)
    def _():
        for r in range(1, ROWS):
            left_copy(left_all.at[r], (r, 0), r).wait_send()

    @pl.when(col == 0)
    def _():
        for x in range(1, 4):
            left_copy(left_in, (row, 8 * x), 8 + x).wait_send()

    @pl.when(lax.rem(col, 8) == 0)
    def _():
        for c in range(1, 8):
            left_copy(left_in, (row, col + c), 16 + c).wait_send()

    for half in range(2):
        for i in range(1, 4):
            pass_copy(half, i, held).wait_send()
        for i in range(2):
            @pl.when(jnp.logical_not((keeps == 1) & (my_z == i)))
            def _():
                first_copy(half, i).wait_send()


def mix_left(left_in, w_outer, base):
    outer = left_in[8:, :CO]
    spread = lax.broadcasted_iota(jnp.int32, (CO, CO * CO), 1) // CO
    spread = jnp.where(spread == lax.broadcasted_iota(jnp.int32, (CO, CO * CO), 0), 1.0, 0.0)
    wide = dot(outer, spread.astype(jnp.bfloat16))
    n = lax.broadcasted_iota(jnp.int32, (CO, CO * CO), 0)
    mine = lax.rem(lax.broadcasted_iota(jnp.int32, (CO, CO * CO), 1), CO) == n
    expanded = [jnp.where(mine, wide[i : i + 1], 0.0).astype(jnp.bfloat16) for i in range(8)]
    mixing = dot(jnp.concatenate(expanded, axis=0), w_outer[...]).astype(jnp.bfloat16)
    for i in range(8):
        for k in range(4):
            base[CZ + CO * k : CZ + CO * k + CO, CZ * i : CZ * i + CZ] = mixing[CO * i : CO * i + CO]


def pair_block(gathered, half, start, base, left, result):
    lane = lax.broadcasted_iota(jnp.int32, (16, CZ), 1)
    parts = []
    for k in range(2):
        packed = gathered[half, start + k, HALF:, :].astype(jnp.float32)
        outer = [jnp.where(lane // CO == m, packed, 0.0) for m in range(4)]
        outer = jnp.concatenate(outer, axis=0).astype(jnp.bfloat16)
        parts.append(jnp.concatenate([gathered[half, start + k, :HALF, :], outer], axis=1))
    rows = jnp.concatenate(parts, axis=0)
    for i in range(0, 8, 2):
        grid = dot(rows, base[:, CZ * i : CZ * i + 2 * CZ])
        for j in range(2):
            total = (grid[:, CZ * j : CZ * j + CZ] + left[i + j : i + j + 1]).astype(jnp.bfloat16)
            for k in range(2):
                first = pl.multiple_of(TOK_DEV * (start + k) + HALF * half, HALF)
                result[i + j, pl.ds(first, HALF), :] = total[HALF * k : HALF * k + HALF]


def body(
    atoms, window_offsets, atom_token, w_query, w_key, w_value, w_out, w_token, gain_token, w_pair, w_outer
):
    hbm = pl.BlockSpec(memory_space=pltpu.HBM)
    dma = pltpu.SemaphoreType.DMA
    bf16, f32 = jnp.bfloat16, jnp.float32
    return pl.pallas_call(
        embed_kernel,
        out_shape=pltpu.VMEM((8, ROWS * TOK_DEV, CZ), bf16),
        in_specs=[hbm] * 11,
        out_specs=pl.BlockSpec(memory_space=pltpu.VMEM),
        scratch_shapes=[
            pltpu.SMEM((ATOMS_DEV // QB,), jnp.int32),
            pltpu.VMEM((ATOMS_DEV,), jnp.int32),
            pltpu.VMEM((AW, AW), bf16),
            pltpu.VMEM((AW, AW), bf16),
            pltpu.VMEM((AW, AW), bf16),
            pltpu.VMEM((AW, AW), bf16),
            pltpu.VMEM((AW, TW), bf16),
            pltpu.VMEM((TW,), bf16),
            pltpu.VMEM((2 * CZ + 2 * CO, TW), bf16),
            pltpu.VMEM((CO * CO, CZ), bf16),
            pltpu.VMEM((2, ROWS, BLK, CZ), bf16),
            pltpu.VMEM((2 * CZ, 8 * CZ), bf16),
            pltpu.VMEM((EXT, AW), bf16),
            pltpu.VMEM((EXT, AW), bf16),
            pltpu.VMEM((AW, ATOMS_DEV), bf16),
            pltpu.VMEM((2, AW + 16, EXT), bf16),
            pltpu.VMEM((AW, ATOMS_DEV), bf16),
            pltpu.VMEM((WIDE, ATOMS_DEV), bf16),
            pltpu.VMEM((AW, ATOMS_DEV), bf16),
            pltpu.VMEM((AW, AW), bf16),
            pltpu.VMEM((TW, AW), bf16),
            pltpu.VMEM((2 * CZ, TW), bf16),
            pltpu.VMEM((8, WIDE), f32),
            pltpu.VMEM((8, WIDE), f32),
            pltpu.VMEM((2, BLK, CZ), bf16),
            pltpu.VMEM((ROWS, 16, CZ), bf16),
            pltpu.VMEM((16, CZ), bf16),
            dma, dma((10,)), dma((2,)), dma((2,)), dma, dma,
            dma((2, 2)), dma((2, 2)), dma((2,)), dma((2, 4)), dma((2, 4)), dma((COLS,)), dma,
        ],
        compiler_params=pltpu.CompilerParams(
            collective_id=0, has_side_effects=True, vmem_limit_bytes=60 * 1024 * 1024
        ),
        name="embed",
    )(
        atoms, window_offsets, atom_token, w_query, w_key, w_value, w_out, w_token, gain_token, w_pair.T,
        w_outer,
    )


def solution(mesh):
    split = P(("row", "col"))
    placed = (P(("row", "col"), None), split, split) + (P(),) * 8
    return jax.shard_map(
        body, mesh=mesh, in_specs=placed, out_specs=P("row", "col", None), check_vma=False
    )
```

```python
import jax
import jax.numpy as jnp
from jax import lax
from jax.experimental import pallas as pl
from jax.experimental.pallas import tpu as pltpu
from jax.sharding import PartitionSpec as P

AW = 128
HEADS = 4
TW = 384
CZ = 128
CO = 32
QB = 32
RIM = 64
ROWS = 8
COLS = 32
DEVICES = ROWS * COLS
ATOMS_DEV = 1536
TOK_DEV = 128
NEXT = 128
NEXT_USED = 96
EXT = RIM + ATOMS_DEV + NEXT
WIDTH = ATOMS_DEV + NEXT
GROUP = 128
GROUPS = ATOMS_DEV // GROUP
UNITS = 2 * GROUPS
AHEAD = 3
BEHIND = 2
HALF = 64
EDGE = 16
TOKENS = (TOK_DEV - 2 * EDGE, 2 * EDGE)
BLOCK = (128, 48)
WIDE = TW + 128
EXP_SCALE = float(32 ** -0.5 * 1.4426950408889634)
MESH = pl.DeviceIdType.MESH
NT = (((1,), (1,)), ((), ()))


def dot(a, b):
    return jnp.dot(a, b, preferred_element_type=jnp.float32)


def place(device):
    return (lax.div(device, COLS), lax.rem(device, COLS))


def dot_nt(a, b):
    return lax.dot_general(a, b, NT, preferred_element_type=jnp.float32)


def turned(w):
    return w[...].astype(jnp.float32).T.astype(jnp.bfloat16)


def unit_scores(unit, keys, queries):
    g, j = unit // 2, unit % 2
    q = queries[:, GROUP * g : GROUP * g + GROUP]
    side = (lax.broadcasted_iota(jnp.int32, (HALF, GROUP), 0) // 32 == j) == (
        lax.broadcasted_iota(jnp.int32, (HALF, GROUP), 1) < HALF
    )
    none = jnp.zeros((HALF, GROUP), jnp.bfloat16)
    heads = [jnp.where(side, q[HALF * t : HALF * t + HALF], none) for t in range(2)]
    operand = jnp.concatenate(
        [jnp.concatenate([heads[0], none], axis=1), jnp.concatenate([none, heads[1]], axis=1)], axis=0
    )
    return dot(keys[HALF * unit : HALF * unit + 192, :], operand)


def unit_softmax(unit, scores, me, off, off_next):
    lane = lax.broadcasted_iota(jnp.int32, (1, GROUP), 1)
    second = lax.rem(lane // QB, 2) == 1
    if unit == UNITS:
        start = off_next[8:9, :].astype(jnp.int32) + RIM
    else:
        start = jnp.where(second, off[2 * unit + 1] + RIM + QB, off[2 * unit] + RIM)
    low, high = start, start + 128
    if unit == 0:
        low = jnp.maximum(low, jnp.where(me == 0, RIM, 0))
    if unit == UNITS - 1:
        high = jnp.minimum(high, jnp.where(me == DEVICES - 1, 128, 192))
    row = lax.broadcasted_iota(jnp.int32, (HALF, GROUP), 0)
    enters, stays = row >= low, row + 128 < high
    parts = []
    for t in range(2):
        tile = scores[:, GROUP * t : GROUP * t + GROUP]
        tile = jnp.concatenate(
            [jnp.where(enters, tile[:64], -1e30), tile[64:128], jnp.where(stays, tile[128:], -1e30)], axis=0
        )
        top = jnp.max(tile, axis=0, keepdims=True)
        parts.append(jnp.exp2((tile - top) * EXP_SCALE).astype(jnp.bfloat16))
    return jnp.concatenate(
        [jnp.concatenate(parts, axis=1), jnp.zeros((HALF, 2 * GROUP), jnp.bfloat16)], axis=0
    )


def group_store(g, mixed, att):
    left = lax.broadcasted_iota(jnp.int32, (1, GROUP), 1) < HALF
    for h in range(HEADS):
        lanes = slice(GROUP * (h // 2), GROUP * (h // 2) + GROUP)
        a, b = mixed if h % 2 == 0 else mixed[::-1]
        total = jnp.where(left, a[AW : AW + 1, lanes], b[AW : AW + 1, lanes])
        value = jnp.where(left, a[32 * h : 32 * h + 32, lanes], b[32 * h : 32 * h + 32, lanes]) * (1.0 / total)
        if h % 2 == 1:
            value = pltpu.roll(value, HALF, 1)
        att[32 * h : 32 * h + 32, GROUP * g : GROUP * g + GROUP] = value.astype(jnp.bfloat16)


def attend(units, me, off, off_next, keys, queries, values, att, mixed):
    scores, lifted = {}, {}
    for i in range(len(units) + AHEAD + BEHIND):
        if i < len(units):
            scores[i] = unit_scores(units[i], keys, queries)
        k = i - AHEAD
        if 0 <= k < len(units):
            lifted[k] = unit_softmax(units[k], scores.pop(k), me, off, off_next)
        k = i - AHEAD - BEHIND
        if 0 <= k < len(units):
            g, j = units[k] // 2, units[k] % 2
            mixed[units[k]] = dot(values[j, :, GROUP * g : GROUP * g + 2 * GROUP], lifted.pop(k))
            if units[k] == UNITS:
                mixed[UNITS + 1] = mixed[UNITS]
            if 2 * g in mixed and 2 * g + 1 in mixed:
                group_store(g, [mixed.pop(2 * g), mixed.pop(2 * g + 1)], att)


def hidden_rows(lo, hi, turned_atoms, att, w_out_t, w_token_t, hid):
    mixed = dot(w_out_t[...], att[:, lo:hi])
    update = (turned_atoms[:, lo:hi].astype(jnp.float32) + mixed).astype(jnp.bfloat16)
    hid[:TW, lo:hi] = jnp.maximum(dot(w_token_t[...], update), 0.0).astype(jnp.bfloat16)


def pooled_rows(first, count, lo, hi, device, token, hid, flags=None):
    slot = token[...].reshape(1, ATOMS_DEV)[:, lo:hi] - device * TOK_DEV
    rows = lax.broadcasted_iota(jnp.int32, (count, hi - lo), 0) + first
    one_hot = jnp.where(rows == slot, 1.0, 0.0).astype(jnp.bfloat16)
    if flags is not None:
        last = lax.broadcasted_iota(jnp.int32, (count, NEXT), 0) == count - 1
        one_hot = jnp.concatenate([one_hot, jnp.where(last, flags, 0.0).astype(jnp.bfloat16)], axis=1)
        hi += NEXT
    return dot_nt(one_hot, hid[:, lo:hi])


def token_normed(pooled, gain):
    count = pooled[:, TW:]
    single = pooled[:, :TW] / jnp.concatenate([count] * 3, axis=1)
    centre = single - jnp.mean(single, axis=1, keepdims=True)
    variance = jnp.mean(centre * centre, axis=1, keepdims=True)
    return (centre * lax.rsqrt(variance + 1e-05) * gain).astype(jnp.bfloat16)


def embed_kernel(
    atoms, off_hbm, token_hbm, wq_hbm, wk_hbm, wv_hbm, w_out_hbm, w_token_hbm, gain_hbm, w_pair_hbm, w_outer_hbm,
    result,
    off, token, wq, wk, wv, w_out, w_token, gain, w_pair, w_outer,
    gathered_inner, gathered_outer, base,
    ext, keys, queries, values, att, hid, turned_atoms, w_out_t, w_token_t, w_right,
    note_out, note_in, block_inner, block_outer, left_all, left_in,
    own_sem, load_sem, halo_send, halo_recv,
    first_send, first_recv, local_sem, pass_send, pass_recv, left_send, left_recv, far_ready, left_ready,
):
    gathered, block = (gathered_inner, gathered_outer), (block_inner, block_outer)
    row = lax.axis_index("row")
    col = lax.axis_index("col")
    me = row * COLS + col
    before = lax.rem(me + DEVICES - 1, DEVICES)
    after = lax.rem(me + 1, DEVICES)
    slot = lax.rem(me, ROWS)
    my_y, my_z = lax.div(row, 2), lax.rem(row, 2)
    my_x, my_zh = lax.div(col, 8), lax.rem(lax.div(col, 2), 4)
    depth = 2 * my_zh + my_z
    group_col = lax.div(me, ROWS)
    relay_y = lax.rem(my_y + 6 + my_zh - 2 * my_z - lax.div(my_x, 2), 4)
    targets = [(2 * relay_y + i) * COLS + group_col for i in range(2)]
    target_depth = [4 * my_z + 2 * lax.div(my_x, 2) + i for i in range(2)]

    def held_by(y):
        return 2 * lax.rem(y + 6 + my_zh - my_x, 4)

    held = held_by(my_y)
    sources = [ROWS * col + held + k for k in range(2)]
    source_depth = held + lax.div(my_zh, 2)
    keeps = jnp.where((targets[0] == me) | (targets[1] == me), 1, 0)
    col_in = lax.rem(col, 8)
    is_head, is_leader, is_first, is_last = col_in == 1, col == 1, me == 0, me == DEVICES - 1
    parent = jnp.where(is_leader, 0, jnp.where(is_head, row * COLS + 1, me - col_in + 1))

    def count(condition):
        return jnp.where(condition, 1, 0)

    def signal(device, semaphore=None):
        pl.semaphore_signal(
            barrier if semaphore is None else semaphore, inc=1, device_id=place(device), device_id_type=MESH
        )

    barrier = pltpu.get_barrier_semaphore()

    @pl.when(jnp.logical_not(is_first))
    def _():
        signal(before)

    @pl.when(jnp.logical_not(is_last))
    def _():
        signal(after)

    @pl.when(is_head)
    def _():
        signal(parent)

    arrivals = 2 + 3 - count(is_first) - count(is_last) + 8 * count(is_first) + 3 * count(is_leader)
    for k in range(2):
        @pl.when((sources[k] != me) & (source_depth >= depth))
        def _():
            signal(sources[k])

        arrivals += count((sources[k] != me) & (source_depth < depth))
    for i in range(2):
        @pl.when((targets[i] != me) & (target_depth[i] > depth))
        def _():
            signal(targets[i])

        arrivals += count((targets[i] != me) & (target_depth[i] <= depth))
    late_targets = sum(count((targets[i] != me) & (target_depth[i] > depth)) for i in range(2))
    for i in range(1, 4):
        signal((2 * lax.rem(my_y + i, 4) + my_z) * COLS + col)
    child = jnp.logical_not(is_head | is_first)
    arrivals += count(child)
    children = 7 - count((row == 0) & is_leader)

    def each_child(act):
        for c in range(8):
            if c != 1:
                @pl.when(is_head & (me + c != 1))
                def _():
                    act(me + c - 1, 16 + c)

    def each_leader(act):
        @pl.when(is_first)
        def _():
            for r in range(ROWS):
                act(r * COLS + 1, r)

    def each_head(act):
        @pl.when(is_leader)
        def _():
            for x in range(1, 4):
                act(me + 8 * x, 8 + x)

    each_child(lambda to, _: signal(to))

    own = pltpu.make_async_copy(atoms, ext.at[pl.ds(RIM, ATOMS_DEV)], own_sem)
    own.start()
    pieces = [
        (wq_hbm, wq), (wk_hbm, wk), (wv_hbm, wv), (off_hbm, off), (w_out_hbm, w_out),
        (token_hbm, token), (w_token_hbm, w_token), (gain_hbm, gain), (w_pair_hbm, w_pair),
        (w_outer_hbm, w_outer),
    ]
    loads = [pltpu.make_async_copy(a, b, load_sem.at[i]) for i, (a, b) in enumerate(pieces)]
    for load in loads:
        load.start()
    for load in loads[:3]:
        load.wait()

    one = lax.broadcasted_iota(jnp.int32, (CZ, CZ), 0) == lax.broadcasted_iota(jnp.int32, (CZ, CZ), 1)
    eye = jnp.where(one, 1.0, 0.0).astype(jnp.bfloat16)
    value_t = turned(wv)
    left_side = jnp.concatenate([turned(wq), value_t, eye], axis=0)
    hid[TW:, :] = jnp.ones((WIDE - TW, WIDTH), jnp.bfloat16)
    for j in range(2):
        values[j, AW:, :] = jnp.ones((16, WIDTH + GROUP), jnp.bfloat16)
    own.wait()
    for lo in range(0, ATOMS_DEV, 512):
        x = ext[RIM + lo : RIM + lo + 512, :]
        keys[RIM + lo : RIM + lo + 512, :] = dot(x, wk[...]).astype(jnp.bfloat16)
    def keep_product(lo, size, product):
        for h in range(HEADS):
            rows = slice(32 * h, 32 * h + 32)
            for part in range(0, size, GROUP):
                q = product[rows, part : part + GROUP]
                if h % 2 == 1:
                    q = pltpu.roll(q, HALF, 1)
                queries[rows, lo + part : lo + part + GROUP] = q.astype(jnp.bfloat16)
        values[1, :AW, lo : lo + size] = product[AW : 2 * AW].astype(jnp.bfloat16)
        turned_atoms[:, lo : lo + size] = product[2 * AW :].astype(jnp.bfloat16)

    for lo in range(0, ATOMS_DEV, 256):
        keep_product(lo, 256, dot_nt(left_side, ext[RIM + lo : RIM + lo + 256, :]))
    for lo in range(128, ATOMS_DEV, 256):
        hi = min(lo + 256, ATOMS_DEV)
        values[0, :AW, lo:hi] = dot_nt(value_t, ext[lo:hi, :]).astype(jnp.bfloat16)
    pad = jnp.zeros((RIM, AW), jnp.bfloat16)
    rest = jnp.concatenate([ext[ATOMS_DEV : ATOMS_DEV + RIM, :], pad], axis=0)
    values[0, :AW, ATOMS_DEV : ATOMS_DEV + GROUP] = dot_nt(value_t, rest).astype(jnp.bfloat16)

    for load in loads[3:]:
        load.wait()
    flags = token[...].reshape(1, ATOMS_DEV)[:, :NEXT] == me * TOK_DEV - 1
    upper = lax.broadcasted_iota(jnp.int32, (16, NEXT), 0) < 8
    note = jnp.where(upper, jnp.where(flags, 1.0, 0.0), off[0].astype(jnp.float32))
    note_out[...] = note.astype(jnp.bfloat16)
    ext[RIM + ATOMS_DEV + NEXT_USED :, :] = jnp.zeros((NEXT - NEXT_USED, AW), jnp.bfloat16)

    @pl.when(is_first)
    def _():
        ext[:RIM, :] = jnp.zeros((RIM, AW), jnp.bfloat16)

    @pl.when(is_last)
    def _():
        ext[RIM + ATOMS_DEV :, :] = jnp.zeros((NEXT, AW), jnp.bfloat16)
        note_in[...] = jnp.zeros((16, NEXT), jnp.bfloat16)

    pl.semaphore_wait(barrier, arrivals)
    for k in range(2):
        @pl.when((sources[k] != me) & (source_depth < depth))
        def _():
            signal(sources[k], far_ready)

    @pl.when(child)
    def _():
        signal(parent, left_ready)

    to_after = pltpu.make_async_remote_copy(
        src_ref=atoms.at[pl.ds(ATOMS_DEV - RIM, RIM)], dst_ref=ext.at[pl.ds(0, RIM)],
        send_sem=halo_send.at[0], recv_sem=halo_recv.at[0],
        device_id=place(after), device_id_type=MESH,
    )
    to_before = [
        pltpu.make_async_remote_copy(
            src_ref=atoms.at[pl.ds(0, NEXT_USED)], dst_ref=ext.at[pl.ds(RIM + ATOMS_DEV, NEXT_USED)],
            send_sem=halo_send.at[1], recv_sem=halo_recv.at[1],
            device_id=place(before), device_id_type=MESH,
        ),
        pltpu.make_async_remote_copy(
            src_ref=note_out, dst_ref=note_in, send_sem=halo_send.at[2], recv_sem=halo_recv.at[2],
            device_id=place(before), device_id_type=MESH,
        ),
    ]

    @pl.when(jnp.logical_not(is_last))
    def _():
        to_after.start()

    @pl.when(jnp.logical_not(is_first))
    def _():
        for copy in to_before:
            copy.start()

    for i in range(8):
        base[:CZ, CZ * i : CZ * i + CZ] = eye
    w_out_t[...] = turned(w_out)
    w_token_t[...] = turned(w_token)
    w_right[:CZ, :] = w_pair[CZ + CO : 2 * CZ + CO, :]
    for m in range(4):
        w_right[CZ + CO * m : CZ + CO * m + CO, :] = w_pair[2 * CZ + CO :, :]

    mixed = {}
    attend(list(range(1, UNITS - 1)), me, off, note_in, keys, queries, values, att, mixed)

    def first_copy(part, i):
        return pltpu.make_async_remote_copy(
            src_ref=block[part], dst_ref=gathered[part].at[slot],
            send_sem=first_send.at[part, i], recv_sem=first_recv.at[part, lax.rem(slot, 2)],
            device_id=place(targets[i]), device_id_type=MESH,
        )

    def local_copy(part):
        return pltpu.make_async_copy(block[part], gathered[part].at[slot], local_sem.at[part])

    def first_sends(part):
        for i in range(2):
            @pl.when(targets[i] != me)
            def _():
                first_copy(part, i).start()

        @pl.when(keeps == 1)
        def _():
            local_copy(part).start()

    def pass_copy(part, i, start):
        return pltpu.make_async_remote_copy(
            src_ref=gathered[part].at[pl.ds(start, 2)], dst_ref=gathered[part].at[pl.ds(start, 2)],
            send_sem=pass_send.at[part, i], recv_sem=pass_recv.at[part, i],
            device_id=(2 * lax.rem(my_y + i, 4) + my_z, col), device_id_type=MESH,
        )

    def pass_on(part):
        for k in range(2):
            @pl.when(sources[k] != me)
            def _():
                pltpu.make_async_remote_copy(
                    src_ref=block[part], dst_ref=gathered[part].at[held + k],
                    send_sem=first_send.at[part, 0], recv_sem=first_recv.at[part, k],
                    device_id=place(sources[k]), device_id_type=MESH,
                ).wait_recv()

        @pl.when(keeps == 1)
        def _():
            local_copy(part).wait()

        for i in range(1, 4):
            pass_copy(part, i, held).start()

    def finish(part, pooled):
        tokens = TOKENS[part]
        normed = token_normed(pooled, gain[...].reshape(1, TW).astype(jnp.float32))
        right = dot_nt(normed, w_right[...])
        quarter = tokens // 4
        lane = lax.broadcasted_iota(jnp.int32, (quarter, CZ), 1)
        packed = right[:quarter, CZ:]
        for m in range(1, 4):
            packed = jnp.where(lane // CO == m, right[quarter * m : quarter * m + quarter, CZ:], packed)
        empty = jnp.zeros((BLOCK[part] - tokens - quarter, CZ), jnp.float32)
        block[part][:tokens, :] = right[:, :CZ].astype(jnp.bfloat16)
        block[part][tokens:, :] = jnp.concatenate([packed, empty], axis=0).astype(jnp.bfloat16)
        return normed

    hidden_rows(GROUP, ATOMS_DEV - GROUP, turned_atoms, att, w_out_t, w_token_t, hid)
    pooled = pooled_rows(EDGE, TOKENS[0], GROUP, ATOMS_DEV - GROUP, me, token, hid)
    inner = finish(0, pooled)

    @pl.when(late_targets == 0)
    def _():
        first_sends(0)

    @pl.when(jnp.logical_not(is_last))
    def _():
        for copy in to_before:
            copy.wait_recv()

    @pl.when(jnp.logical_not(is_first))
    def _():
        to_after.wait_recv()

    keys[:RIM, :] = dot(ext[:RIM, :], wk[...]).astype(jnp.bfloat16)
    values[0, :AW, :GROUP] = dot_nt(value_t, ext[:GROUP, :]).astype(jnp.bfloat16)
    x = ext[RIM + ATOMS_DEV :, :]
    keys[RIM + ATOMS_DEV :, :] = dot(x, wk[...]).astype(jnp.bfloat16)
    keep_product(ATOMS_DEV, NEXT, dot_nt(left_side, x))
    rest = jnp.concatenate([ext[ATOMS_DEV:, :], pad], axis=0)
    values[0, :AW, ATOMS_DEV:] = dot_nt(value_t, rest).astype(jnp.bfloat16)
    attend([0, UNITS, UNITS - 1], me, off, note_in, keys, queries, values, att, mixed)

    hidden_rows(0, GROUP, turned_atoms, att, w_out_t, w_token_t, hid)
    hidden_rows(ATOMS_DEV - GROUP, WIDTH, turned_atoms, att, w_out_t, w_token_t, hid)
    low = pooled_rows(0, EDGE, 0, 256, me, token, hid)
    flags = note_in[:1, :].astype(jnp.float32)
    high = pooled_rows(TOK_DEV - EDGE, EDGE, ATOMS_DEV - 256, ATOMS_DEV, me, token, hid, flags)
    outer = finish(1, jnp.concatenate([low, high], axis=0))

    @pl.when(late_targets == 0)
    def _():
        first_sends(1)

    def left_copy(source, to, index):
        return pltpu.make_async_remote_copy(
            src_ref=source, dst_ref=left_in, send_sem=left_send.at[index], recv_sem=left_recv,
            device_id=place(to), device_id_type=MESH,
        )

    def left_to(child, index):
        return left_copy(left_all.at[index] if index < ROWS else left_in, child, index)

    @pl.when(is_first)
    def _():
        normed = jnp.concatenate([outer[:EDGE], inner[: HALF - EDGE]], axis=0)
        left = dot_nt(normed, w_pair[: 2 * CZ, :])
        for r in range(ROWS):
            rows = left[8 * r : 8 * r + 8]
            left_all[r] = jnp.concatenate([rows[:, :CZ], rows[:, CZ:]], axis=0).astype(jnp.bfloat16)
        left_in[...] = left_all[0]

    each_leader(lambda to, index: left_to(to, index).start())

    @pl.when(is_leader)
    def _():
        left_copy(left_in, parent, 0).wait_recv()

    each_head(lambda to, index: left_to(to, index).start())

    @pl.when(late_targets != 0)
    def _():
        pl.semaphore_wait(far_ready, late_targets)
        first_sends(0)
        first_sends(1)

    @pl.when(is_head & jnp.logical_not(is_leader))
    def _():
        left_copy(left_in, parent, 0).wait_recv()

    @pl.when(is_head)
    def _():
        pl.semaphore_wait(left_ready, children)

    each_child(lambda to, index: left_to(to, index).start())
    pass_on(0)
    pass_on(1)

    @pl.when(child)
    def _():
        left_copy(left_in, parent, 0).wait_recv()

    mix_left(left_in, w_outer, base)
    left = left_in[:8, :].astype(jnp.float32)

    def arrived(part):
        for i in range(1, 4):
            theirs = held_by(my_y + 4 - i)
            pass_copy(part, i, theirs).wait_recv()
            pair_block(gathered[part], part, theirs, base, left, result)

    pair_block(gathered[0], 0, held, base, left, result)
    arrived(0)
    pair_block(gathered[1], 1, held, base, left, result)
    arrived(1)

    for each in (each_leader, each_head, each_child):
        each(lambda to, index: left_to(to, index).wait_send())

    @pl.when(jnp.logical_not(is_last))
    def _():
        to_after.wait_send()

    @pl.when(jnp.logical_not(is_first))
    def _():
        for copy in to_before:
            copy.wait_send()

    for part in range(2):
        for i in range(1, 4):
            pass_copy(part, i, held).wait_send()
        for i in range(2):
            @pl.when(targets[i] != me)
            def _():
                first_copy(part, i).wait_send()


def mix_left(left_in, w_outer, base):
    outer = left_in[8:, :CO]
    spread = lax.broadcasted_iota(jnp.int32, (CO, CO * CO), 1) // CO
    spread = jnp.where(spread == lax.broadcasted_iota(jnp.int32, (CO, CO * CO), 0), 1.0, 0.0)
    wide = dot(outer, spread.astype(jnp.bfloat16))
    n = lax.broadcasted_iota(jnp.int32, (CO, CO * CO), 0)
    mine = lax.rem(lax.broadcasted_iota(jnp.int32, (CO, CO * CO), 1), CO) == n
    expanded = [jnp.where(mine, wide[i : i + 1], 0.0).astype(jnp.bfloat16) for i in range(8)]
    mixing = dot(jnp.concatenate(expanded, axis=0), w_outer[...]).astype(jnp.bfloat16)
    for i in range(8):
        for k in range(4):
            base[CZ + CO * k : CZ + CO * k + CO, CZ * i : CZ * i + CZ] = mixing[CO * i : CO * i + CO]


def pair_block(gathered, part, start, base, left, result):
    tokens, quarter = TOKENS[part], TOKENS[part] // 4
    lane = lax.broadcasted_iota(jnp.int32, (quarter, CZ), 1)
    pieces = []
    for k in range(2):
        packed = gathered[start + k, tokens:, :].astype(jnp.float32)[:quarter]
        outer = [jnp.where(lane // CO == m, packed, 0.0) for m in range(4)]
        outer = jnp.concatenate(outer, axis=0).astype(jnp.bfloat16)
        pieces.append(jnp.concatenate([gathered[start + k, :tokens, :], outer], axis=1))
    rows = jnp.concatenate(pieces, axis=0)
    spans = [(0, EDGE, tokens)] if part == 0 else [(0, 0, EDGE), (EDGE, TOK_DEV - EDGE, EDGE)]
    for i in range(0, 8, 2):
        grid = dot(rows, base[:, CZ * i : CZ * i + 2 * CZ])
        for j in range(2):
            total = (grid[:, CZ * j : CZ * j + CZ] + left[i + j : i + j + 1]).astype(jnp.bfloat16)
            for k in range(2):
                for first, to, size in spans:
                    target = pl.multiple_of(TOK_DEV * (start + k) + to, EDGE)
                    result[i + j, pl.ds(target, size), :] = total[tokens * k + first : tokens * k + first + size]


def body(
    atoms, window_offsets, atom_token, w_query, w_key, w_value, w_out, w_token, gain_token, w_pair, w_outer
):
    hbm = pl.BlockSpec(memory_space=pltpu.HBM)
    dma = pltpu.SemaphoreType.DMA
    bf16 = jnp.bfloat16
    return pl.pallas_call(
        embed_kernel,
        out_shape=pltpu.VMEM((8, ROWS * TOK_DEV, CZ), bf16),
        in_specs=[hbm] * 11,
        out_specs=pl.BlockSpec(memory_space=pltpu.VMEM),
        scratch_shapes=[
            pltpu.SMEM((ATOMS_DEV // QB,), jnp.int32),
            pltpu.VMEM((ATOMS_DEV,), jnp.int32),
            pltpu.VMEM((AW, AW), bf16),
            pltpu.VMEM((AW, AW), bf16),
            pltpu.VMEM((AW, AW), bf16),
            pltpu.VMEM((AW, AW), bf16),
            pltpu.VMEM((AW, TW), bf16),
            pltpu.VMEM((TW,), bf16),
            pltpu.VMEM((2 * CZ + 2 * CO, TW), bf16),
            pltpu.VMEM((CO * CO, CZ), bf16),
            pltpu.VMEM((ROWS, BLOCK[0], CZ), bf16),
            pltpu.VMEM((ROWS, BLOCK[1], CZ), bf16),
            pltpu.VMEM((2 * CZ, 8 * CZ), bf16),
            pltpu.VMEM((EXT, AW), bf16),
            pltpu.VMEM((EXT, AW), bf16),
            pltpu.VMEM((AW, WIDTH), bf16),
            pltpu.VMEM((2, AW + 16, WIDTH + GROUP), bf16),
            pltpu.VMEM((AW, WIDTH), bf16),
            pltpu.VMEM((WIDE, WIDTH), bf16),
            pltpu.VMEM((AW, WIDTH), bf16),
            pltpu.VMEM((AW, AW), bf16),
            pltpu.VMEM((TW, AW), bf16),
            pltpu.VMEM((2 * CZ, TW), bf16),
            pltpu.VMEM((16, NEXT), bf16),
            pltpu.VMEM((16, NEXT), bf16),
            pltpu.VMEM((BLOCK[0], CZ), bf16),
            pltpu.VMEM((BLOCK[1], CZ), bf16),
            pltpu.VMEM((ROWS, 16, CZ), bf16),
            pltpu.VMEM((16, CZ), bf16),
            dma, dma((10,)), dma((3,)), dma((3,)),
            dma((2, 2)), dma((2, 2)), dma((2,)), dma((2, 4)), dma((2, 4)), dma((COLS,)), dma,
            pltpu.SemaphoreType.REGULAR, pltpu.SemaphoreType.REGULAR,
        ],
        compiler_params=pltpu.CompilerParams(
            collective_id=0, has_side_effects=True, vmem_limit_bytes=60 * 1024 * 1024
        ),
        name="embed",
    )(
        atoms, window_offsets, atom_token, w_query, w_key, w_value, w_out, w_token, gain_token, w_pair.T,
        w_outer,
    )


def solution(mesh):
    split = P(("row", "col"))
    placed = (P(("row", "col"), None), split, split) + (P(),) * 8
    return jax.shard_map(
        body, mesh=mesh, in_specs=placed, out_specs=P("row", "col", None), check_vma=False
    )
```

```python
import jax
import jax.numpy as jnp
from jax import lax
from jax.experimental import pallas as pl
from jax.experimental.pallas import tpu as pltpu
from jax.sharding import PartitionSpec as P

AW = 128
HEADS = 4
TW = 384
CZ = 128
CO = 32
QB = 32
RIM = 64
ROWS = 8
COLS = 32
DEVICES = ROWS * COLS
ATOMS_DEV = 1536
TOK_DEV = 128
NEXT = 128
NEXT_USED = 96
EXT = RIM + ATOMS_DEV + NEXT
WIDTH = ATOMS_DEV + NEXT
GROUP = 128
GROUPS = ATOMS_DEV // GROUP
UNITS = 2 * GROUPS
AHEAD = 3
BEHIND = 2
HALF = 64
EDGE = 16
INNER = ((UNITS - 2, 128, 1408, 16, 96, 128, 1408),)
TOKENS = tuple(piece[4] for piece in INNER) + (32,)
PARTS = len(TOKENS)
SPANS = tuple(((0, piece[3], piece[4]),) for piece in INNER) + (((0, 0, 16), (16, 112, 16)),)
WIDE = TW + 128
EXP_SCALE = float(32 ** -0.5 * 1.4426950408889634)
MESH = pl.DeviceIdType.MESH
NT = (((1,), (1,)), ((), ()))


def dot(a, b):
    return jnp.dot(a, b, preferred_element_type=jnp.float32)


def place(device):
    return (lax.div(device, COLS), lax.rem(device, COLS))


def dot_nt(a, b):
    return lax.dot_general(a, b, NT, preferred_element_type=jnp.float32)


def turned(w):
    return w[...].astype(jnp.float32).T.astype(jnp.bfloat16)


def unit_scores(unit, keys, queries):
    g, j = unit // 2, unit % 2
    q = queries[:, GROUP * g : GROUP * g + GROUP]
    side = (lax.broadcasted_iota(jnp.int32, (HALF, GROUP), 0) // 32 == j) == (
        lax.broadcasted_iota(jnp.int32, (HALF, GROUP), 1) < HALF
    )
    none = jnp.zeros((HALF, GROUP), jnp.bfloat16)
    heads = [jnp.where(side, q[HALF * t : HALF * t + HALF], none) for t in range(2)]
    operand = jnp.concatenate(
        [jnp.concatenate([heads[0], none], axis=1), jnp.concatenate([none, heads[1]], axis=1)], axis=0
    )
    return dot(keys[HALF * unit : HALF * unit + 192, :], operand)


def unit_softmax(unit, scores, me, off, off_next):
    lane = lax.broadcasted_iota(jnp.int32, (1, GROUP), 1)
    second = lax.rem(lane // QB, 2) == 1
    if unit == UNITS:
        start = off_next[8:9, :].astype(jnp.int32) + RIM
    else:
        start = jnp.where(second, off[2 * unit + 1] + RIM + QB, off[2 * unit] + RIM)
    low, high = start, start + 128
    if unit == 0:
        low = jnp.maximum(low, jnp.where(me == 0, RIM, 0))
    if unit == UNITS - 1:
        high = jnp.minimum(high, jnp.where(me == DEVICES - 1, 128, 192))
    row = lax.broadcasted_iota(jnp.int32, (HALF, GROUP), 0)
    enters, stays = row >= low, row + 128 < high
    parts = []
    for t in range(2):
        tile = scores[:, GROUP * t : GROUP * t + GROUP]
        tile = jnp.concatenate(
            [jnp.where(enters, tile[:64], -1e30), tile[64:128], jnp.where(stays, tile[128:], -1e30)], axis=0
        )
        top = jnp.max(tile, axis=0, keepdims=True)
        parts.append(jnp.exp2((tile - top) * EXP_SCALE).astype(jnp.bfloat16))
    return jnp.concatenate(
        [jnp.concatenate(parts, axis=1), jnp.zeros((HALF, 2 * GROUP), jnp.bfloat16)], axis=0
    )


def group_store(g, mixed, att):
    left = lax.broadcasted_iota(jnp.int32, (1, GROUP), 1) < HALF
    for h in range(HEADS):
        lanes = slice(GROUP * (h // 2), GROUP * (h // 2) + GROUP)
        a, b = mixed if h % 2 == 0 else mixed[::-1]
        total = jnp.where(left, a[AW : AW + 1, lanes], b[AW : AW + 1, lanes])
        value = jnp.where(left, a[32 * h : 32 * h + 32, lanes], b[32 * h : 32 * h + 32, lanes]) * (1.0 / total)
        if h % 2 == 1:
            value = pltpu.roll(value, HALF, 1)
        att[32 * h : 32 * h + 32, GROUP * g : GROUP * g + GROUP] = value.astype(jnp.bfloat16)


def attend(units, me, off, off_next, keys, queries, values, att, mixed):
    scores, lifted = {}, {}
    for i in range(len(units) + AHEAD + BEHIND):
        if i < len(units):
            scores[i] = unit_scores(units[i], keys, queries)
        k = i - AHEAD
        if 0 <= k < len(units):
            lifted[k] = unit_softmax(units[k], scores.pop(k), me, off, off_next)
        k = i - AHEAD - BEHIND
        if 0 <= k < len(units):
            g, j = units[k] // 2, units[k] % 2
            mixed[units[k]] = dot(values[j, :, GROUP * g : GROUP * g + 2 * GROUP], lifted.pop(k))
            if units[k] == UNITS:
                mixed[UNITS + 1] = mixed[UNITS]
            if 2 * g in mixed and 2 * g + 1 in mixed:
                group_store(g, [mixed.pop(2 * g), mixed.pop(2 * g + 1)], att)
            yield units[k]


def hidden_rows(lo, hi, turned_atoms, att, w_out_t, w_token_t, hid):
    mixed = dot(w_out_t[...], att[:, lo:hi])
    update = (turned_atoms[:, lo:hi].astype(jnp.float32) + mixed).astype(jnp.bfloat16)
    hid[:TW, lo:hi] = jnp.maximum(dot(w_token_t[...], update), 0.0).astype(jnp.bfloat16)


def pooled_rows(first, count, lo, hi, device, token, hid, flags=None):
    slot = token[...].reshape(1, ATOMS_DEV)[:, lo:hi] - device * TOK_DEV
    rows = lax.broadcasted_iota(jnp.int32, (count, hi - lo), 0) + first
    one_hot = jnp.where(rows == slot, 1.0, 0.0).astype(jnp.bfloat16)
    if flags is not None:
        last = lax.broadcasted_iota(jnp.int32, (count, NEXT), 0) == count - 1
        one_hot = jnp.concatenate([one_hot, jnp.where(last, flags, 0.0).astype(jnp.bfloat16)], axis=1)
        hi += NEXT
    return dot_nt(one_hot, hid[:, lo:hi])


def token_normed(pooled, gain):
    count = pooled[:, TW:]
    single = pooled[:, :TW] / jnp.concatenate([count] * 3, axis=1)
    centre = single - jnp.mean(single, axis=1, keepdims=True)
    variance = jnp.mean(centre * centre, axis=1, keepdims=True)
    return (centre * lax.rsqrt(variance + 1e-05) * gain).astype(jnp.bfloat16)


def embed_kernel(
    atoms, off_hbm, token_hbm, wq_hbm, wk_hbm, wv_hbm, w_out_hbm, w_token_hbm, gain_hbm, w_pair_hbm, w_outer_hbm,
    result,
    off, token, wq, wk, wv, w_out, w_token, gain, w_pair, w_outer,
    gathered0, gathered1, base,
    ext, keys, queries, values, att, hid, turned_atoms, w_out_t, w_token_t, w_right,
    note_out, note_in, block0, block1, left_all, left_in,
    own_sem, load_sem, halo_send, halo_recv,
    first_send, first_recv, local_sem, pass_send, pass_recv, left_send, left_recv, far_ready, left_ready,
):
    gathered, block = (gathered0, gathered1), (block0, block1)
    row = lax.axis_index("row")
    col = lax.axis_index("col")
    me = row * COLS + col
    before = lax.rem(me + DEVICES - 1, DEVICES)
    after = lax.rem(me + 1, DEVICES)
    slot = lax.rem(me, ROWS)
    my_y, my_z = lax.div(row, 2), lax.rem(row, 2)
    my_x, my_zh = lax.div(col, 8), lax.rem(lax.div(col, 2), 4)
    depth = 2 * my_zh + my_z
    group_col = lax.div(me, ROWS)
    relay_y = lax.rem(my_y + 6 + my_zh - 2 * my_z - lax.div(my_x, 2), 4)
    my_core = lax.rem(col, 2)
    target = (2 * relay_y + my_core) * COLS + group_col
    target_depth = 4 * my_z + 2 * lax.div(my_x, 2) + my_core

    def held_by(y, z):
        return 2 * lax.rem(y + 6 + my_zh - my_x, 4) + z

    held = held_by(my_y, my_z)
    source = ROWS * col + held
    source_depth = 2 * lax.div(held, 2) + lax.div(my_zh, 2)
    keeps = target == me
    peers = [(i, j) for i in range(4) for j in range(2) if i + j > 0]
    col_in = lax.rem(col, 8)
    is_head, is_leader, is_first, is_last = col_in == 1, col == 1, me == 0, me == DEVICES - 1
    parent = jnp.where(is_leader, 0, jnp.where(is_head, row * COLS + 1, me - col_in + 1))

    def count(condition):
        return jnp.where(condition, 1, 0)

    def signal(device, semaphore=None):
        pl.semaphore_signal(
            barrier if semaphore is None else semaphore, inc=1, device_id=place(device), device_id_type=MESH
        )

    own = pltpu.make_async_copy(atoms, ext.at[pl.ds(RIM, ATOMS_DEV)], own_sem)
    own.start()
    pieces = [
        (wq_hbm, wq), (wk_hbm, wk), (wv_hbm, wv), (off_hbm, off), (w_out_hbm, w_out),
        (token_hbm, token), (w_token_hbm, w_token), (gain_hbm, gain), (w_pair_hbm, w_pair),
        (w_outer_hbm, w_outer),
    ]
    loads = [pltpu.make_async_copy(a, b, load_sem.at[i]) for i, (a, b) in enumerate(pieces)]
    for load in loads:
        load.start()

    barrier = pltpu.get_barrier_semaphore()

    @pl.when(jnp.logical_not(is_first))
    def _():
        signal(before)

    @pl.when(jnp.logical_not(is_last))
    def _():
        signal(after)

    @pl.when(is_head)
    def _():
        signal(parent)

    arrivals = 2 - count(is_first) - count(is_last) + 8 * count(is_first) + 3 * count(is_leader)

    @pl.when((source != me) & (source_depth >= depth))
    def _():
        signal(source)

    @pl.when(jnp.logical_not(keeps) & (target_depth > depth))
    def _():
        signal(target)

    arrivals += count((source != me) & (source_depth < depth))
    arrivals += count(jnp.logical_not(keeps) & (target_depth <= depth))
    late_target = jnp.logical_not(keeps) & (target_depth > depth)

    def peer(i, j):
        return (2 * lax.rem(my_y + i, 4) + lax.rem(my_z + j, 2)) * COLS + col

    for i, j in peers:
        signal(peer(i, j))
    arrivals += len(peers)
    child = jnp.logical_not(is_head | is_first)
    arrivals += count(child)
    children = 7 - count((row == 0) & is_leader)

    def each_child(act):
        for c in range(8):
            if c != 1:
                @pl.when(is_head & (me + c != 1))
                def _():
                    act(me + c - 1, 16 + c)

    def each_leader(act):
        @pl.when(is_first)
        def _():
            for r in range(ROWS):
                act(r * COLS + 1, r)

    def each_head(act):
        @pl.when(is_leader)
        def _():
            for x in range(1, 4):
                act(me + 8 * x, 8 + x)

    each_child(lambda to, _: signal(to))

    for load in loads[:3]:
        load.wait()

    one = lax.broadcasted_iota(jnp.int32, (CZ, CZ), 0) == lax.broadcasted_iota(jnp.int32, (CZ, CZ), 1)
    eye = jnp.where(one, 1.0, 0.0).astype(jnp.bfloat16)
    value_t = turned(wv)
    left_side = jnp.concatenate([turned(wq), value_t, eye], axis=0)
    hid[TW:, :] = jnp.ones((WIDE - TW, WIDTH), jnp.bfloat16)
    for j in range(2):
        values[j, AW:, :] = jnp.ones((16, WIDTH + GROUP), jnp.bfloat16)
    own.wait()
    for lo in range(0, ATOMS_DEV, 512):
        x = ext[RIM + lo : RIM + lo + 512, :]
        keys[RIM + lo : RIM + lo + 512, :] = dot(x, wk[...]).astype(jnp.bfloat16)
    def keep_product(lo, size, product):
        for h in range(HEADS):
            rows = slice(32 * h, 32 * h + 32)
            for part in range(0, size, GROUP):
                q = product[rows, part : part + GROUP]
                if h % 2 == 1:
                    q = pltpu.roll(q, HALF, 1)
                queries[rows, lo + part : lo + part + GROUP] = q.astype(jnp.bfloat16)
        values[1, :AW, lo : lo + size] = product[AW : 2 * AW].astype(jnp.bfloat16)
        turned_atoms[:, lo : lo + size] = product[2 * AW :].astype(jnp.bfloat16)

    for lo in range(0, ATOMS_DEV, 256):
        keep_product(lo, 256, dot_nt(left_side, ext[RIM + lo : RIM + lo + 256, :]))
    for lo in range(128, ATOMS_DEV, 256):
        hi = min(lo + 256, ATOMS_DEV)
        values[0, :AW, lo:hi] = dot_nt(value_t, ext[lo:hi, :]).astype(jnp.bfloat16)
    pad = jnp.zeros((RIM, AW), jnp.bfloat16)
    rest = jnp.concatenate([ext[ATOMS_DEV : ATOMS_DEV + RIM, :], pad], axis=0)
    values[0, :AW, ATOMS_DEV : ATOMS_DEV + GROUP] = dot_nt(value_t, rest).astype(jnp.bfloat16)

    for load in loads[3:]:
        load.wait()
    flags = token[...].reshape(1, ATOMS_DEV)[:, :NEXT] == me * TOK_DEV - 1
    upper = lax.broadcasted_iota(jnp.int32, (16, NEXT), 0) < 8
    note = jnp.where(upper, jnp.where(flags, 1.0, 0.0), off[0].astype(jnp.float32))
    note_out[...] = note.astype(jnp.bfloat16)
    ext[RIM + ATOMS_DEV + NEXT_USED :, :] = jnp.zeros((NEXT - NEXT_USED, AW), jnp.bfloat16)

    @pl.when(is_first)
    def _():
        ext[:RIM, :] = jnp.zeros((RIM, AW), jnp.bfloat16)

    @pl.when(is_last)
    def _():
        ext[RIM + ATOMS_DEV :, :] = jnp.zeros((NEXT, AW), jnp.bfloat16)
        note_in[...] = jnp.zeros((16, NEXT), jnp.bfloat16)

    pl.semaphore_wait(barrier, arrivals)

    @pl.when((source != me) & (source_depth < depth))
    def _():
        signal(source, far_ready)

    @pl.when(child)
    def _():
        signal(parent, left_ready)

    to_after = pltpu.make_async_remote_copy(
        src_ref=atoms.at[pl.ds(ATOMS_DEV - RIM, RIM)], dst_ref=ext.at[pl.ds(0, RIM)],
        send_sem=halo_send.at[0], recv_sem=halo_recv.at[0],
        device_id=place(after), device_id_type=MESH,
    )
    to_before = [
        pltpu.make_async_remote_copy(
            src_ref=atoms.at[pl.ds(0, NEXT_USED)], dst_ref=ext.at[pl.ds(RIM + ATOMS_DEV, NEXT_USED)],
            send_sem=halo_send.at[1], recv_sem=halo_recv.at[1],
            device_id=place(before), device_id_type=MESH,
        ),
        pltpu.make_async_remote_copy(
            src_ref=note_out, dst_ref=note_in, send_sem=halo_send.at[2], recv_sem=halo_recv.at[2],
            device_id=place(before), device_id_type=MESH,
        ),
    ]

    @pl.when(jnp.logical_not(is_last))
    def _():
        to_after.start()

    @pl.when(jnp.logical_not(is_first))
    def _():
        for copy in to_before:
            copy.start()

    for i in range(8):
        base[:CZ, CZ * i : CZ * i + CZ] = eye
    w_out_t[...] = turned(w_out)
    w_token_t[...] = turned(w_token)
    w_right[:CZ, :] = w_pair[CZ + CO : 2 * CZ + CO, :]
    for m in range(4):
        w_right[CZ + CO * m : CZ + CO * m + CO, :] = w_pair[2 * CZ + CO :, :]

    mixed = {}
    inner_units = attend(list(range(1, UNITS - 1)), me, off, note_in, keys, queries, values, att, mixed)

    def first_copy(part):
        return pltpu.make_async_remote_copy(
            src_ref=block[part], dst_ref=gathered[part].at[slot],
            send_sem=first_send.at[part], recv_sem=first_recv.at[part],
            device_id=place(target), device_id_type=MESH,
        )

    def local_copy(part):
        return pltpu.make_async_copy(block[part], gathered[part].at[slot], local_sem.at[part])

    def first_sends(part):
        @pl.when(jnp.logical_not(keeps))
        def _():
            first_copy(part).start()

        @pl.when(keeps)
        def _():
            local_copy(part).start()

    def pass_copy(part, i, j, holder):
        return pltpu.make_async_remote_copy(
            src_ref=gathered[part].at[holder], dst_ref=gathered[part].at[holder],
            send_sem=pass_send.at[part, 2 * i + j], recv_sem=pass_recv.at[part, 2 * i + j],
            device_id=place(peer(i, j)), device_id_type=MESH,
        )

    def pass_on(part):
        @pl.when(source != me)
        def _():
            pltpu.make_async_remote_copy(
                src_ref=block[part], dst_ref=gathered[part].at[held],
                send_sem=first_send.at[part], recv_sem=first_recv.at[part],
                device_id=place(source), device_id_type=MESH,
            ).wait_recv()

        @pl.when(source == me)
        def _():
            local_copy(part).wait()

        for i, j in peers:
            pass_copy(part, i, j, held).start()

    def finish(part, pooled):
        tokens = TOKENS[part]
        normed = token_normed(pooled, gain[...].reshape(1, TW).astype(jnp.float32))
        right = dot_nt(normed, w_right[...])
        lane = lax.broadcasted_iota(jnp.int32, (16, CZ), 1)
        packed = []
        for m in range(tokens // 16):
            rows = right[16 * m : 16 * m + 16, CZ:]
            if m % 4 == 0:
                packed.append(rows)
            else:
                packed[-1] = jnp.where(lane // CO == m % 4, rows, packed[-1])
        packed = jnp.concatenate(packed, axis=0)
        block[part][:tokens, :] = right[:, :CZ].astype(jnp.bfloat16)
        block[part][tokens:, :] = packed.astype(jnp.bfloat16)
        return normed

    def early_sends(part):
        @pl.when(jnp.logical_not(late_target))
        def _():
            first_sends(part)

    normed = []
    for part, (last, lo, hi, first, number, start, stop) in enumerate(INNER):
        for unit in inner_units:
            if unit == last:
                break
        hidden_rows(lo, hi, turned_atoms, att, w_out_t, w_token_t, hid)
        normed.append(finish(part, pooled_rows(first, number, start, stop, me, token, hid)))
        early_sends(part)

    @pl.when(jnp.logical_not(is_last))
    def _():
        for copy in to_before:
            copy.wait_recv()

    @pl.when(jnp.logical_not(is_first))
    def _():
        to_after.wait_recv()

    keys[:RIM, :] = dot(ext[:RIM, :], wk[...]).astype(jnp.bfloat16)
    values[0, :AW, :GROUP] = dot_nt(value_t, ext[:GROUP, :]).astype(jnp.bfloat16)
    x = ext[RIM + ATOMS_DEV :, :]
    keys[RIM + ATOMS_DEV :, :] = dot(x, wk[...]).astype(jnp.bfloat16)
    keep_product(ATOMS_DEV, NEXT, dot_nt(left_side, x))
    rest = jnp.concatenate([ext[ATOMS_DEV:, :], pad], axis=0)
    values[0, :AW, ATOMS_DEV:] = dot_nt(value_t, rest).astype(jnp.bfloat16)
    for _ in attend([0, UNITS, UNITS - 1], me, off, note_in, keys, queries, values, att, mixed):
        pass

    hidden_rows(0, GROUP, turned_atoms, att, w_out_t, w_token_t, hid)
    hidden_rows(ATOMS_DEV - GROUP, WIDTH, turned_atoms, att, w_out_t, w_token_t, hid)
    low = pooled_rows(0, EDGE, 0, 256, me, token, hid)
    flags = note_in[:1, :].astype(jnp.float32)
    high = pooled_rows(TOK_DEV - EDGE, EDGE, ATOMS_DEV - 256, ATOMS_DEV, me, token, hid, flags)
    outer = finish(PARTS - 1, jnp.concatenate([low, high], axis=0))

    early_sends(PARTS - 1)

    def left_copy(source, to, index):
        return pltpu.make_async_remote_copy(
            src_ref=source, dst_ref=left_in, send_sem=left_send.at[index], recv_sem=left_recv,
            device_id=place(to), device_id_type=MESH,
        )

    def left_to(child, index):
        return left_copy(left_all.at[index] if index < ROWS else left_in, child, index)

    @pl.when(is_first)
    def _():
        first_rows = jnp.concatenate([outer[:EDGE], normed[0][: HALF - EDGE]], axis=0)
        left = dot_nt(first_rows, w_pair[: 2 * CZ, :])
        for r in range(ROWS):
            rows = left[8 * r : 8 * r + 8]
            left_all[r] = jnp.concatenate([rows[:, :CZ], rows[:, CZ:]], axis=0).astype(jnp.bfloat16)
        left_in[...] = left_all[0]

    each_leader(lambda to, index: left_to(to, index).start())

    @pl.when(is_leader)
    def _():
        left_copy(left_in, parent, 0).wait_recv()

    each_head(lambda to, index: left_to(to, index).start())

    @pl.when(late_target)
    def _():
        pl.semaphore_wait(far_ready, 1)
        for part in range(PARTS):
            first_sends(part)

    @pl.when(is_head & jnp.logical_not(is_leader))
    def _():
        left_copy(left_in, parent, 0).wait_recv()

    @pl.when(is_head)
    def _():
        pl.semaphore_wait(left_ready, children)

    each_child(lambda to, index: left_to(to, index).start())
    for part in range(PARTS):
        pass_on(part)

    @pl.when(child)
    def _():
        left_copy(left_in, parent, 0).wait_recv()

    mix_left(left_in, w_outer, base)
    left = left_in[:8, :].astype(jnp.float32)

    for part in range(PARTS):
        for i, j in peers:
            pass_copy(part, i, j, held_by(my_y + 4 - i, lax.rem(my_z + j, 2))).wait_recv()
        pair_part(gathered[part], part, base, left, result)

    for each in (each_leader, each_head, each_child):
        each(lambda to, index: left_to(to, index).wait_send())

    @pl.when(jnp.logical_not(is_last))
    def _():
        to_after.wait_send()

    @pl.when(jnp.logical_not(is_first))
    def _():
        for copy in to_before:
            copy.wait_send()

    for part in range(PARTS):
        for i, j in peers:
            pass_copy(part, i, j, held).wait_send()

        @pl.when(jnp.logical_not(keeps))
        def _():
            first_copy(part).wait_send()


def mix_left(left_in, w_outer, base):
    outer = left_in[8:, :CO]
    spread = lax.broadcasted_iota(jnp.int32, (CO, CO * CO), 1) // CO
    spread = jnp.where(spread == lax.broadcasted_iota(jnp.int32, (CO, CO * CO), 0), 1.0, 0.0)
    wide = dot(outer, spread.astype(jnp.bfloat16))
    n = lax.broadcasted_iota(jnp.int32, (CO, CO * CO), 0)
    mine = lax.rem(lax.broadcasted_iota(jnp.int32, (CO, CO * CO), 1), CO) == n
    expanded = [jnp.where(mine, wide[i : i + 1], 0.0).astype(jnp.bfloat16) for i in range(8)]
    mixing = dot(jnp.concatenate(expanded, axis=0), w_outer[...]).astype(jnp.bfloat16)
    for i in range(8):
        for k in range(4):
            base[CZ + CO * k : CZ + CO * k + CO, CZ * i : CZ * i + CZ] = mixing[CO * i : CO * i + CO]


def packed_rows(tokens):
    return 16 * -(-tokens // 64)


def pair_part(gathered, part, base, left, result):
    tokens = TOKENS[part]
    lane = lax.broadcasted_iota(jnp.int32, (16, CZ), 1)
    pieces = []
    for k in range(ROWS):
        packed = gathered[k, tokens:, :].astype(jnp.float32)
        outer = [
            jnp.where(lane // CO == m % 4, packed[16 * (m // 4) : 16 * (m // 4) + 16], 0.0)
            for m in range(tokens // 16)
        ]
        outer = jnp.concatenate(outer, axis=0).astype(jnp.bfloat16)
        pieces.append(jnp.concatenate([gathered[k, :tokens, :], outer], axis=1))
    rows = jnp.concatenate(pieces, axis=0)
    for i in range(0, 8, 2):
        grid = dot(rows, base[:, CZ * i : CZ * i + 2 * CZ])
        for j in range(2):
            total = (grid[:, CZ * j : CZ * j + CZ] + left[i + j : i + j + 1]).astype(jnp.bfloat16)
            for k in range(ROWS):
                for first, to, size in SPANS[part]:
                    to += TOK_DEV * k
                    first += tokens * k
                    result[i + j, to : to + size, :] = total[first : first + size]


def body(
    atoms, window_offsets, atom_token, w_query, w_key, w_value, w_out, w_token, gain_token, w_pair, w_outer
):
    hbm = pl.BlockSpec(memory_space=pltpu.HBM)
    dma = pltpu.SemaphoreType.DMA
    bf16 = jnp.bfloat16
    return pl.pallas_call(
        embed_kernel,
        out_shape=pltpu.VMEM((8, ROWS * TOK_DEV, CZ), bf16),
        in_specs=[hbm] * 11,
        out_specs=pl.BlockSpec(memory_space=pltpu.VMEM),
        scratch_shapes=[
            pltpu.SMEM((ATOMS_DEV // QB,), jnp.int32),
            pltpu.VMEM((ATOMS_DEV,), jnp.int32),
            pltpu.VMEM((AW, AW), bf16),
            pltpu.VMEM((AW, AW), bf16),
            pltpu.VMEM((AW, AW), bf16),
            pltpu.VMEM((AW, AW), bf16),
            pltpu.VMEM((AW, TW), bf16),
            pltpu.VMEM((TW,), bf16),
            pltpu.VMEM((2 * CZ + 2 * CO, TW), bf16),
            pltpu.VMEM((CO * CO, CZ), bf16),
            *[pltpu.VMEM((ROWS, tokens + packed_rows(tokens), CZ), bf16) for tokens in TOKENS],
            pltpu.VMEM((2 * CZ, 8 * CZ), bf16),
            pltpu.VMEM((EXT, AW), bf16),
            pltpu.VMEM((EXT, AW), bf16),
            pltpu.VMEM((AW, WIDTH), bf16),
            pltpu.VMEM((2, AW + 16, WIDTH + GROUP), bf16),
            pltpu.VMEM((AW, WIDTH), bf16),
            pltpu.VMEM((WIDE, WIDTH), bf16),
            pltpu.VMEM((AW, WIDTH), bf16),
            pltpu.VMEM((AW, AW), bf16),
            pltpu.VMEM((TW, AW), bf16),
            pltpu.VMEM((2 * CZ, TW), bf16),
            pltpu.VMEM((16, NEXT), bf16),
            pltpu.VMEM((16, NEXT), bf16),
            *[pltpu.VMEM((tokens + packed_rows(tokens), CZ), bf16) for tokens in TOKENS],
            pltpu.VMEM((ROWS, 16, CZ), bf16),
            pltpu.VMEM((16, CZ), bf16),
            dma, dma((10,)), dma((3,)), dma((3,)),
            dma((PARTS,)), dma((PARTS,)), dma((PARTS,)), dma((PARTS, ROWS)), dma((PARTS, ROWS)), dma((COLS,)), dma,
            pltpu.SemaphoreType.REGULAR, pltpu.SemaphoreType.REGULAR,
        ],
        compiler_params=pltpu.CompilerParams(
            collective_id=0, has_side_effects=True, vmem_limit_bytes=60 * 1024 * 1024
        ),
        name="embed",
    )(
        atoms, window_offsets, atom_token, w_query, w_key, w_value, w_out, w_token, gain_token, w_pair.T,
        w_outer,
    )


def solution(mesh):
    split = P(("row", "col"))
    placed = (P(("row", "col"), None), split, split) + (P(),) * 8
    return jax.shard_map(
        body, mesh=mesh, in_specs=placed, out_specs=P("row", "col", None), check_vma=False
    )
```

```python
import jax
import jax.numpy as jnp
from jax import lax
from jax.experimental import pallas as pl
from jax.experimental.pallas import tpu as pltpu
from jax.sharding import PartitionSpec as P

AW = 128
HEADS = 4
TW = 384
CZ = 128
CO = 32
QB = 32
RIM = 64
ROWS = 8
COLS = 32
DEVICES = ROWS * COLS
ATOMS_DEV = 1536
TOK_DEV = 128
NEXT = 128
NEXT_USED = 96
EXT = RIM + ATOMS_DEV + NEXT
WIDTH = ATOMS_DEV + NEXT
GROUP = 128
GROUPS = ATOMS_DEV // GROUP
UNITS = 2 * GROUPS
AHEAD = 3
BEHIND = 2
HALF = 64
EDGE = 16
INNER = ((UNITS - 2, 128, 1408, 16, 96, 128, 1408),)
TOKENS = tuple(piece[4] for piece in INNER) + (32,)
PARTS = len(TOKENS)
SPANS = tuple(((0, piece[3], piece[4]),) for piece in INNER) + (((0, 0, 16), (16, 112, 16)),)
WIDE = TW + 128
EXP_SCALE = float(32 ** -0.5 * 1.4426950408889634)
MESH = pl.DeviceIdType.MESH
NT = (((1,), (1,)), ((), ()))


def dot(a, b):
    return jnp.dot(a, b, preferred_element_type=jnp.float32)


def place(device):
    return (lax.div(device, COLS), lax.rem(device, COLS))


def dot_nt(a, b):
    return lax.dot_general(a, b, NT, preferred_element_type=jnp.float32)


def turned(w):
    return w[...].astype(jnp.float32).T.astype(jnp.bfloat16)


def unit_scores(unit, keys, queries):
    g, j = unit // 2, unit % 2
    q = queries[:, GROUP * g : GROUP * g + GROUP]
    side = (lax.broadcasted_iota(jnp.int32, (HALF, GROUP), 0) // 32 == j) == (
        lax.broadcasted_iota(jnp.int32, (HALF, GROUP), 1) < HALF
    )
    none = jnp.zeros((HALF, GROUP), jnp.bfloat16)
    heads = [jnp.where(side, q[HALF * t : HALF * t + HALF], none) for t in range(2)]
    operand = jnp.concatenate(
        [jnp.concatenate([heads[0], none], axis=1), jnp.concatenate([none, heads[1]], axis=1)], axis=0
    )
    return dot(keys[HALF * unit : HALF * unit + 192, :], operand)


def unit_softmax(unit, scores, me, off, off_next):
    lane = lax.broadcasted_iota(jnp.int32, (1, GROUP), 1)
    second = lax.rem(lane // QB, 2) == 1
    if unit == UNITS:
        start = off_next[8:9, :].astype(jnp.int32) + RIM
    else:
        start = jnp.where(second, off[2 * unit + 1] + RIM + QB, off[2 * unit] + RIM)
    low, high = start, start + 128
    if unit == 0:
        low = jnp.maximum(low, jnp.where(me == 0, RIM, 0))
    if unit == UNITS - 1:
        high = jnp.minimum(high, jnp.where(me == DEVICES - 1, 128, 192))
    row = lax.broadcasted_iota(jnp.int32, (HALF, GROUP), 0)
    enters, stays = row >= low, row + 128 < high
    parts = []
    for t in range(2):
        tile = scores[:, GROUP * t : GROUP * t + GROUP]
        tile = jnp.concatenate(
            [jnp.where(enters, tile[:64], -1e30), tile[64:128], jnp.where(stays, tile[128:], -1e30)], axis=0
        )
        top = jnp.max(tile, axis=0, keepdims=True)
        parts.append(jnp.exp2((tile - top) * EXP_SCALE).astype(jnp.bfloat16))
    return jnp.concatenate(
        [jnp.concatenate(parts, axis=1), jnp.zeros((HALF, 2 * GROUP), jnp.bfloat16)], axis=0
    )


def group_store(g, mixed, att):
    left = lax.broadcasted_iota(jnp.int32, (1, GROUP), 1) < HALF
    for h in range(HEADS):
        lanes = slice(GROUP * (h // 2), GROUP * (h // 2) + GROUP)
        a, b = mixed if h % 2 == 0 else mixed[::-1]
        total = jnp.where(left, a[AW : AW + 1, lanes], b[AW : AW + 1, lanes])
        value = jnp.where(left, a[32 * h : 32 * h + 32, lanes], b[32 * h : 32 * h + 32, lanes]) * (1.0 / total)
        if h % 2 == 1:
            value = pltpu.roll(value, HALF, 1)
        att[32 * h : 32 * h + 32, GROUP * g : GROUP * g + GROUP] = value.astype(jnp.bfloat16)


def attend(units, me, off, off_next, keys, queries, values, att, mixed):
    scores, lifted = {}, {}
    for i in range(len(units) + AHEAD + BEHIND):
        if i < len(units):
            scores[i] = unit_scores(units[i], keys, queries)
        k = i - AHEAD
        if 0 <= k < len(units):
            lifted[k] = unit_softmax(units[k], scores.pop(k), me, off, off_next)
        k = i - AHEAD - BEHIND
        if 0 <= k < len(units):
            g, j = units[k] // 2, units[k] % 2
            mixed[units[k]] = dot(values[j, :, GROUP * g : GROUP * g + 2 * GROUP], lifted.pop(k))
            if units[k] == UNITS:
                mixed[UNITS + 1] = mixed[UNITS]
            if 2 * g in mixed and 2 * g + 1 in mixed:
                group_store(g, [mixed.pop(2 * g), mixed.pop(2 * g + 1)], att)
            yield units[k]


def hidden_rows(lo, hi, turned_atoms, att, w_out_t, w_token_t, hid):
    mixed = dot(w_out_t[...], att[:, lo:hi])
    update = (turned_atoms[:, lo:hi].astype(jnp.float32) + mixed).astype(jnp.bfloat16)
    hid[:TW, lo:hi] = jnp.maximum(dot(w_token_t[...], update), 0.0).astype(jnp.bfloat16)


def pooled_rows(first, count, lo, hi, device, token, hid, flags=None):
    slot = token[...].reshape(1, ATOMS_DEV)[:, lo:hi] - device * TOK_DEV
    rows = lax.broadcasted_iota(jnp.int32, (count, hi - lo), 0) + first
    one_hot = jnp.where(rows == slot, 1.0, 0.0).astype(jnp.bfloat16)
    if flags is not None:
        last = lax.broadcasted_iota(jnp.int32, (count, NEXT), 0) == count - 1
        one_hot = jnp.concatenate([one_hot, jnp.where(last, flags, 0.0).astype(jnp.bfloat16)], axis=1)
        hi += NEXT
    return dot_nt(one_hot, hid[:, lo:hi])


def token_normed(pooled, gain):
    count = pooled[:, TW:]
    single = pooled[:, :TW] / jnp.concatenate([count] * 3, axis=1)
    centre = single - jnp.mean(single, axis=1, keepdims=True)
    variance = jnp.mean(centre * centre, axis=1, keepdims=True)
    return (centre * lax.rsqrt(variance + 1e-05) * gain).astype(jnp.bfloat16)


def embed_kernel(
    atoms, off_hbm, token_hbm, wq_hbm, wk_hbm, wv_hbm, w_out_hbm, w_token_hbm, gain_hbm, w_pair_hbm, w_outer_hbm,
    result,
    off, token, wq, wk, wv, w_out, w_token, gain, w_pair, w_outer,
    gathered0, gathered1, base,
    ext, keys, queries, values, att, hid, turned_atoms, w_out_t, w_token_t, w_right,
    note_out, note_in, block0, block1, left_all, left_in,
    own_sem, load_sem, halo_send, halo_recv,
    first_send, first_recv, local_sem, pass_send, pass_recv, left_send, left_recv, far_ready, left_ready, pass_ready,
):
    gathered, block = (gathered0, gathered1), (block0, block1)
    row = lax.axis_index("row")
    col = lax.axis_index("col")
    me = row * COLS + col
    before = lax.rem(me + DEVICES - 1, DEVICES)
    after = lax.rem(me + 1, DEVICES)
    slot = lax.rem(me, ROWS)
    my_y, my_z = lax.div(row, 2), lax.rem(row, 2)
    my_x, my_zh = lax.div(col, 8), lax.rem(lax.div(col, 2), 4)
    depth = 2 * my_zh + my_z
    group_col = lax.div(me, ROWS)
    relay_y = lax.rem(my_y + 6 + my_zh - 2 * my_z - lax.div(my_x, 2) + 2 * lax.rem(my_x, 2), 4)
    my_core = lax.rem(col, 2)
    target = (2 * relay_y + my_core) * COLS + group_col
    target_depth = 4 * my_z + 2 * lax.div(my_x, 2) + my_core

    def held_by(y, z):
        return 2 * lax.rem(y + 6 + my_zh - my_x + 2 * my_core, 4) + z

    held = held_by(my_y, my_z)
    source = ROWS * col + held
    source_depth = 2 * lax.div(held, 2) + lax.div(my_zh, 2)
    keeps = target == me
    peers = [(2, 1), (2, 0), (1, 1), (3, 1), (1, 0), (3, 0), (0, 1)]
    col_in = lax.rem(col, 8)
    is_head, is_leader, is_first, is_last = col_in == 1, col == 1, me == 0, me == DEVICES - 1
    parent = jnp.where(is_leader, 0, jnp.where(is_head, row * COLS + 1, me - col_in + 1))

    def count(condition):
        return jnp.where(condition, 1, 0)

    def signal(device, semaphore=None):
        pl.semaphore_signal(
            barrier if semaphore is None else semaphore, inc=1, device_id=place(device), device_id_type=MESH
        )

    own = [
        pltpu.make_async_copy(atoms.at[pl.ds(lo, 512)], ext.at[pl.ds(RIM + lo, 512)], own_sem.at[lo // 512])
        for lo in range(0, ATOMS_DEV, 512)
    ]
    for copy in own:
        copy.start()
    pieces = [
        (wq_hbm, wq), (wk_hbm, wk), (wv_hbm, wv), (off_hbm, off), (w_out_hbm, w_out),
        (token_hbm, token), (w_token_hbm, w_token), (gain_hbm, gain), (w_pair_hbm, w_pair),
        (w_outer_hbm, w_outer),
    ]
    loads = [pltpu.make_async_copy(a, b, load_sem.at[i]) for i, (a, b) in enumerate(pieces)]
    for load in loads:
        load.start()

    barrier = pltpu.get_barrier_semaphore()

    @pl.when(jnp.logical_not(is_first))
    def _():
        signal(before)

    @pl.when(jnp.logical_not(is_last))
    def _():
        signal(after)

    @pl.when(is_head)
    def _():
        signal(parent)

    arrivals = 2 - count(is_first) - count(is_last) + 8 * count(is_first) + 3 * count(is_leader)

    @pl.when((source != me) & (source_depth >= depth))
    def _():
        signal(source)

    @pl.when(jnp.logical_not(keeps) & (target_depth > depth))
    def _():
        signal(target)

    arrivals += count((source != me) & (source_depth < depth))
    arrivals += count(jnp.logical_not(keeps) & (target_depth <= depth))
    late_target = jnp.logical_not(keeps) & (target_depth > depth)

    def peer(i, j):
        return (2 * lax.rem(my_y + i, 4) + lax.rem(my_z + j, 2)) * COLS + col

    for i, j in peers:
        @pl.when(peer(i, j) > me)
        def _():
            signal(peer(i, j))
    arrivals += row
    child = jnp.logical_not(is_head | is_first)
    arrivals += count(child)
    children = 7 - count((row == 0) & is_leader)

    def each_child(act):
        for c in range(8):
            if c != 1:
                @pl.when(is_head & (me + c != 1))
                def _():
                    act(me + c - 1, 16 + c)

    def each_leader(act):
        @pl.when(is_first)
        def _():
            for r in range(ROWS):
                act(r * COLS + 1, r)

    def each_head(act):
        @pl.when(is_leader)
        def _():
            for x in range(1, 4):
                act(me + 8 * x, 8 + x)

    each_child(lambda to, _: signal(to))

    for load in loads[:3]:
        load.wait()

    one = lax.broadcasted_iota(jnp.int32, (CZ, CZ), 0) == lax.broadcasted_iota(jnp.int32, (CZ, CZ), 1)
    eye = jnp.where(one, 1.0, 0.0).astype(jnp.bfloat16)
    value_t = turned(wv)
    left_side = jnp.concatenate([turned(wq), value_t, eye], axis=0)
    hid[TW:, :] = jnp.ones((WIDE - TW, WIDTH), jnp.bfloat16)
    for j in range(2):
        values[j, AW:, :] = jnp.ones((16, WIDTH + GROUP), jnp.bfloat16)
    def keep_product(lo, size, product):
        for h in range(HEADS):
            rows = slice(32 * h, 32 * h + 32)
            for part in range(0, size, GROUP):
                q = product[rows, part : part + GROUP]
                if h % 2 == 1:
                    q = pltpu.roll(q, HALF, 1)
                queries[rows, lo + part : lo + part + GROUP] = q.astype(jnp.bfloat16)
        values[1, :AW, lo : lo + size] = product[AW : 2 * AW].astype(jnp.bfloat16)
        turned_atoms[:, lo : lo + size] = product[2 * AW :].astype(jnp.bfloat16)

    for lo in range(0, ATOMS_DEV, 512):
        own[lo // 512].wait()
        x = ext[RIM + lo : RIM + lo + 512, :]
        keys[RIM + lo : RIM + lo + 512, :] = dot(x, wk[...]).astype(jnp.bfloat16)
        for part in range(0, 512, 256):
            keep_product(lo + part, 256, dot_nt(left_side, x[part : part + 256]))
    for load in loads[3:]:
        load.wait()
    flags = token[...].reshape(1, ATOMS_DEV)[:, :NEXT] == me * TOK_DEV - 1
    upper = lax.broadcasted_iota(jnp.int32, (16, NEXT), 0) < 8
    note = jnp.where(upper, jnp.where(flags, 1.0, 0.0), off[0].astype(jnp.float32))
    note_out[...] = note.astype(jnp.bfloat16)
    ext[RIM + ATOMS_DEV + NEXT_USED :, :] = jnp.zeros((NEXT - NEXT_USED, AW), jnp.bfloat16)

    @pl.when(is_first)
    def _():
        ext[:RIM, :] = jnp.zeros((RIM, AW), jnp.bfloat16)

    @pl.when(is_last)
    def _():
        ext[RIM + ATOMS_DEV :, :] = jnp.zeros((NEXT, AW), jnp.bfloat16)
        note_in[...] = jnp.zeros((16, NEXT), jnp.bfloat16)

    pl.semaphore_wait(barrier, arrivals)

    to_after = pltpu.make_async_remote_copy(
        src_ref=atoms.at[pl.ds(ATOMS_DEV - RIM, RIM)], dst_ref=ext.at[pl.ds(0, RIM)],
        send_sem=halo_send.at[0], recv_sem=halo_recv.at[0],
        device_id=place(after), device_id_type=MESH,
    )
    to_before = [
        pltpu.make_async_remote_copy(
            src_ref=atoms.at[pl.ds(0, NEXT_USED)], dst_ref=ext.at[pl.ds(RIM + ATOMS_DEV, NEXT_USED)],
            send_sem=halo_send.at[1], recv_sem=halo_recv.at[1],
            device_id=place(before), device_id_type=MESH,
        ),
        pltpu.make_async_remote_copy(
            src_ref=note_out, dst_ref=note_in, send_sem=halo_send.at[2], recv_sem=halo_recv.at[2],
            device_id=place(before), device_id_type=MESH,
        ),
    ]

    @pl.when(jnp.logical_not(is_last))
    def _():
        to_after.start()

    @pl.when(jnp.logical_not(is_first))
    def _():
        for copy in to_before:
            copy.start()

    @pl.when((source != me) & (source_depth < depth))
    def _():
        signal(source, far_ready)

    @pl.when(child)
    def _():
        signal(parent, left_ready)

    for i, j in peers:
        @pl.when(peer(i, j) < me)
        def _():
            signal(peer(i, j), pass_ready)

    for lo in range(128, ATOMS_DEV, 256):
        hi = min(lo + 256, ATOMS_DEV)
        values[0, :AW, lo:hi] = dot_nt(value_t, ext[lo:hi, :]).astype(jnp.bfloat16)
    pad = jnp.zeros((RIM, AW), jnp.bfloat16)
    rest = jnp.concatenate([ext[ATOMS_DEV : ATOMS_DEV + RIM, :], pad], axis=0)
    values[0, :AW, ATOMS_DEV : ATOMS_DEV + GROUP] = dot_nt(value_t, rest).astype(jnp.bfloat16)

    for i in range(8):
        base[:CZ, CZ * i : CZ * i + CZ] = eye
    w_out_t[...] = turned(w_out)
    w_token_t[...] = turned(w_token)
    w_right[:CZ, :] = w_pair[CZ + CO : 2 * CZ + CO, :]
    for m in range(4):
        w_right[CZ + CO * m : CZ + CO * m + CO, :] = w_pair[2 * CZ + CO :, :]

    mixed = {}
    inner_units = attend(list(range(1, UNITS - 1)), me, off, note_in, keys, queries, values, att, mixed)

    def first_copy(part):
        return pltpu.make_async_remote_copy(
            src_ref=block[part], dst_ref=gathered[part].at[slot],
            send_sem=first_send.at[part], recv_sem=first_recv.at[part],
            device_id=place(target), device_id_type=MESH,
        )

    def local_copy(part):
        return pltpu.make_async_copy(block[part], gathered[part].at[slot], local_sem.at[part])

    def first_sends(part):
        @pl.when(jnp.logical_not(keeps))
        def _():
            first_copy(part).start()

        @pl.when(keeps)
        def _():
            local_copy(part).start()

    def pass_copy(part, i, j, holder):
        return pltpu.make_async_remote_copy(
            src_ref=gathered[part].at[holder], dst_ref=gathered[part].at[holder],
            send_sem=pass_send.at[part, 2 * i + j], recv_sem=pass_recv.at[part, 2 * i + j],
            device_id=place(peer(i, j)), device_id_type=MESH,
        )

    def pass_on(part):
        @pl.when(source != me)
        def _():
            pltpu.make_async_remote_copy(
                src_ref=block[part], dst_ref=gathered[part].at[held],
                send_sem=first_send.at[part], recv_sem=first_recv.at[part],
                device_id=place(source), device_id_type=MESH,
            ).wait_recv()

        @pl.when(source == me)
        def _():
            local_copy(part).wait()

        for i, j in peers:
            pass_copy(part, i, j, held).start()

    def finish(part, pooled):
        tokens = TOKENS[part]
        normed = token_normed(pooled, gain[...].reshape(1, TW).astype(jnp.float32))
        right = dot_nt(normed, w_right[...])
        lane = lax.broadcasted_iota(jnp.int32, (16, CZ), 1)
        packed = []
        for m in range(tokens // 16):
            rows = right[16 * m : 16 * m + 16, CZ:]
            if m % 4 == 0:
                packed.append(rows)
            else:
                packed[-1] = jnp.where(lane // CO == m % 4, rows, packed[-1])
        packed = jnp.concatenate(packed, axis=0)
        block[part][:tokens, :] = right[:, :CZ].astype(jnp.bfloat16)
        block[part][tokens:, :] = packed.astype(jnp.bfloat16)
        return normed

    def early_sends(part):
        @pl.when(jnp.logical_not(late_target))
        def _():
            first_sends(part)

    normed = []
    for part, (last, lo, hi, first, number, start, stop) in enumerate(INNER):
        for unit in inner_units:
            if unit == last:
                break
        hidden_rows(lo, hi, turned_atoms, att, w_out_t, w_token_t, hid)
        normed.append(finish(part, pooled_rows(first, number, start, stop, me, token, hid)))
        early_sends(part)

    @pl.when(jnp.logical_not(is_last))
    def _():
        for copy in to_before:
            copy.wait_recv()

    @pl.when(jnp.logical_not(is_first))
    def _():
        to_after.wait_recv()

    keys[:RIM, :] = dot(ext[:RIM, :], wk[...]).astype(jnp.bfloat16)
    values[0, :AW, :GROUP] = dot_nt(value_t, ext[:GROUP, :]).astype(jnp.bfloat16)
    x = ext[RIM + ATOMS_DEV :, :]
    keys[RIM + ATOMS_DEV :, :] = dot(x, wk[...]).astype(jnp.bfloat16)
    keep_product(ATOMS_DEV, NEXT, dot_nt(left_side, x))
    rest = jnp.concatenate([ext[ATOMS_DEV:, :], pad], axis=0)
    values[0, :AW, ATOMS_DEV:] = dot_nt(value_t, rest).astype(jnp.bfloat16)
    for _ in attend([0, UNITS, UNITS - 1], me, off, note_in, keys, queries, values, att, mixed):
        pass

    hidden_rows(0, GROUP, turned_atoms, att, w_out_t, w_token_t, hid)
    hidden_rows(ATOMS_DEV - GROUP, WIDTH, turned_atoms, att, w_out_t, w_token_t, hid)
    low = pooled_rows(0, EDGE, 0, 256, me, token, hid)
    flags = note_in[:1, :].astype(jnp.float32)
    high = pooled_rows(TOK_DEV - EDGE, EDGE, ATOMS_DEV - 256, ATOMS_DEV, me, token, hid, flags)
    outer = finish(PARTS - 1, jnp.concatenate([low, high], axis=0))

    early_sends(PARTS - 1)

    def left_copy(source, to, index):
        return pltpu.make_async_remote_copy(
            src_ref=source, dst_ref=left_in, send_sem=left_send.at[index], recv_sem=left_recv,
            device_id=place(to), device_id_type=MESH,
        )

    def left_to(child, index):
        return left_copy(left_all.at[index] if index < ROWS else left_in, child, index)

    @pl.when(is_first)
    def _():
        first_rows = jnp.concatenate([outer[:EDGE], normed[0][: HALF - EDGE]], axis=0)
        left = dot_nt(first_rows, w_pair[: 2 * CZ, :])
        for r in range(ROWS):
            rows = left[8 * r : 8 * r + 8]
            left_all[r] = jnp.concatenate([rows[:, :CZ], rows[:, CZ:]], axis=0).astype(jnp.bfloat16)
        left_in[...] = left_all[0]

    each_leader(lambda to, index: left_to(to, index).start())

    @pl.when(is_leader)
    def _():
        left_copy(left_in, parent, 0).wait_recv()

    each_head(lambda to, index: left_to(to, index).start())

    @pl.when(late_target)
    def _():
        pl.semaphore_wait(far_ready, 1)
        for part in range(PARTS):
            first_sends(part)

    @pl.when(is_head & jnp.logical_not(is_leader))
    def _():
        left_copy(left_in, parent, 0).wait_recv()

    @pl.when(is_head)
    def _():
        pl.semaphore_wait(left_ready, children)

    each_child(lambda to, index: left_to(to, index).start())
    @pl.when(row < ROWS - 1)
    def _():
        pl.semaphore_wait(pass_ready, ROWS - 1 - row)

    for part in range(PARTS):
        pass_on(part)

    @pl.when(child)
    def _():
        left_copy(left_in, parent, 0).wait_recv()

    mix_left(left_in, w_outer, base)
    left = left_in[:8, :].astype(jnp.float32)

    for part in range(PARTS):
        for i, j in peers:
            pass_copy(part, i, j, held_by(my_y + 4 - i, lax.rem(my_z + j, 2))).wait_recv()
        pair_part(gathered[part], part, base, left, result)

    for each in (each_leader, each_head, each_child):
        each(lambda to, index: left_to(to, index).wait_send())

    @pl.when(jnp.logical_not(is_last))
    def _():
        to_after.wait_send()

    @pl.when(jnp.logical_not(is_first))
    def _():
        for copy in to_before:
            copy.wait_send()

    for part in range(PARTS):
        for i, j in peers:
            pass_copy(part, i, j, held).wait_send()

        @pl.when(jnp.logical_not(keeps))
        def _():
            first_copy(part).wait_send()


def mix_left(left_in, w_outer, base):
    outer = left_in[8:, :CO]
    spread = lax.broadcasted_iota(jnp.int32, (CO, CO * CO), 1) // CO
    spread = jnp.where(spread == lax.broadcasted_iota(jnp.int32, (CO, CO * CO), 0), 1.0, 0.0)
    wide = dot(outer, spread.astype(jnp.bfloat16))
    n = lax.broadcasted_iota(jnp.int32, (CO, CO * CO), 0)
    mine = lax.rem(lax.broadcasted_iota(jnp.int32, (CO, CO * CO), 1), CO) == n
    expanded = [jnp.where(mine, wide[i : i + 1], 0.0).astype(jnp.bfloat16) for i in range(8)]
    mixing = dot(jnp.concatenate(expanded, axis=0), w_outer[...]).astype(jnp.bfloat16)
    for i in range(8):
        for k in range(4):
            base[CZ + CO * k : CZ + CO * k + CO, CZ * i : CZ * i + CZ] = mixing[CO * i : CO * i + CO]


def packed_rows(tokens):
    return 16 * -(-tokens // 64)


def pair_part(gathered, part, base, left, result):
    tokens = TOKENS[part]
    lane = lax.broadcasted_iota(jnp.int32, (16, CZ), 1)
    pieces = []
    for k in range(ROWS):
        packed = gathered[k, tokens:, :].astype(jnp.float32)
        outer = [
            jnp.where(lane // CO == m % 4, packed[16 * (m // 4) : 16 * (m // 4) + 16], 0.0)
            for m in range(tokens // 16)
        ]
        outer = jnp.concatenate(outer, axis=0).astype(jnp.bfloat16)
        pieces.append(jnp.concatenate([gathered[k, :tokens, :], outer], axis=1))
    rows = jnp.concatenate(pieces, axis=0)
    for i in range(0, 8, 2):
        grid = dot(rows, base[:, CZ * i : CZ * i + 2 * CZ])
        for j in range(2):
            total = (grid[:, CZ * j : CZ * j + CZ] + left[i + j : i + j + 1]).astype(jnp.bfloat16)
            for k in range(ROWS):
                for first, to, size in SPANS[part]:
                    to += TOK_DEV * k
                    first += tokens * k
                    result[i + j, to : to + size, :] = total[first : first + size]


def body(
    atoms, window_offsets, atom_token, w_query, w_key, w_value, w_out, w_token, gain_token, w_pair, w_outer
):
    hbm = pl.BlockSpec(memory_space=pltpu.HBM)
    dma = pltpu.SemaphoreType.DMA
    bf16 = jnp.bfloat16
    return pl.pallas_call(
        embed_kernel,
        out_shape=pltpu.VMEM((8, ROWS * TOK_DEV, CZ), bf16),
        in_specs=[hbm] * 11,
        out_specs=pl.BlockSpec(memory_space=pltpu.VMEM),
        scratch_shapes=[
            pltpu.SMEM((ATOMS_DEV // QB,), jnp.int32),
            pltpu.VMEM((ATOMS_DEV,), jnp.int32),
            pltpu.VMEM((AW, AW), bf16),
            pltpu.VMEM((AW, AW), bf16),
            pltpu.VMEM((AW, AW), bf16),
            pltpu.VMEM((AW, AW), bf16),
            pltpu.VMEM((AW, TW), bf16),
            pltpu.VMEM((TW,), bf16),
            pltpu.VMEM((2 * CZ + 2 * CO, TW), bf16),
            pltpu.VMEM((CO * CO, CZ), bf16),
            *[pltpu.VMEM((ROWS, tokens + packed_rows(tokens), CZ), bf16) for tokens in TOKENS],
            pltpu.VMEM((2 * CZ, 8 * CZ), bf16),
            pltpu.VMEM((EXT, AW), bf16),
            pltpu.VMEM((EXT, AW), bf16),
            pltpu.VMEM((AW, WIDTH), bf16),
            pltpu.VMEM((2, AW + 16, WIDTH + GROUP), bf16),
            pltpu.VMEM((AW, WIDTH), bf16),
            pltpu.VMEM((WIDE, WIDTH), bf16),
            pltpu.VMEM((AW, WIDTH), bf16),
            pltpu.VMEM((AW, AW), bf16),
            pltpu.VMEM((TW, AW), bf16),
            pltpu.VMEM((2 * CZ, TW), bf16),
            pltpu.VMEM((16, NEXT), bf16),
            pltpu.VMEM((16, NEXT), bf16),
            *[pltpu.VMEM((tokens + packed_rows(tokens), CZ), bf16) for tokens in TOKENS],
            pltpu.VMEM((ROWS, 16, CZ), bf16),
            pltpu.VMEM((16, CZ), bf16),
            dma((3,)), dma((10,)), dma((3,)), dma((3,)),
            dma((PARTS,)), dma((PARTS,)), dma((PARTS,)), dma((PARTS, ROWS)), dma((PARTS, ROWS)), dma((COLS,)), dma,
            *[pltpu.SemaphoreType.REGULAR] * 3,
        ],
        compiler_params=pltpu.CompilerParams(
            collective_id=0, has_side_effects=True, vmem_limit_bytes=60 * 1024 * 1024
        ),
        name="embed",
    )(
        atoms, window_offsets, atom_token, w_query, w_key, w_value, w_out, w_token, gain_token, w_pair.T,
        w_outer,
    )


def solution(mesh):
    split = P(("row", "col"))
    placed = (P(("row", "col"), None), split, split) + (P(),) * 8
    return jax.shard_map(
        body, mesh=mesh, in_specs=placed, out_specs=P("row", "col", None), check_vma=False
    )
```

```python
import jax
import jax.numpy as jnp
from jax import lax
from jax.experimental import pallas as pl
from jax.experimental.pallas import tpu as pltpu
from jax.sharding import PartitionSpec as P

AW = 128
HEADS = 4
TW = 384
CZ = 128
CO = 32
QB = 32
RIM = 64
ROWS = 8
COLS = 32
DEVICES = ROWS * COLS
ATOMS_DEV = 1536
TOK_DEV = 128
NEXT = 128
NEXT_USED = 96
EXT = RIM + ATOMS_DEV + NEXT
WIDTH = ATOMS_DEV + NEXT
GROUP = 128
GROUPS = ATOMS_DEV // GROUP
UNITS = 2 * GROUPS
AHEAD = 3
BEHIND = 2
HALF = 64
EDGE = 16
INNER = ((UNITS - 2, 128, 1408, 16, 96, 128, 1408),)
TOKENS = tuple(piece[4] for piece in INNER) + (32,)
PARTS = len(TOKENS)
SPANS = tuple(((0, piece[3], piece[4]),) for piece in INNER) + (((0, 0, 16), (16, 112, 16)),)
WIDE = TW + 128
EXP_SCALE = float(32 ** -0.5 * 1.4426950408889634)
MESH = pl.DeviceIdType.MESH
NT = (((1,), (1,)), ((), ()))


def dot(a, b):
    return jnp.dot(a, b, preferred_element_type=jnp.float32)


def place(device):
    return (lax.div(device, COLS), lax.rem(device, COLS))


def dot_nt(a, b):
    return lax.dot_general(a, b, NT, preferred_element_type=jnp.float32)


def turned(w):
    return w[...].astype(jnp.float32).T.astype(jnp.bfloat16)


def unit_scores(unit, keys, queries):
    g, j = unit // 2, unit % 2
    q = queries[:, GROUP * g : GROUP * g + GROUP]
    side = (lax.broadcasted_iota(jnp.int32, (HALF, GROUP), 0) // 32 == j) == (
        lax.broadcasted_iota(jnp.int32, (HALF, GROUP), 1) < HALF
    )
    none = jnp.zeros((HALF, GROUP), jnp.bfloat16)
    heads = [jnp.where(side, q[HALF * t : HALF * t + HALF], none) for t in range(2)]
    operand = jnp.concatenate(
        [jnp.concatenate([heads[0], none], axis=1), jnp.concatenate([none, heads[1]], axis=1)], axis=0
    )
    return dot(keys[HALF * unit : HALF * unit + 192, :], operand)


def unit_softmax(unit, scores, me, off, off_next):
    lane = lax.broadcasted_iota(jnp.int32, (1, GROUP), 1)
    second = lax.rem(lane // QB, 2) == 1
    if unit == UNITS:
        start = off_next[8:9, :].astype(jnp.int32) + RIM
    else:
        start = jnp.where(second, off[2 * unit + 1] + RIM + QB, off[2 * unit] + RIM)
    low, high = start, start + 128
    if unit == 0:
        low = jnp.maximum(low, jnp.where(me == 0, RIM, 0))
    if unit == UNITS - 1:
        high = jnp.minimum(high, jnp.where(me == DEVICES - 1, 128, 192))
    row = lax.broadcasted_iota(jnp.int32, (HALF, GROUP), 0)
    enters, stays = row >= low, row + 128 < high
    parts = []
    for t in range(2):
        tile = scores[:, GROUP * t : GROUP * t + GROUP]
        tile = jnp.concatenate(
            [jnp.where(enters, tile[:64], -1e30), tile[64:128], jnp.where(stays, tile[128:], -1e30)], axis=0
        )
        top = jnp.max(tile, axis=0, keepdims=True)
        parts.append(jnp.exp2((tile - top) * EXP_SCALE).astype(jnp.bfloat16))
    return jnp.concatenate(
        [jnp.concatenate(parts, axis=1), jnp.zeros((HALF, 2 * GROUP), jnp.bfloat16)], axis=0
    )


def group_store(g, mixed, att):
    left = lax.broadcasted_iota(jnp.int32, (1, GROUP), 1) < HALF
    for h in range(HEADS):
        lanes = slice(GROUP * (h // 2), GROUP * (h // 2) + GROUP)
        a, b = mixed if h % 2 == 0 else mixed[::-1]
        total = jnp.where(left, a[AW : AW + 1, lanes], b[AW : AW + 1, lanes])
        value = jnp.where(left, a[32 * h : 32 * h + 32, lanes], b[32 * h : 32 * h + 32, lanes]) * (1.0 / total)
        if h % 2 == 1:
            value = pltpu.roll(value, HALF, 1)
        att[32 * h : 32 * h + 32, GROUP * g : GROUP * g + GROUP] = value.astype(jnp.bfloat16)


def attend(units, me, off, off_next, keys, queries, values, att, mixed):
    scores, lifted = {}, {}
    for i in range(len(units) + AHEAD + BEHIND):
        if i < len(units):
            scores[i] = unit_scores(units[i], keys, queries)
        k = i - AHEAD
        if 0 <= k < len(units):
            lifted[k] = unit_softmax(units[k], scores.pop(k), me, off, off_next)
        k = i - AHEAD - BEHIND
        if 0 <= k < len(units):
            g, j = units[k] // 2, units[k] % 2
            mixed[units[k]] = dot(values[j, :, GROUP * g : GROUP * g + 2 * GROUP], lifted.pop(k))
            if units[k] == UNITS:
                mixed[UNITS + 1] = mixed[UNITS]
            if 2 * g in mixed and 2 * g + 1 in mixed:
                group_store(g, [mixed.pop(2 * g), mixed.pop(2 * g + 1)], att)
            yield units[k]


def hidden_rows(lo, hi, turned_atoms, att, w_out_t, w_token_t, hid):
    mixed = dot(w_out_t[...], att[:, lo:hi])
    update = (turned_atoms[:, lo:hi].astype(jnp.float32) + mixed).astype(jnp.bfloat16)
    hid[:TW, lo:hi] = jnp.maximum(dot(w_token_t[...], update), 0.0).astype(jnp.bfloat16)


def pooled_rows(first, count, lo, hi, device, token, hid, flags=None):
    slot = token[...].reshape(1, ATOMS_DEV)[:, lo:hi] - device * TOK_DEV
    rows = lax.broadcasted_iota(jnp.int32, (count, hi - lo), 0) + first
    one_hot = jnp.where(rows == slot, 1.0, 0.0).astype(jnp.bfloat16)
    if flags is not None:
        last = lax.broadcasted_iota(jnp.int32, (count, NEXT), 0) == count - 1
        one_hot = jnp.concatenate([one_hot, jnp.where(last, flags, 0.0).astype(jnp.bfloat16)], axis=1)
        hi += NEXT
    return dot_nt(one_hot, hid[:, lo:hi])


def token_normed(pooled, gain):
    count = pooled[:, TW:]
    single = pooled[:, :TW] / jnp.concatenate([count] * 3, axis=1)
    centre = single - jnp.mean(single, axis=1, keepdims=True)
    variance = jnp.mean(centre * centre, axis=1, keepdims=True)
    return (centre * lax.rsqrt(variance + 1e-05) * gain).astype(jnp.bfloat16)


def embed_kernel(
    atoms, off_hbm, token_hbm, wq_hbm, wk_hbm, wv_hbm, w_out_hbm, w_token_hbm, gain_hbm, w_pair_hbm, w_outer_hbm,
    result,
    off, token, wq, wk, wv, w_out, w_token, gain, w_pair, w_outer,
    gathered0, gathered1, base,
    ext, keys, queries, values, att, hid, turned_atoms, w_out_t, w_token_t, w_right,
    note_out, note_in, block0, block1, left_all, left_in,
    own_sem, load_sem, halo_send, halo_recv,
    first_send, first_recv, local_sem, pass_send, pass_recv, left_send, left_recv, far_ready, left_ready, pass_ready,
):
    gathered, block = (gathered0, gathered1), (block0, block1)
    row = lax.axis_index("row")
    col = lax.axis_index("col")
    me = row * COLS + col
    before = lax.rem(me + DEVICES - 1, DEVICES)
    after = lax.rem(me + 1, DEVICES)
    slot = lax.rem(me, ROWS)
    my_y, my_z = lax.div(row, 2), lax.rem(row, 2)
    my_x, my_zh = lax.div(col, 8), lax.rem(lax.div(col, 2), 4)
    depth = 2 * my_zh + my_z
    group_col = lax.div(me, ROWS)
    relay_y = lax.rem(my_y + 6 + my_zh - 2 * my_z - lax.div(my_x, 2) + 2 * lax.rem(my_x, 2), 4)
    my_core = lax.rem(col, 2)
    target = (2 * relay_y + my_core) * COLS + group_col
    target_depth = 4 * my_z + 2 * lax.div(my_x, 2) + my_core

    def held_by(y, z):
        return 2 * lax.rem(y + 6 + my_zh - my_x + 2 * my_core, 4) + z

    held = held_by(my_y, my_z)
    source = ROWS * col + held
    source_depth = 2 * lax.div(held, 2) + lax.div(my_zh, 2)
    keeps = target == me
    peers = [(2, 1), (2, 0), (1, 1), (3, 1), (1, 0), (3, 0), (0, 1)]
    col_in = lax.rem(col, 8)
    is_head, is_leader, is_first, is_last = col_in == 1, col == 1, me == 0, me == DEVICES - 1
    parent = jnp.where(is_leader, 0, jnp.where(is_head, row * COLS + 1, me - col_in + 1))

    def count(condition):
        return jnp.where(condition, 1, 0)

    def signal(device, semaphore=None):
        pl.semaphore_signal(
            barrier if semaphore is None else semaphore, inc=1, device_id=place(device), device_id_type=MESH
        )

    own = [
        pltpu.make_async_copy(atoms.at[pl.ds(lo, 512)], ext.at[pl.ds(RIM + lo, 512)], own_sem.at[lo // 512])
        for lo in range(0, ATOMS_DEV, 512)
    ]
    for copy in own:
        copy.start()
    pieces = [
        (wq_hbm, wq), (wk_hbm, wk), (wv_hbm, wv), (off_hbm, off), (w_out_hbm, w_out),
        (token_hbm, token), (w_token_hbm, w_token), (gain_hbm, gain), (w_pair_hbm, w_pair),
        (w_outer_hbm, w_outer),
    ]
    loads = [pltpu.make_async_copy(a, b, load_sem.at[i]) for i, (a, b) in enumerate(pieces)]
    for load in loads:
        load.start()

    barrier = pltpu.get_barrier_semaphore()

    @pl.when(jnp.logical_not(is_first))
    def _():
        signal(before)

    @pl.when(jnp.logical_not(is_last))
    def _():
        signal(after)

    @pl.when(is_head)
    def _():
        signal(parent)

    arrivals = 2 - count(is_first) - count(is_last) + 8 * count(is_first) + 3 * count(is_leader)

    @pl.when((source != me) & (source_depth >= depth))
    def _():
        signal(source)

    @pl.when(jnp.logical_not(keeps) & (target_depth > depth))
    def _():
        signal(target)

    arrivals += count((source != me) & (source_depth < depth))
    arrivals += count(jnp.logical_not(keeps) & (target_depth <= depth))
    late_target = jnp.logical_not(keeps) & (target_depth > depth)

    def peer(i, j):
        return (2 * lax.rem(my_y + i, 4) + lax.rem(my_z + j, 2)) * COLS + col

    for i, j in peers:
        @pl.when(peer(i, j) > me)
        def _():
            signal(peer(i, j))
    arrivals += row
    child = jnp.logical_not(is_head | is_first)
    arrivals += count(child)
    children = 7 - count((row == 0) & is_leader)

    def each_child(act):
        for c in range(8):
            if c != 1:
                @pl.when(is_head & (me + c != 1))
                def _():
                    act(me + c - 1, 16 + c)

    def each_leader(act):
        @pl.when(is_first)
        def _():
            for r in range(ROWS):
                act(r * COLS + 1, r)

    def each_head(act):
        @pl.when(is_leader)
        def _():
            for x in range(1, 4):
                act(me + 8 * x, 8 + x)

    each_child(lambda to, _: signal(to))

    for load in loads[:3]:
        load.wait()

    one = lax.broadcasted_iota(jnp.int32, (CZ, CZ), 0) == lax.broadcasted_iota(jnp.int32, (CZ, CZ), 1)
    eye = jnp.where(one, 1.0, 0.0).astype(jnp.bfloat16)
    value_t = turned(wv)
    left_side = jnp.concatenate([turned(wq), value_t, eye], axis=0)
    hid[TW:, :] = jnp.ones((WIDE - TW, WIDTH), jnp.bfloat16)
    for j in range(2):
        values[j, AW:, :] = jnp.ones((16, WIDTH + GROUP), jnp.bfloat16)
    def keep_product(lo, size, product):
        for h in range(HEADS):
            rows = slice(32 * h, 32 * h + 32)
            for part in range(0, size, GROUP):
                q = product[rows, part : part + GROUP]
                if h % 2 == 1:
                    q = pltpu.roll(q, HALF, 1)
                queries[rows, lo + part : lo + part + GROUP] = q.astype(jnp.bfloat16)
        values[1, :AW, lo : lo + size] = product[AW : 2 * AW].astype(jnp.bfloat16)
        turned_atoms[:, lo : lo + size] = product[2 * AW :].astype(jnp.bfloat16)

    for lo in range(0, ATOMS_DEV, 512):
        own[lo // 512].wait()
        x = ext[RIM + lo : RIM + lo + 512, :]
        keys[RIM + lo : RIM + lo + 512, :] = dot(x, wk[...]).astype(jnp.bfloat16)
        for part in range(0, 512, 256):
            keep_product(lo + part, 256, dot_nt(left_side, x[part : part + 256]))
    for load in loads[3:]:
        load.wait()
    flags = token[...].reshape(1, ATOMS_DEV)[:, :NEXT] == me * TOK_DEV - 1
    upper = lax.broadcasted_iota(jnp.int32, (16, NEXT), 0) < 8
    note = jnp.where(upper, jnp.where(flags, 1.0, 0.0), off[0].astype(jnp.float32))
    note_out[...] = note.astype(jnp.bfloat16)
    ext[RIM + ATOMS_DEV + NEXT_USED :, :] = jnp.zeros((NEXT - NEXT_USED, AW), jnp.bfloat16)

    @pl.when(is_first)
    def _():
        ext[:RIM, :] = jnp.zeros((RIM, AW), jnp.bfloat16)

    @pl.when(is_last)
    def _():
        ext[RIM + ATOMS_DEV :, :] = jnp.zeros((NEXT, AW), jnp.bfloat16)
        note_in[...] = jnp.zeros((16, NEXT), jnp.bfloat16)

    pl.semaphore_wait(barrier, arrivals)

    to_after = pltpu.make_async_remote_copy(
        src_ref=atoms.at[pl.ds(ATOMS_DEV - RIM, RIM)], dst_ref=ext.at[pl.ds(0, RIM)],
        send_sem=halo_send.at[0], recv_sem=halo_recv.at[0],
        device_id=place(after), device_id_type=MESH,
    )
    to_before = [
        pltpu.make_async_remote_copy(
            src_ref=atoms.at[pl.ds(0, NEXT_USED)], dst_ref=ext.at[pl.ds(RIM + ATOMS_DEV, NEXT_USED)],
            send_sem=halo_send.at[1], recv_sem=halo_recv.at[1],
            device_id=place(before), device_id_type=MESH,
        ),
        pltpu.make_async_remote_copy(
            src_ref=note_out, dst_ref=note_in, send_sem=halo_send.at[2], recv_sem=halo_recv.at[2],
            device_id=place(before), device_id_type=MESH,
        ),
    ]

    @pl.when(jnp.logical_not(is_last))
    def _():
        to_after.start()

    @pl.when(jnp.logical_not(is_first))
    def _():
        for copy in to_before:
            copy.start()

    @pl.when((source != me) & (source_depth < depth))
    def _():
        signal(source, far_ready)

    @pl.when(child)
    def _():
        signal(parent, left_ready)

    for i, j in peers:
        @pl.when(peer(i, j) < me)
        def _():
            signal(peer(i, j), pass_ready)

    for lo in range(128, ATOMS_DEV, 256):
        hi = min(lo + 256, ATOMS_DEV)
        values[0, :AW, lo:hi] = dot_nt(value_t, ext[lo:hi, :]).astype(jnp.bfloat16)
    pad = jnp.zeros((RIM, AW), jnp.bfloat16)
    rest = jnp.concatenate([ext[ATOMS_DEV : ATOMS_DEV + RIM, :], pad], axis=0)
    values[0, :AW, ATOMS_DEV : ATOMS_DEV + GROUP] = dot_nt(value_t, rest).astype(jnp.bfloat16)

    for i in range(8):
        base[:CZ, CZ * i : CZ * i + CZ] = eye
    w_out_t[...] = turned(w_out)
    w_token_t[...] = turned(w_token)
    w_right[:CZ, :] = w_pair[CZ + CO : 2 * CZ + CO, :]
    for m in range(4):
        w_right[CZ + CO * m : CZ + CO * m + CO, :] = w_pair[2 * CZ + CO :, :]

    mixed = {}
    inner_units = attend(list(range(1, UNITS - 1)), me, off, note_in, keys, queries, values, att, mixed)

    def first_copy(part):
        return pltpu.make_async_remote_copy(
            src_ref=block[part], dst_ref=gathered[part].at[slot],
            send_sem=first_send.at[part], recv_sem=first_recv.at[part],
            device_id=place(target), device_id_type=MESH,
        )

    def local_copy(part):
        return pltpu.make_async_copy(block[part], gathered[part].at[slot], local_sem.at[part])

    def first_sends(part):
        @pl.when(jnp.logical_not(keeps))
        def _():
            first_copy(part).start()

        @pl.when(keeps)
        def _():
            local_copy(part).start()

    def pass_copy(part, i, j, holder):
        return pltpu.make_async_remote_copy(
            src_ref=gathered[part].at[holder], dst_ref=gathered[part].at[holder],
            send_sem=pass_send.at[part], recv_sem=pass_recv.at[part],
            device_id=place(peer(i, j)), device_id_type=MESH,
        )

    def pass_all(part):
        blocks = gathered[part].at[pl.ds(0, ROWS - 1)]
        return pltpu.make_async_remote_copy(
            src_ref=blocks, dst_ref=blocks, send_sem=pass_send.at[part], recv_sem=pass_recv.at[part],
            device_id=place(peer(0, 1)), device_id_type=MESH,
        )

    def pass_on(part):
        @pl.when(source != me)
        def _():
            pltpu.make_async_remote_copy(
                src_ref=block[part], dst_ref=gathered[part].at[held],
                send_sem=first_send.at[part], recv_sem=first_recv.at[part],
                device_id=place(source), device_id_type=MESH,
            ).wait_recv()

        @pl.when(source == me)
        def _():
            local_copy(part).wait()

        for i, j in peers:
            pass_copy(part, i, j, held).start()

    def finish(part, pooled):
        tokens = TOKENS[part]
        normed = token_normed(pooled, gain[...].reshape(1, TW).astype(jnp.float32))
        right = dot_nt(normed, w_right[...])
        lane = lax.broadcasted_iota(jnp.int32, (16, CZ), 1)
        packed = []
        for m in range(tokens // 16):
            rows = right[16 * m : 16 * m + 16, CZ:]
            if m % 4 == 0:
                packed.append(rows)
            else:
                packed[-1] = jnp.where(lane // CO == m % 4, rows, packed[-1])
        packed = jnp.concatenate(packed, axis=0)
        block[part][:tokens, :] = right[:, :CZ].astype(jnp.bfloat16)
        block[part][tokens:, :] = packed.astype(jnp.bfloat16)
        return normed

    def early_sends(part):
        @pl.when(jnp.logical_not(late_target))
        def _():
            first_sends(part)

    normed = []
    for part, (last, lo, hi, first, number, start, stop) in enumerate(INNER):
        for unit in inner_units:
            if unit == last:
                break
        hidden_rows(lo, hi, turned_atoms, att, w_out_t, w_token_t, hid)
        normed.append(finish(part, pooled_rows(first, number, start, stop, me, token, hid)))
        early_sends(part)

    @pl.when(jnp.logical_not(is_last))
    def _():
        for copy in to_before:
            copy.wait_recv()

    @pl.when(jnp.logical_not(is_first))
    def _():
        to_after.wait_recv()

    keys[:RIM, :] = dot(ext[:RIM, :], wk[...]).astype(jnp.bfloat16)
    values[0, :AW, :GROUP] = dot_nt(value_t, ext[:GROUP, :]).astype(jnp.bfloat16)
    x = ext[RIM + ATOMS_DEV :, :]
    keys[RIM + ATOMS_DEV :, :] = dot(x, wk[...]).astype(jnp.bfloat16)
    keep_product(ATOMS_DEV, NEXT, dot_nt(left_side, x))
    rest = jnp.concatenate([ext[ATOMS_DEV:, :], pad], axis=0)
    values[0, :AW, ATOMS_DEV:] = dot_nt(value_t, rest).astype(jnp.bfloat16)
    for _ in attend([0, UNITS, UNITS - 1], me, off, note_in, keys, queries, values, att, mixed):
        pass

    hidden_rows(0, GROUP, turned_atoms, att, w_out_t, w_token_t, hid)
    hidden_rows(ATOMS_DEV - GROUP, WIDTH, turned_atoms, att, w_out_t, w_token_t, hid)
    low = pooled_rows(0, EDGE, 0, 256, me, token, hid)
    flags = note_in[:1, :].astype(jnp.float32)
    high = pooled_rows(TOK_DEV - EDGE, EDGE, ATOMS_DEV - 256, ATOMS_DEV, me, token, hid, flags)
    outer = finish(PARTS - 1, jnp.concatenate([low, high], axis=0))

    early_sends(PARTS - 1)

    def left_copy(source, to, index):
        return pltpu.make_async_remote_copy(
            src_ref=source, dst_ref=left_in, send_sem=left_send.at[index], recv_sem=left_recv,
            device_id=place(to), device_id_type=MESH,
        )

    def left_to(child, index):
        return left_copy(left_all.at[index] if index < ROWS else left_in, child, index // 8)

    def left_sent(count, index):
        rows = left_all.at[pl.ds(0, count)]
        return pltpu.make_async_remote_copy(
            src_ref=rows, dst_ref=rows, send_sem=left_send.at[index], recv_sem=left_recv,
            device_id=place(parent), device_id_type=MESH,
        ).wait_send()

    @pl.when(is_first)
    def _():
        first_rows = jnp.concatenate([outer[:EDGE], normed[0][: HALF - EDGE]], axis=0)
        left = dot_nt(first_rows, w_pair[: 2 * CZ, :])
        for r in range(ROWS):
            rows = left[8 * r : 8 * r + 8]
            left_all[r] = jnp.concatenate([rows[:, :CZ], rows[:, CZ:]], axis=0).astype(jnp.bfloat16)
        left_in[...] = left_all[0]

    each_leader(lambda to, index: left_to(to, index).start())

    @pl.when(is_leader)
    def _():
        left_copy(left_in, parent, 0).wait_recv()

    each_head(lambda to, index: left_to(to, index).start())

    @pl.when(late_target)
    def _():
        pl.semaphore_wait(far_ready, 1)
        for part in range(PARTS):
            first_sends(part)

    @pl.when(is_head & jnp.logical_not(is_leader))
    def _():
        left_copy(left_in, parent, 0).wait_recv()

    @pl.when(is_head)
    def _():
        pl.semaphore_wait(left_ready, children)

    each_child(lambda to, index: left_to(to, index).start())
    @pl.when(row < ROWS - 1)
    def _():
        pl.semaphore_wait(pass_ready, ROWS - 1 - row)

    for part in range(PARTS):
        pass_on(part)

    @pl.when(child)
    def _():
        left_copy(left_in, parent, 0).wait_recv()

    mix_left(left_in, w_outer, base)
    left = left_in[:8, :].astype(jnp.float32)

    for part in range(PARTS):
        pass_all(part).wait_recv()
        pair_part(gathered[part], part, base, left, result)

    @pl.when(is_first)
    def _():
        left_sent(8, 0)

    @pl.when(is_leader)
    def _():
        left_sent(3, 1)

    @pl.when(is_head & (me != 1))
    def _():
        left_sent(7, 2)

    @pl.when(me == 1)
    def _():
        left_sent(6, 2)

    @pl.when(jnp.logical_not(is_last))
    def _():
        to_after.wait_send()

    @pl.when(jnp.logical_not(is_first))
    def _():
        for copy in to_before:
            copy.wait_send()

    for part in range(PARTS):
        pass_all(part).wait_send()

        @pl.when(jnp.logical_not(keeps))
        def _():
            first_copy(part).wait_send()


def mix_left(left_in, w_outer, base):
    outer = left_in[8:, :CO]
    spread = lax.broadcasted_iota(jnp.int32, (CO, CO * CO), 1) // CO
    spread = jnp.where(spread == lax.broadcasted_iota(jnp.int32, (CO, CO * CO), 0), 1.0, 0.0)
    wide = dot(outer, spread.astype(jnp.bfloat16))
    n = lax.broadcasted_iota(jnp.int32, (CO, CO * CO), 0)
    mine = lax.rem(lax.broadcasted_iota(jnp.int32, (CO, CO * CO), 1), CO) == n
    expanded = [jnp.where(mine, wide[i : i + 1], 0.0).astype(jnp.bfloat16) for i in range(8)]
    mixing = dot(jnp.concatenate(expanded, axis=0), w_outer[...]).astype(jnp.bfloat16)
    for i in range(8):
        for k in range(4):
            base[CZ + CO * k : CZ + CO * k + CO, CZ * i : CZ * i + CZ] = mixing[CO * i : CO * i + CO]


def packed_rows(tokens):
    return 16 * -(-tokens // 64)


def pair_part(gathered, part, base, left, result):
    tokens = TOKENS[part]
    lane = lax.broadcasted_iota(jnp.int32, (16, CZ), 1)
    pieces = []
    for k in range(ROWS):
        packed = gathered[k, tokens:, :].astype(jnp.float32)
        outer = [
            jnp.where(lane // CO == m % 4, packed[16 * (m // 4) : 16 * (m // 4) + 16], 0.0)
            for m in range(tokens // 16)
        ]
        outer = jnp.concatenate(outer, axis=0).astype(jnp.bfloat16)
        pieces.append(jnp.concatenate([gathered[k, :tokens, :], outer], axis=1))
    rows = jnp.concatenate(pieces, axis=0)
    for i in range(0, 8, 2):
        grid = dot(rows, base[:, CZ * i : CZ * i + 2 * CZ])
        for j in range(2):
            total = (grid[:, CZ * j : CZ * j + CZ] + left[i + j : i + j + 1]).astype(jnp.bfloat16)
            for k in range(ROWS):
                for first, to, size in SPANS[part]:
                    to += TOK_DEV * k
                    first += tokens * k
                    result[i + j, to : to + size, :] = total[first : first + size]


def body(
    atoms, window_offsets, atom_token, w_query, w_key, w_value, w_out, w_token, gain_token, w_pair, w_outer
):
    hbm = pl.BlockSpec(memory_space=pltpu.HBM)
    dma = pltpu.SemaphoreType.DMA
    bf16 = jnp.bfloat16
    return pl.pallas_call(
        embed_kernel,
        out_shape=pltpu.VMEM((8, ROWS * TOK_DEV, CZ), bf16),
        in_specs=[hbm] * 11,
        out_specs=pl.BlockSpec(memory_space=pltpu.VMEM),
        scratch_shapes=[
            pltpu.SMEM((ATOMS_DEV // QB,), jnp.int32),
            pltpu.VMEM((ATOMS_DEV,), jnp.int32),
            pltpu.VMEM((AW, AW), bf16),
            pltpu.VMEM((AW, AW), bf16),
            pltpu.VMEM((AW, AW), bf16),
            pltpu.VMEM((AW, AW), bf16),
            pltpu.VMEM((AW, TW), bf16),
            pltpu.VMEM((TW,), bf16),
            pltpu.VMEM((2 * CZ + 2 * CO, TW), bf16),
            pltpu.VMEM((CO * CO, CZ), bf16),
            *[pltpu.VMEM((ROWS, tokens + packed_rows(tokens), CZ), bf16) for tokens in TOKENS],
            pltpu.VMEM((2 * CZ, 8 * CZ), bf16),
            pltpu.VMEM((EXT, AW), bf16),
            pltpu.VMEM((EXT, AW), bf16),
            pltpu.VMEM((AW, WIDTH), bf16),
            pltpu.VMEM((2, AW + 16, WIDTH + GROUP), bf16),
            pltpu.VMEM((AW, WIDTH), bf16),
            pltpu.VMEM((WIDE, WIDTH), bf16),
            pltpu.VMEM((AW, WIDTH), bf16),
            pltpu.VMEM((AW, AW), bf16),
            pltpu.VMEM((TW, AW), bf16),
            pltpu.VMEM((2 * CZ, TW), bf16),
            pltpu.VMEM((16, NEXT), bf16),
            pltpu.VMEM((16, NEXT), bf16),
            *[pltpu.VMEM((tokens + packed_rows(tokens), CZ), bf16) for tokens in TOKENS],
            pltpu.VMEM((ROWS, 16, CZ), bf16),
            pltpu.VMEM((16, CZ), bf16),
            dma((3,)), dma((10,)), dma((3,)), dma((3,)),
            dma((PARTS,)), dma((PARTS,)), dma((PARTS,)), dma((PARTS,)), dma((PARTS,)), dma((3,)), dma,
            *[pltpu.SemaphoreType.REGULAR] * 3,
        ],
        compiler_params=pltpu.CompilerParams(
            collective_id=0, has_side_effects=True, vmem_limit_bytes=60 * 1024 * 1024
        ),
        name="embed",
    )(
        atoms, window_offsets, atom_token, w_query, w_key, w_value, w_out, w_token, gain_token, w_pair.T,
        w_outer,
    )


def solution(mesh):
    split = P(("row", "col"))
    placed = (P(("row", "col"), None), split, split) + (P(),) * 8
    return jax.shard_map(
        body, mesh=mesh, in_specs=placed, out_specs=P("row", "col", None), check_vma=False
    )
```

```python
import jax
import jax.numpy as jnp
from jax import lax
from jax.experimental import pallas as pl
from jax.experimental.pallas import tpu as pltpu
from jax.sharding import PartitionSpec as P

AW = 128
HEADS = 4
TW = 384
CZ = 128
CO = 32
QB = 32
RIM = 64
ROWS = 8
COLS = 32
DEVICES = ROWS * COLS
ATOMS_DEV = 1536
TOK_DEV = 128
NEXT = 128
NEXT_USED = 96
EXT = RIM + ATOMS_DEV + NEXT
WIDTH = ATOMS_DEV + NEXT
GROUP = 128
GROUPS = ATOMS_DEV // GROUP
UNITS = 2 * GROUPS
AHEAD = 3
BEHIND = 2
HALF = 64
EDGE = 16
INNER = ((UNITS - 2, 128, 1408, 16, 96, 128, 1408),)
TOKENS = tuple(piece[4] for piece in INNER) + (32,)
PARTS = len(TOKENS)
SPANS = tuple(((0, piece[3], piece[4]),) for piece in INNER) + (((0, 0, 16), (16, 112, 16)),)
WIDE = TW + 128
EXP_SCALE = float(32 ** -0.5 * 1.4426950408889634)
MESH = pl.DeviceIdType.MESH
NT = (((1,), (1,)), ((), ()))


def dot(a, b):
    return jnp.dot(a, b, preferred_element_type=jnp.float32)


def place(device):
    return (lax.div(device, COLS), lax.rem(device, COLS))


def dot_nt(a, b):
    return lax.dot_general(a, b, NT, preferred_element_type=jnp.float32)


def turned(w):
    return w[...].astype(jnp.float32).T.astype(jnp.bfloat16)


def unit_scores(unit, keys, queries):
    g, j = unit // 2, unit % 2
    q = queries[:, GROUP * g : GROUP * g + GROUP]
    side = (lax.broadcasted_iota(jnp.int32, (HALF, GROUP), 0) // 32 == j) == (
        lax.broadcasted_iota(jnp.int32, (HALF, GROUP), 1) < HALF
    )
    none = jnp.zeros((HALF, GROUP), jnp.bfloat16)
    heads = [jnp.where(side, q[HALF * t : HALF * t + HALF], none) for t in range(2)]
    operand = jnp.concatenate(
        [jnp.concatenate([heads[0], none], axis=1), jnp.concatenate([none, heads[1]], axis=1)], axis=0
    )
    return dot(keys[HALF * unit : HALF * unit + 192, :], operand)


def unit_softmax(unit, scores, me, off, off_next):
    lane = lax.broadcasted_iota(jnp.int32, (1, GROUP), 1)
    second = lax.rem(lane // QB, 2) == 1
    if unit == UNITS:
        start = off_next[8:9, :].astype(jnp.int32) + RIM
    else:
        start = jnp.where(second, off[2 * unit + 1] + RIM + QB, off[2 * unit] + RIM)
    low, high = start, start + 128
    if unit == 0:
        low = jnp.maximum(low, jnp.where(me == 0, RIM, 0))
    if unit == UNITS - 1:
        high = jnp.minimum(high, jnp.where(me == DEVICES - 1, 128, 192))
    row = lax.broadcasted_iota(jnp.int32, (HALF, GROUP), 0)
    enters, stays = row >= low, row + 128 < high
    parts = []
    for t in range(2):
        tile = scores[:, GROUP * t : GROUP * t + GROUP]
        tile = jnp.concatenate(
            [jnp.where(enters, tile[:64], -1e30), tile[64:128], jnp.where(stays, tile[128:], -1e30)], axis=0
        )
        top = jnp.max(tile, axis=0, keepdims=True)
        parts.append(jnp.exp2((tile - top) * EXP_SCALE).astype(jnp.bfloat16))
    return jnp.concatenate(
        [jnp.concatenate(parts, axis=1), jnp.zeros((HALF, 2 * GROUP), jnp.bfloat16)], axis=0
    )


def group_store(g, mixed, att):
    left = lax.broadcasted_iota(jnp.int32, (1, GROUP), 1) < HALF
    for h in range(HEADS):
        lanes = slice(GROUP * (h // 2), GROUP * (h // 2) + GROUP)
        a, b = mixed if h % 2 == 0 else mixed[::-1]
        total = jnp.where(left, a[AW : AW + 1, lanes], b[AW : AW + 1, lanes])
        value = jnp.where(left, a[32 * h : 32 * h + 32, lanes], b[32 * h : 32 * h + 32, lanes]) * (1.0 / total)
        if h % 2 == 1:
            value = pltpu.roll(value, HALF, 1)
        att[32 * h : 32 * h + 32, GROUP * g : GROUP * g + GROUP] = value.astype(jnp.bfloat16)


def attend(units, me, off, off_next, keys, queries, values, att, mixed):
    scores, lifted = {}, {}
    for i in range(len(units) + AHEAD + BEHIND):
        if i < len(units):
            scores[i] = unit_scores(units[i], keys, queries)
        k = i - AHEAD
        if 0 <= k < len(units):
            lifted[k] = unit_softmax(units[k], scores.pop(k), me, off, off_next)
        k = i - AHEAD - BEHIND
        if 0 <= k < len(units):
            g, j = units[k] // 2, units[k] % 2
            mixed[units[k]] = dot(values[j, :, GROUP * g : GROUP * g + 2 * GROUP], lifted.pop(k))
            if units[k] == UNITS:
                mixed[UNITS + 1] = mixed[UNITS]
            if 2 * g in mixed and 2 * g + 1 in mixed:
                group_store(g, [mixed.pop(2 * g), mixed.pop(2 * g + 1)], att)
            yield units[k]


def hidden_rows(lo, hi, turned_atoms, att, w_out_t, w_token_t, hid):
    mixed = dot(w_out_t[...], att[:, lo:hi])
    update = (turned_atoms[:, lo:hi].astype(jnp.float32) + mixed).astype(jnp.bfloat16)
    hid[:TW, lo:hi] = jnp.maximum(dot(w_token_t[...], update), 0.0).astype(jnp.bfloat16)


def pooled_rows(first, count, lo, hi, device, token, hid, flags=None):
    slot = token[...].reshape(1, ATOMS_DEV)[:, lo:hi] - device * TOK_DEV
    rows = lax.broadcasted_iota(jnp.int32, (count, hi - lo), 0) + first
    one_hot = jnp.where(rows == slot, 1.0, 0.0).astype(jnp.bfloat16)
    if flags is not None:
        last = lax.broadcasted_iota(jnp.int32, (count, NEXT), 0) == count - 1
        one_hot = jnp.concatenate([one_hot, jnp.where(last, flags, 0.0).astype(jnp.bfloat16)], axis=1)
        hi += NEXT
    return dot_nt(one_hot, hid[:, lo:hi])


def token_normed(pooled, gain):
    count = pooled[:, TW:]
    single = pooled[:, :TW] / jnp.concatenate([count] * 3, axis=1)
    centre = single - jnp.mean(single, axis=1, keepdims=True)
    variance = jnp.mean(centre * centre, axis=1, keepdims=True)
    return (centre * lax.rsqrt(variance + 1e-05) * gain).astype(jnp.bfloat16)


def embed_kernel(
    atoms, off_hbm, token_hbm, wq_hbm, wk_hbm, wv_hbm, w_out_hbm, w_token_hbm, gain_hbm, w_pair_hbm, w_outer_hbm,
    result,
    off, token, wq, wk, wv, w_out, w_token, gain, w_pair, w_outer,
    gathered0, gathered1, base,
    ext, keys, queries, values, att, hid, turned_atoms, w_out_t, w_token_t, w_right,
    note_out, note_in, block0, block1, left_all, left_in,
    own_sem, load_sem, halo_send, halo_recv,
    first_send, first_recv, local_sem, pass_send, pass_recv, left_send, left_recv, far_ready, left_ready, pass_ready,
):
    gathered, block = (gathered0, gathered1), (block0, block1)
    row = lax.axis_index("row")
    col = lax.axis_index("col")
    me = row * COLS + col
    before = lax.rem(me + DEVICES - 1, DEVICES)
    after = lax.rem(me + 1, DEVICES)
    slot = lax.rem(me, ROWS)
    my_y, my_z = lax.div(row, 2), lax.rem(row, 2)
    my_x, my_zh = lax.div(col, 8), lax.rem(lax.div(col, 2), 4)
    depth = 2 * my_zh + my_z
    group_col = lax.div(me, ROWS)
    relay_y = lax.rem(my_y + 6 + my_zh - 2 * my_z - lax.div(my_x, 2) + 2 * lax.rem(my_x, 2), 4)
    my_core = lax.rem(col, 2)
    target = (2 * relay_y + my_core) * COLS + group_col
    target_depth = 4 * my_z + 2 * lax.div(my_x, 2) + my_core

    def held_by(y, z):
        return 2 * lax.rem(y + 6 + my_zh - my_x + 2 * my_core, 4) + z

    held = held_by(my_y, my_z)
    source = ROWS * col + held
    source_depth = 2 * lax.div(held, 2) + lax.div(my_zh, 2)
    keeps = target == me
    peers = [(2, 1), (2, 0), (1, 1), (3, 1), (1, 0), (3, 0), (0, 1)]
    col_in = lax.rem(col, 8)
    is_head, is_leader, is_first, is_last = col_in == 1, col == 1, me == 0, me == DEVICES - 1
    parent = jnp.where(is_leader, 0, jnp.where(is_head, row * COLS + 1, me - col_in + 1))

    def count(condition):
        return jnp.where(condition, 1, 0)

    def signal(device, semaphore=None):
        pl.semaphore_signal(
            barrier if semaphore is None else semaphore, inc=1, device_id=place(device), device_id_type=MESH
        )

    own = [
        pltpu.make_async_copy(atoms.at[pl.ds(lo, 512)], ext.at[pl.ds(RIM + lo, 512)], own_sem.at[lo // 512])
        for lo in range(0, ATOMS_DEV, 512)
    ]
    for copy in own:
        copy.start()
    pieces = [
        (wq_hbm, wq), (wk_hbm, wk), (wv_hbm, wv), (off_hbm, off), (token_hbm, token),
        (w_out_hbm, w_out), (w_token_hbm, w_token), (gain_hbm, gain), (w_pair_hbm, w_pair),
        (w_outer_hbm, w_outer),
    ]
    loads = [pltpu.make_async_copy(a, b, load_sem.at[i]) for i, (a, b) in enumerate(pieces)]
    for load in loads:
        load.start()

    barrier = pltpu.get_barrier_semaphore()

    @pl.when(jnp.logical_not(is_first))
    def _():
        signal(before)

    @pl.when(jnp.logical_not(is_last))
    def _():
        signal(after)

    @pl.when(is_head)
    def _():
        signal(parent)

    arrivals = 2 - count(is_first) - count(is_last) + 8 * count(is_first) + 3 * count(is_leader)

    @pl.when((source != me) & (source_depth >= depth))
    def _():
        signal(source)

    @pl.when(jnp.logical_not(keeps) & (target_depth > depth))
    def _():
        signal(target)

    arrivals += count((source != me) & (source_depth < depth))
    arrivals += count(jnp.logical_not(keeps) & (target_depth <= depth))
    late_target = jnp.logical_not(keeps) & (target_depth > depth)

    def peer(i, j):
        return (2 * lax.rem(my_y + i, 4) + lax.rem(my_z + j, 2)) * COLS + col

    for i, j in peers:
        @pl.when(peer(i, j) > me)
        def _():
            signal(peer(i, j))
    arrivals += row
    child = jnp.logical_not(is_head | is_first)
    arrivals += count(child)
    children = 7 - count((row == 0) & is_leader)

    def each_child(act):
        for c in range(8):
            if c != 1:
                @pl.when(is_head & (me + c != 1))
                def _():
                    act(me + c - 1, 16 + c)

    def each_leader(act):
        @pl.when(is_first)
        def _():
            for r in range(ROWS):
                act(r * COLS + 1, r)

    def each_head(act):
        @pl.when(is_leader)
        def _():
            for x in range(1, 4):
                act(me + 8 * x, 8 + x)

    each_child(lambda to, _: signal(to))

    for load in loads[:3]:
        load.wait()

    one = lax.broadcasted_iota(jnp.int32, (CZ, CZ), 0) == lax.broadcasted_iota(jnp.int32, (CZ, CZ), 1)
    eye = jnp.where(one, 1.0, 0.0).astype(jnp.bfloat16)
    value_t = turned(wv)
    left_side = jnp.concatenate([turned(wq), value_t, eye], axis=0)
    hid[TW:, :] = jnp.ones((WIDE - TW, WIDTH), jnp.bfloat16)
    for j in range(2):
        values[j, AW:, :] = jnp.ones((16, WIDTH + GROUP), jnp.bfloat16)
    def keep_product(lo, size, product):
        for h in range(HEADS):
            rows = slice(32 * h, 32 * h + 32)
            for part in range(0, size, GROUP):
                q = product[rows, part : part + GROUP]
                if h % 2 == 1:
                    q = pltpu.roll(q, HALF, 1)
                queries[rows, lo + part : lo + part + GROUP] = q.astype(jnp.bfloat16)
        values[1, :AW, lo : lo + size] = product[AW : 2 * AW].astype(jnp.bfloat16)
        turned_atoms[:, lo : lo + size] = product[2 * AW :].astype(jnp.bfloat16)

    for lo in range(0, ATOMS_DEV, 512):
        own[lo // 512].wait()
        x = ext[RIM + lo : RIM + lo + 512, :]
        keys[RIM + lo : RIM + lo + 512, :] = dot(x, wk[...]).astype(jnp.bfloat16)
        for part in range(0, 512, 256):
            keep_product(lo + part, 256, dot_nt(left_side, x[part : part + 256]))
    for load in loads[3:5]:
        load.wait()
    flags = token[...].reshape(1, ATOMS_DEV)[:, :NEXT] == me * TOK_DEV - 1
    upper = lax.broadcasted_iota(jnp.int32, (16, NEXT), 0) < 8
    note = jnp.where(upper, jnp.where(flags, 1.0, 0.0), off[0].astype(jnp.float32))
    note_out[...] = note.astype(jnp.bfloat16)
    ext[RIM + ATOMS_DEV + NEXT_USED :, :] = jnp.zeros((NEXT - NEXT_USED, AW), jnp.bfloat16)

    @pl.when(is_first)
    def _():
        ext[:RIM, :] = jnp.zeros((RIM, AW), jnp.bfloat16)

    @pl.when(is_last)
    def _():
        ext[RIM + ATOMS_DEV :, :] = jnp.zeros((NEXT, AW), jnp.bfloat16)
        note_in[...] = jnp.zeros((16, NEXT), jnp.bfloat16)

    pl.semaphore_wait(barrier, arrivals)

    to_after = pltpu.make_async_remote_copy(
        src_ref=atoms.at[pl.ds(ATOMS_DEV - RIM, RIM)], dst_ref=ext.at[pl.ds(0, RIM)],
        send_sem=halo_send.at[0], recv_sem=halo_recv.at[0],
        device_id=place(after), device_id_type=MESH,
    )
    to_before = [
        pltpu.make_async_remote_copy(
            src_ref=atoms.at[pl.ds(0, NEXT_USED)], dst_ref=ext.at[pl.ds(RIM + ATOMS_DEV, NEXT_USED)],
            send_sem=halo_send.at[1], recv_sem=halo_recv.at[1],
            device_id=place(before), device_id_type=MESH,
        ),
        pltpu.make_async_remote_copy(
            src_ref=note_out, dst_ref=note_in, send_sem=halo_send.at[2], recv_sem=halo_recv.at[2],
            device_id=place(before), device_id_type=MESH,
        ),
    ]

    @pl.when(jnp.logical_not(is_last))
    def _():
        to_after.start()

    @pl.when(jnp.logical_not(is_first))
    def _():
        for copy in to_before:
            copy.start()

    @pl.when((source != me) & (source_depth < depth))
    def _():
        signal(source, far_ready)

    @pl.when(child)
    def _():
        signal(parent, left_ready)

    for i, j in peers:
        @pl.when(peer(i, j) < me)
        def _():
            signal(peer(i, j), pass_ready)

    for lo in range(128, ATOMS_DEV, 256):
        hi = min(lo + 256, ATOMS_DEV)
        values[0, :AW, lo:hi] = dot_nt(value_t, ext[lo:hi, :]).astype(jnp.bfloat16)
    pad = jnp.zeros((RIM, AW), jnp.bfloat16)
    rest = jnp.concatenate([ext[ATOMS_DEV : ATOMS_DEV + RIM, :], pad], axis=0)
    values[0, :AW, ATOMS_DEV : ATOMS_DEV + GROUP] = dot_nt(value_t, rest).astype(jnp.bfloat16)

    for load in loads[5:]:
        load.wait()
    for i in range(8):
        base[:CZ, CZ * i : CZ * i + CZ] = eye
    w_out_t[...] = turned(w_out)
    w_token_t[...] = turned(w_token)
    w_right[:CZ, :] = w_pair[CZ + CO : 2 * CZ + CO, :]
    for m in range(4):
        w_right[CZ + CO * m : CZ + CO * m + CO, :] = w_pair[2 * CZ + CO :, :]

    mixed = {}
    inner_units = attend(list(range(1, UNITS - 1)), me, off, note_in, keys, queries, values, att, mixed)

    def first_copy(part):
        return pltpu.make_async_remote_copy(
            src_ref=block[part], dst_ref=gathered[part].at[slot],
            send_sem=first_send.at[part], recv_sem=first_recv.at[part],
            device_id=place(target), device_id_type=MESH,
        )

    def local_copy(part):
        return pltpu.make_async_copy(block[part], gathered[part].at[slot], local_sem.at[part])

    def first_sends(part):
        @pl.when(jnp.logical_not(keeps))
        def _():
            first_copy(part).start()

        @pl.when(keeps)
        def _():
            local_copy(part).start()

    def pass_copy(part, i, j, holder):
        return pltpu.make_async_remote_copy(
            src_ref=gathered[part].at[holder], dst_ref=gathered[part].at[holder],
            send_sem=pass_send.at[part], recv_sem=pass_recv.at[part],
            device_id=place(peer(i, j)), device_id_type=MESH,
        )

    def pass_all(part):
        blocks = gathered[part].at[pl.ds(0, ROWS - 1)]
        return pltpu.make_async_remote_copy(
            src_ref=blocks, dst_ref=blocks, send_sem=pass_send.at[part], recv_sem=pass_recv.at[part],
            device_id=place(peer(0, 1)), device_id_type=MESH,
        )

    def pass_on(part):
        @pl.when(source != me)
        def _():
            pltpu.make_async_remote_copy(
                src_ref=block[part], dst_ref=gathered[part].at[held],
                send_sem=first_send.at[part], recv_sem=first_recv.at[part],
                device_id=place(source), device_id_type=MESH,
            ).wait_recv()

        @pl.when(source == me)
        def _():
            local_copy(part).wait()

        for i, j in peers:
            pass_copy(part, i, j, held).start()

    def finish(part, pooled):
        tokens = TOKENS[part]
        normed = token_normed(pooled, gain[...].reshape(1, TW).astype(jnp.float32))
        right = dot_nt(normed, w_right[...])
        lane = lax.broadcasted_iota(jnp.int32, (16, CZ), 1)
        packed = []
        for m in range(tokens // 16):
            rows = right[16 * m : 16 * m + 16, CZ:]
            if m % 4 == 0:
                packed.append(rows)
            else:
                packed[-1] = jnp.where(lane // CO == m % 4, rows, packed[-1])
        packed = jnp.concatenate(packed, axis=0)
        block[part][:tokens, :] = right[:, :CZ].astype(jnp.bfloat16)
        block[part][tokens:, :] = packed.astype(jnp.bfloat16)
        return normed

    def early_sends(part):
        @pl.when(jnp.logical_not(late_target))
        def _():
            first_sends(part)

    normed = []
    for part, (last, lo, hi, first, number, start, stop) in enumerate(INNER):
        for unit in inner_units:
            if unit == last:
                break
        hidden_rows(lo, hi, turned_atoms, att, w_out_t, w_token_t, hid)
        normed.append(finish(part, pooled_rows(first, number, start, stop, me, token, hid)))
        early_sends(part)

    @pl.when(jnp.logical_not(is_last))
    def _():
        for copy in to_before:
            copy.wait_recv()

    @pl.when(jnp.logical_not(is_first))
    def _():
        to_after.wait_recv()

    keys[:RIM, :] = dot(ext[:RIM, :], wk[...]).astype(jnp.bfloat16)
    values[0, :AW, :GROUP] = dot_nt(value_t, ext[:GROUP, :]).astype(jnp.bfloat16)
    x = ext[RIM + ATOMS_DEV :, :]
    keys[RIM + ATOMS_DEV :, :] = dot(x, wk[...]).astype(jnp.bfloat16)
    keep_product(ATOMS_DEV, NEXT, dot_nt(left_side, x))
    rest = jnp.concatenate([ext[ATOMS_DEV:, :], pad], axis=0)
    values[0, :AW, ATOMS_DEV:] = dot_nt(value_t, rest).astype(jnp.bfloat16)
    for _ in attend([0, UNITS, UNITS - 1], me, off, note_in, keys, queries, values, att, mixed):
        pass

    hidden_rows(0, GROUP, turned_atoms, att, w_out_t, w_token_t, hid)
    hidden_rows(ATOMS_DEV - GROUP, WIDTH, turned_atoms, att, w_out_t, w_token_t, hid)
    low = pooled_rows(0, EDGE, 0, 256, me, token, hid)
    flags = note_in[:1, :].astype(jnp.float32)
    high = pooled_rows(TOK_DEV - EDGE, EDGE, ATOMS_DEV - 256, ATOMS_DEV, me, token, hid, flags)
    outer = finish(PARTS - 1, jnp.concatenate([low, high], axis=0))

    early_sends(PARTS - 1)

    def left_copy(source, to, index):
        return pltpu.make_async_remote_copy(
            src_ref=source, dst_ref=left_in, send_sem=left_send.at[index], recv_sem=left_recv,
            device_id=place(to), device_id_type=MESH,
        )

    def left_to(child, index):
        return left_copy(left_all.at[index] if index < ROWS else left_in, child, index // 8)

    def left_sent(count, index):
        rows = left_all.at[pl.ds(0, count)]
        return pltpu.make_async_remote_copy(
            src_ref=rows, dst_ref=rows, send_sem=left_send.at[index], recv_sem=left_recv,
            device_id=place(parent), device_id_type=MESH,
        ).wait_send()

    @pl.when(is_first)
    def _():
        first_rows = jnp.concatenate([outer[:EDGE], normed[0][: HALF - EDGE]], axis=0)
        left = dot_nt(first_rows, w_pair[: 2 * CZ, :])
        for r in range(ROWS):
            rows = left[8 * r : 8 * r + 8]
            left_all[r] = jnp.concatenate([rows[:, :CZ], rows[:, CZ:]], axis=0).astype(jnp.bfloat16)
        left_in[...] = left_all[0]

    each_leader(lambda to, index: left_to(to, index).start())

    @pl.when(is_leader)
    def _():
        left_copy(left_in, parent, 0).wait_recv()

    each_head(lambda to, index: left_to(to, index).start())

    @pl.when(late_target)
    def _():
        pl.semaphore_wait(far_ready, 1)
        for part in range(PARTS):
            first_sends(part)

    @pl.when(is_head & jnp.logical_not(is_leader))
    def _():
        left_copy(left_in, parent, 0).wait_recv()

    @pl.when(is_head)
    def _():
        pl.semaphore_wait(left_ready, children)

    each_child(lambda to, index: left_to(to, index).start())
    @pl.when(row < ROWS - 1)
    def _():
        pl.semaphore_wait(pass_ready, ROWS - 1 - row)

    for part in range(PARTS):
        pass_on(part)

    @pl.when(child)
    def _():
        left_copy(left_in, parent, 0).wait_recv()

    mix_left(left_in, w_outer, base)
    left = left_in[:8, :].astype(jnp.float32)

    for part in range(PARTS):
        pass_all(part).wait_recv()
        pair_part(gathered[part], part, base, left, result)

    @pl.when(is_first)
    def _():
        left_sent(8, 0)

    @pl.when(is_leader)
    def _():
        left_sent(3, 1)

    @pl.when(is_head & (me != 1))
    def _():
        left_sent(7, 2)

    @pl.when(me == 1)
    def _():
        left_sent(6, 2)

    @pl.when(jnp.logical_not(is_last))
    def _():
        to_after.wait_send()

    @pl.when(jnp.logical_not(is_first))
    def _():
        for copy in to_before:
            copy.wait_send()

    for part in range(PARTS):
        pass_all(part).wait_send()

        @pl.when(jnp.logical_not(keeps))
        def _():
            first_copy(part).wait_send()


def mix_left(left_in, w_outer, base):
    outer = left_in[8:, :CO]
    spread = lax.broadcasted_iota(jnp.int32, (CO, CO * CO), 1) // CO
    spread = jnp.where(spread == lax.broadcasted_iota(jnp.int32, (CO, CO * CO), 0), 1.0, 0.0)
    wide = dot(outer, spread.astype(jnp.bfloat16))
    n = lax.broadcasted_iota(jnp.int32, (CO, CO * CO), 0)
    mine = lax.rem(lax.broadcasted_iota(jnp.int32, (CO, CO * CO), 1), CO) == n
    expanded = [jnp.where(mine, wide[i : i + 1], 0.0).astype(jnp.bfloat16) for i in range(8)]
    mixing = dot(jnp.concatenate(expanded, axis=0), w_outer[...]).astype(jnp.bfloat16)
    for i in range(8):
        for k in range(4):
            base[CZ + CO * k : CZ + CO * k + CO, CZ * i : CZ * i + CZ] = mixing[CO * i : CO * i + CO]


def packed_rows(tokens):
    return 16 * -(-tokens // 64)


def pair_part(gathered, part, base, left, result):
    tokens = TOKENS[part]
    lane = lax.broadcasted_iota(jnp.int32, (16, CZ), 1)
    pieces = []
    for k in range(ROWS):
        packed = gathered[k, tokens:, :].astype(jnp.float32)
        outer = [
            jnp.where(lane // CO == m % 4, packed[16 * (m // 4) : 16 * (m // 4) + 16], 0.0)
            for m in range(tokens // 16)
        ]
        outer = jnp.concatenate(outer, axis=0).astype(jnp.bfloat16)
        pieces.append(jnp.concatenate([gathered[k, :tokens, :], outer], axis=1))
    rows = jnp.concatenate(pieces, axis=0)
    for i in range(0, 8, 2):
        grid = dot(rows, base[:, CZ * i : CZ * i + 2 * CZ])
        for j in range(2):
            total = (grid[:, CZ * j : CZ * j + CZ] + left[i + j : i + j + 1]).astype(jnp.bfloat16)
            for k in range(ROWS):
                for first, to, size in SPANS[part]:
                    to += TOK_DEV * k
                    first += tokens * k
                    result[i + j, to : to + size, :] = total[first : first + size]


def body(
    atoms, window_offsets, atom_token, w_query, w_key, w_value, w_out, w_token, gain_token, w_pair, w_outer
):
    hbm = pl.BlockSpec(memory_space=pltpu.HBM)
    dma = pltpu.SemaphoreType.DMA
    bf16 = jnp.bfloat16
    return pl.pallas_call(
        embed_kernel,
        out_shape=pltpu.VMEM((8, ROWS * TOK_DEV, CZ), bf16),
        in_specs=[hbm] * 11,
        out_specs=pl.BlockSpec(memory_space=pltpu.VMEM),
        scratch_shapes=[
            pltpu.SMEM((ATOMS_DEV // QB,), jnp.int32),
            pltpu.VMEM((ATOMS_DEV,), jnp.int32),
            pltpu.VMEM((AW, AW), bf16),
            pltpu.VMEM((AW, AW), bf16),
            pltpu.VMEM((AW, AW), bf16),
            pltpu.VMEM((AW, AW), bf16),
            pltpu.VMEM((AW, TW), bf16),
            pltpu.VMEM((TW,), bf16),
            pltpu.VMEM((2 * CZ + 2 * CO, TW), bf16),
            pltpu.VMEM((CO * CO, CZ), bf16),
            *[pltpu.VMEM((ROWS, tokens + packed_rows(tokens), CZ), bf16) for tokens in TOKENS],
            pltpu.VMEM((2 * CZ, 8 * CZ), bf16),
            pltpu.VMEM((EXT, AW), bf16),
            pltpu.VMEM((EXT, AW), bf16),
            pltpu.VMEM((AW, WIDTH), bf16),
            pltpu.VMEM((2, AW + 16, WIDTH + GROUP), bf16),
            pltpu.VMEM((AW, WIDTH), bf16),
            pltpu.VMEM((WIDE, WIDTH), bf16),
            pltpu.VMEM((AW, WIDTH), bf16),
            pltpu.VMEM((AW, AW), bf16),
            pltpu.VMEM((TW, AW), bf16),
            pltpu.VMEM((2 * CZ, TW), bf16),
            pltpu.VMEM((16, NEXT), bf16),
            pltpu.VMEM((16, NEXT), bf16),
            *[pltpu.VMEM((tokens + packed_rows(tokens), CZ), bf16) for tokens in TOKENS],
            pltpu.VMEM((ROWS, 16, CZ), bf16),
            pltpu.VMEM((16, CZ), bf16),
            dma((3,)), dma((10,)), dma((3,)), dma((3,)),
            dma((PARTS,)), dma((PARTS,)), dma((PARTS,)), dma((PARTS,)), dma((PARTS,)), dma((3,)), dma,
            *[pltpu.SemaphoreType.REGULAR] * 3,
        ],
        compiler_params=pltpu.CompilerParams(
            collective_id=0, has_side_effects=True, vmem_limit_bytes=60 * 1024 * 1024
        ),
        name="embed",
    )(
        atoms, window_offsets, atom_token, w_query, w_key, w_value, w_out, w_token, gain_token, w_pair.T,
        w_outer,
    )


def solution(mesh):
    split = P(("row", "col"))
    placed = (P(("row", "col"), None), split, split) + (P(),) * 8
    return jax.shard_map(
        body, mesh=mesh, in_specs=placed, out_specs=P("row", "col", None), check_vma=False
    )
```

```python
import jax
import jax.numpy as jnp
from jax import lax
from jax.experimental import pallas as pl
from jax.experimental.pallas import tpu as pltpu
from jax.sharding import PartitionSpec as P

AW = 128
HEADS = 4
TW = 384
CZ = 128
CO = 32
QB = 32
RIM = 64
ROWS = 8
COLS = 32
DEVICES = ROWS * COLS
ATOMS_DEV = 1536
TOK_DEV = 128
NEXT = 128
NEXT_USED = 96
EXT = RIM + ATOMS_DEV + NEXT
WIDTH = ATOMS_DEV + NEXT
GROUP = 128
GROUPS = ATOMS_DEV // GROUP
UNITS = 2 * GROUPS
AHEAD = 3
BEHIND = 2
HALF = 64
EDGE = 16
INNER = ((UNITS - 2, 128, 1408, 16, 96, 128, 1408),)
TOKENS = tuple(piece[4] for piece in INNER) + (32,)
PARTS = len(TOKENS)
SPANS = tuple(((0, piece[3], piece[4]),) for piece in INNER) + (((0, 0, 16), (16, 112, 16)),)
WIDE = TW + 128
EXP_SCALE = float(32 ** -0.5 * 1.4426950408889634)
MESH = pl.DeviceIdType.MESH
NT = (((1,), (1,)), ((), ()))


def dot(a, b):
    return jnp.dot(a, b, preferred_element_type=jnp.float32)


def place(device):
    return (lax.div(device, COLS), lax.rem(device, COLS))


def dot_nt(a, b):
    return lax.dot_general(a, b, NT, preferred_element_type=jnp.float32)


def turned(w):
    return w[...].astype(jnp.float32).T.astype(jnp.bfloat16)


def unit_scores(unit, keys, queries):
    g, j = unit // 2, unit % 2
    q = queries[:, GROUP * g : GROUP * g + GROUP]
    side = (lax.broadcasted_iota(jnp.int32, (HALF, GROUP), 0) // 32 == j) == (
        lax.broadcasted_iota(jnp.int32, (HALF, GROUP), 1) < HALF
    )
    none = jnp.zeros((HALF, GROUP), jnp.bfloat16)
    heads = [jnp.where(side, q[HALF * t : HALF * t + HALF], none) for t in range(2)]
    operand = jnp.concatenate(
        [jnp.concatenate([heads[0], none], axis=1), jnp.concatenate([none, heads[1]], axis=1)], axis=0
    )
    return dot(keys[HALF * unit : HALF * unit + 192, :], operand)


def unit_softmax(unit, scores, me, off, off_next):
    lane = lax.broadcasted_iota(jnp.int32, (1, GROUP), 1)
    second = lax.rem(lane // QB, 2) == 1
    if unit == UNITS:
        start = off_next[8:9, :].astype(jnp.int32) + RIM
    else:
        start = jnp.where(second, off[2 * unit + 1] + RIM + QB, off[2 * unit] + RIM)
    low, high = start, start + 128
    if unit == 0:
        low = jnp.maximum(low, jnp.where(me == 0, RIM, 0))
    if unit == UNITS - 1:
        high = jnp.minimum(high, jnp.where(me == DEVICES - 1, 128, 192))
    row = lax.broadcasted_iota(jnp.int32, (HALF, GROUP), 0)
    enters, stays = row >= low, row + 128 < high
    parts = []
    for t in range(2):
        tile = scores[:, GROUP * t : GROUP * t + GROUP]
        tile = jnp.concatenate(
            [jnp.where(enters, tile[:64], -1e30), tile[64:128], jnp.where(stays, tile[128:], -1e30)], axis=0
        )
        top = jnp.max(tile, axis=0, keepdims=True)
        parts.append(jnp.exp2((tile - top) * EXP_SCALE).astype(jnp.bfloat16))
    return jnp.concatenate(
        [jnp.concatenate(parts, axis=1), jnp.zeros((HALF, 2 * GROUP), jnp.bfloat16)], axis=0
    )


def group_store(g, mixed, att):
    left = lax.broadcasted_iota(jnp.int32, (1, GROUP), 1) < HALF
    for h in range(HEADS):
        lanes = slice(GROUP * (h // 2), GROUP * (h // 2) + GROUP)
        a, b = mixed if h % 2 == 0 else mixed[::-1]
        total = jnp.where(left, a[AW : AW + 1, lanes], b[AW : AW + 1, lanes])
        value = jnp.where(left, a[32 * h : 32 * h + 32, lanes], b[32 * h : 32 * h + 32, lanes]) * (1.0 / total)
        if h % 2 == 1:
            value = pltpu.roll(value, HALF, 1)
        att[32 * h : 32 * h + 32, GROUP * g : GROUP * g + GROUP] = value.astype(jnp.bfloat16)


def attend(units, me, off, off_next, keys, queries, values, att, mixed):
    scores, lifted = {}, {}
    for i in range(len(units) + AHEAD + BEHIND):
        if i < len(units):
            scores[i] = unit_scores(units[i], keys, queries)
        k = i - AHEAD
        if 0 <= k < len(units):
            lifted[k] = unit_softmax(units[k], scores.pop(k), me, off, off_next)
        k = i - AHEAD - BEHIND
        if 0 <= k < len(units):
            g, j = units[k] // 2, units[k] % 2
            mixed[units[k]] = dot(values[j, :, GROUP * g : GROUP * g + 2 * GROUP], lifted.pop(k))
            if units[k] == UNITS:
                mixed[UNITS + 1] = mixed[UNITS]
            if 2 * g in mixed and 2 * g + 1 in mixed:
                group_store(g, [mixed.pop(2 * g), mixed.pop(2 * g + 1)], att)
            yield units[k]


def hidden_rows(lo, hi, turned_atoms, att, w_out_t, w_token_t, hid):
    mixed = dot(w_out_t[...], att[:, lo:hi])
    update = (turned_atoms[:, lo:hi].astype(jnp.float32) + mixed).astype(jnp.bfloat16)
    hid[:TW, lo:hi] = jnp.maximum(dot(w_token_t[...], update), 0.0).astype(jnp.bfloat16)


def pooled_rows(first, count, lo, hi, device, token, hid, flags=None):
    slot = token[...].reshape(1, ATOMS_DEV)[:, lo:hi] - device * TOK_DEV
    rows = lax.broadcasted_iota(jnp.int32, (count, hi - lo), 0) + first
    one_hot = jnp.where(rows == slot, 1.0, 0.0).astype(jnp.bfloat16)
    if flags is not None:
        last = lax.broadcasted_iota(jnp.int32, (count, NEXT), 0) == count - 1
        one_hot = jnp.concatenate([one_hot, jnp.where(last, flags, 0.0).astype(jnp.bfloat16)], axis=1)
        hi += NEXT
    return dot_nt(one_hot, hid[:, lo:hi])


def token_normed(pooled, gain):
    count = pooled[:, TW:]
    single = pooled[:, :TW] / jnp.concatenate([count] * 3, axis=1)
    centre = single - jnp.mean(single, axis=1, keepdims=True)
    variance = jnp.mean(centre * centre, axis=1, keepdims=True)
    return (centre * lax.rsqrt(variance + 1e-05) * gain).astype(jnp.bfloat16)


def embed_kernel(
    atoms, off_hbm, token_hbm, wq_hbm, wk_hbm, wv_hbm, w_out_hbm, w_token_hbm, gain_hbm, w_pair_hbm, w_outer_hbm,
    result,
    off, token, wq, wk, wv, w_out, w_token, gain, w_pair, w_outer,
    gathered0, gathered1, base,
    ext, keys, queries, values, att, hid, turned_atoms, w_out_t, w_token_t, w_right,
    note_out, note_in, block0, block1, left_all, left_in,
    own_sem, load_sem, halo_send, halo_recv,
    first_send, first_recv, local_sem, pass_send, pass_recv, left_send, left_recv, far_ready, left_ready, pass_ready,
):
    gathered, block = (gathered0, gathered1), (block0, block1)
    row = lax.axis_index("row")
    col = lax.axis_index("col")
    me = row * COLS + col
    before = lax.rem(me + DEVICES - 1, DEVICES)
    after = lax.rem(me + 1, DEVICES)
    slot = lax.rem(me, ROWS)
    my_y, my_z = lax.div(row, 2), lax.rem(row, 2)
    my_x, my_zh = lax.div(col, 8), lax.rem(lax.div(col, 2), 4)
    depth = 2 * my_zh + my_z
    group_col = lax.div(me, ROWS)
    relay_y = lax.rem(my_y + 6 + my_zh - 2 * my_z - lax.div(my_x, 2) + 2 * lax.rem(my_x, 2), 4)
    my_core = lax.rem(col, 2)
    target = (2 * relay_y + my_core) * COLS + group_col
    target_depth = 4 * my_z + 2 * lax.div(my_x, 2) + my_core

    def held_by(y, z):
        return 2 * lax.rem(y + 6 + my_zh - my_x + 2 * my_core, 4) + z

    held = held_by(my_y, my_z)
    source = ROWS * col + held
    source_depth = 2 * lax.div(held, 2) + lax.div(my_zh, 2)
    keeps = target == me
    peers = [(2, 1), (2, 0), (1, 1), (3, 1), (1, 0), (3, 0), (0, 1)]
    col_in = lax.rem(col, 8)
    is_head, is_leader, is_first, is_last = col_in == 1, col == 1, me == 0, me == DEVICES - 1
    parent = jnp.where(is_leader, 0, jnp.where(is_head, row * COLS + 1, me - col_in + 1))

    def count(condition):
        return jnp.where(condition, 1, 0)

    def signal(device, semaphore=None):
        pl.semaphore_signal(
            barrier if semaphore is None else semaphore, inc=1, device_id=place(device), device_id_type=MESH
        )

    barrier = pltpu.get_barrier_semaphore()
    @pl.when(jnp.logical_not(is_first))
    def _():
        signal(before)

    @pl.when(jnp.logical_not(is_last))
    def _():
        signal(after)

    own = [
        pltpu.make_async_copy(atoms.at[pl.ds(lo, 512)], ext.at[pl.ds(RIM + lo, 512)], own_sem.at[lo // 512])
        for lo in range(0, ATOMS_DEV, 512)
    ]
    for copy in own:
        copy.start()
    pieces = [
        (wq_hbm, wq), (wk_hbm, wk), (wv_hbm, wv), (off_hbm, off), (token_hbm, token),
        (w_out_hbm, w_out), (w_token_hbm, w_token), (gain_hbm, gain), (w_pair_hbm, w_pair),
        (w_outer_hbm, w_outer),
    ]
    loads = [pltpu.make_async_copy(a, b, load_sem.at[i]) for i, (a, b) in enumerate(pieces)]
    for load in loads:
        load.start()


    @pl.when(is_head)
    def _():
        signal(parent)

    arrivals = 2 - count(is_first) - count(is_last) + 8 * count(is_first) + 3 * count(is_leader)

    @pl.when((source != me) & (source_depth >= depth))
    def _():
        signal(source)

    @pl.when(jnp.logical_not(keeps) & (target_depth > depth))
    def _():
        signal(target)

    arrivals += count((source != me) & (source_depth < depth))
    arrivals += count(jnp.logical_not(keeps) & (target_depth <= depth))
    late_target = jnp.logical_not(keeps) & (target_depth > depth)

    def peer(i, j):
        return (2 * lax.rem(my_y + i, 4) + lax.rem(my_z + j, 2)) * COLS + col

    for i, j in peers:
        @pl.when(peer(i, j) > me)
        def _():
            signal(peer(i, j))
    arrivals += row
    child = jnp.logical_not(is_head | is_first)
    arrivals += count(child)
    children = 7 - count((row == 0) & is_leader)

    def each_child(act):
        for c in range(8):
            if c != 1:
                @pl.when(is_head & (me + c != 1))
                def _():
                    act(me + c - 1, 16 + c)

    def each_leader(act):
        @pl.when(is_first)
        def _():
            for r in range(ROWS):
                act(r * COLS + 1, r)

    def each_head(act):
        @pl.when(is_leader)
        def _():
            for x in range(1, 4):
                act(me + 8 * x, 8 + x)

    each_child(lambda to, _: signal(to))

    for load in loads[:3]:
        load.wait()

    one = lax.broadcasted_iota(jnp.int32, (CZ, CZ), 0) == lax.broadcasted_iota(jnp.int32, (CZ, CZ), 1)
    eye = jnp.where(one, 1.0, 0.0).astype(jnp.bfloat16)
    value_t = turned(wv)
    left_side = jnp.concatenate([turned(wq), value_t, eye], axis=0)
    hid[TW:, :] = jnp.ones((WIDE - TW, WIDTH), jnp.bfloat16)
    for j in range(2):
        values[j, AW:, :] = jnp.ones((16, WIDTH + GROUP), jnp.bfloat16)
    def keep_product(lo, size, product):
        for h in range(HEADS):
            rows = slice(32 * h, 32 * h + 32)
            for part in range(0, size, GROUP):
                q = product[rows, part : part + GROUP]
                if h % 2 == 1:
                    q = pltpu.roll(q, HALF, 1)
                queries[rows, lo + part : lo + part + GROUP] = q.astype(jnp.bfloat16)
        values[1, :AW, lo : lo + size] = product[AW : 2 * AW].astype(jnp.bfloat16)
        turned_atoms[:, lo : lo + size] = product[2 * AW :].astype(jnp.bfloat16)

    for lo in range(0, 512, 512):
        own[lo // 512].wait()
        x = ext[RIM + lo : RIM + lo + 512, :]
        keys[RIM + lo : RIM + lo + 512, :] = dot(x, wk[...]).astype(jnp.bfloat16)
        for part in range(0, 512, 256):
            keep_product(lo + part, 256, dot_nt(left_side, x[part : part + 256]))
    for load in loads[3:5]:
        load.wait()
    flags = token[...].reshape(1, ATOMS_DEV)[:, :NEXT] == me * TOK_DEV - 1
    upper = lax.broadcasted_iota(jnp.int32, (16, NEXT), 0) < 8
    note = jnp.where(upper, jnp.where(flags, 1.0, 0.0), off[0].astype(jnp.float32))
    note_out[...] = note.astype(jnp.bfloat16)
    ext[RIM + ATOMS_DEV + NEXT_USED :, :] = jnp.zeros((NEXT - NEXT_USED, AW), jnp.bfloat16)

    @pl.when(is_first)
    def _():
        ext[:RIM, :] = jnp.zeros((RIM, AW), jnp.bfloat16)

    @pl.when(is_last)
    def _():
        ext[RIM + ATOMS_DEV :, :] = jnp.zeros((NEXT, AW), jnp.bfloat16)
        note_in[...] = jnp.zeros((16, NEXT), jnp.bfloat16)

    pl.semaphore_wait(barrier, arrivals)

    to_after = pltpu.make_async_remote_copy(
        src_ref=atoms.at[pl.ds(ATOMS_DEV - RIM, RIM)], dst_ref=ext.at[pl.ds(0, RIM)],
        send_sem=halo_send.at[0], recv_sem=halo_recv.at[0],
        device_id=place(after), device_id_type=MESH,
    )
    to_before = [
        pltpu.make_async_remote_copy(
            src_ref=atoms.at[pl.ds(0, NEXT_USED)], dst_ref=ext.at[pl.ds(RIM + ATOMS_DEV, NEXT_USED)],
            send_sem=halo_send.at[1], recv_sem=halo_recv.at[1],
            device_id=place(before), device_id_type=MESH,
        ),
        pltpu.make_async_remote_copy(
            src_ref=note_out, dst_ref=note_in, send_sem=halo_send.at[2], recv_sem=halo_recv.at[2],
            device_id=place(before), device_id_type=MESH,
        ),
    ]

    @pl.when(jnp.logical_not(is_last))
    def _():
        to_after.start()

    @pl.when(jnp.logical_not(is_first))
    def _():
        for copy in to_before:
            copy.start()

    @pl.when((source != me) & (source_depth < depth))
    def _():
        signal(source, far_ready)

    @pl.when(child)
    def _():
        signal(parent, left_ready)

    for i, j in peers:
        @pl.when(peer(i, j) < me)
        def _():
            signal(peer(i, j), pass_ready)

    for lo in range(512, ATOMS_DEV, 512):
        own[lo // 512].wait()
        x = ext[RIM + lo : RIM + lo + 512, :]
        keys[RIM + lo : RIM + lo + 512, :] = dot(x, wk[...]).astype(jnp.bfloat16)
        for part in range(0, 512, 256):
            keep_product(lo + part, 256, dot_nt(left_side, x[part : part + 256]))
    for lo in range(128, ATOMS_DEV, 256):
        hi = min(lo + 256, ATOMS_DEV)
        values[0, :AW, lo:hi] = dot_nt(value_t, ext[lo:hi, :]).astype(jnp.bfloat16)
    pad = jnp.zeros((RIM, AW), jnp.bfloat16)
    rest = jnp.concatenate([ext[ATOMS_DEV : ATOMS_DEV + RIM, :], pad], axis=0)
    values[0, :AW, ATOMS_DEV : ATOMS_DEV + GROUP] = dot_nt(value_t, rest).astype(jnp.bfloat16)

    for load in loads[5:]:
        load.wait()
    for i in range(8):
        base[:CZ, CZ * i : CZ * i + CZ] = eye
    w_out_t[...] = turned(w_out)
    w_token_t[...] = turned(w_token)
    w_right[:CZ, :] = w_pair[CZ + CO : 2 * CZ + CO, :]
    for m in range(4):
        w_right[CZ + CO * m : CZ + CO * m + CO, :] = w_pair[2 * CZ + CO :, :]

    mixed = {}
    inner_units = attend(list(range(1, UNITS - 1)), me, off, note_in, keys, queries, values, att, mixed)

    def first_copy(part):
        return pltpu.make_async_remote_copy(
            src_ref=block[part], dst_ref=gathered[part].at[slot],
            send_sem=first_send.at[part], recv_sem=first_recv.at[part],
            device_id=place(target), device_id_type=MESH,
        )

    def local_copy(part):
        return pltpu.make_async_copy(block[part], gathered[part].at[slot], local_sem.at[part])

    def first_sends(part):
        @pl.when(jnp.logical_not(keeps))
        def _():
            first_copy(part).start()

        @pl.when(keeps)
        def _():
            local_copy(part).start()

    def pass_copy(part, i, j, holder):
        return pltpu.make_async_remote_copy(
            src_ref=gathered[part].at[holder], dst_ref=gathered[part].at[holder],
            send_sem=pass_send.at[part], recv_sem=pass_recv.at[part],
            device_id=place(peer(i, j)), device_id_type=MESH,
        )

    def pass_all(part):
        blocks = gathered[part].at[pl.ds(0, ROWS - 1)]
        return pltpu.make_async_remote_copy(
            src_ref=blocks, dst_ref=blocks, send_sem=pass_send.at[part], recv_sem=pass_recv.at[part],
            device_id=place(peer(0, 1)), device_id_type=MESH,
        )

    def pass_on(part):
        @pl.when(source != me)
        def _():
            pltpu.make_async_remote_copy(
                src_ref=block[part], dst_ref=gathered[part].at[held],
                send_sem=first_send.at[part], recv_sem=first_recv.at[part],
                device_id=place(source), device_id_type=MESH,
            ).wait_recv()

        @pl.when(source == me)
        def _():
            local_copy(part).wait()

        for i, j in peers:
            pass_copy(part, i, j, held).start()

    def finish(part, pooled):
        tokens = TOKENS[part]
        normed = token_normed(pooled, gain[...].reshape(1, TW).astype(jnp.float32))
        right = dot_nt(normed, w_right[...])
        lane = lax.broadcasted_iota(jnp.int32, (16, CZ), 1)
        packed = []
        for m in range(tokens // 16):
            rows = right[16 * m : 16 * m + 16, CZ:]
            if m % 4 == 0:
                packed.append(rows)
            else:
                packed[-1] = jnp.where(lane // CO == m % 4, rows, packed[-1])
        packed = jnp.concatenate(packed, axis=0)
        block[part][:tokens, :] = right[:, :CZ].astype(jnp.bfloat16)
        block[part][tokens:, :] = packed.astype(jnp.bfloat16)
        return normed

    def early_sends(part):
        @pl.when(jnp.logical_not(late_target))
        def _():
            first_sends(part)

    normed = []
    for part, (last, lo, hi, first, number, start, stop) in enumerate(INNER):
        for unit in inner_units:
            if unit == last:
                break
        hidden_rows(lo, hi, turned_atoms, att, w_out_t, w_token_t, hid)
        normed.append(finish(part, pooled_rows(first, number, start, stop, me, token, hid)))
        early_sends(part)

    @pl.when(jnp.logical_not(is_last))
    def _():
        for copy in to_before:
            copy.wait_recv()

    @pl.when(jnp.logical_not(is_first))
    def _():
        to_after.wait_recv()

    keys[:RIM, :] = dot(ext[:RIM, :], wk[...]).astype(jnp.bfloat16)
    values[0, :AW, :GROUP] = dot_nt(value_t, ext[:GROUP, :]).astype(jnp.bfloat16)
    x = ext[RIM + ATOMS_DEV :, :]
    keys[RIM + ATOMS_DEV :, :] = dot(x, wk[...]).astype(jnp.bfloat16)
    keep_product(ATOMS_DEV, NEXT, dot_nt(left_side, x))
    rest = jnp.concatenate([ext[ATOMS_DEV:, :], pad], axis=0)
    values[0, :AW, ATOMS_DEV:] = dot_nt(value_t, rest).astype(jnp.bfloat16)
    for _ in attend([0, UNITS, UNITS - 1], me, off, note_in, keys, queries, values, att, mixed):
        pass

    hidden_rows(0, GROUP, turned_atoms, att, w_out_t, w_token_t, hid)
    hidden_rows(ATOMS_DEV - GROUP, WIDTH, turned_atoms, att, w_out_t, w_token_t, hid)
    low = pooled_rows(0, EDGE, 0, 256, me, token, hid)
    flags = note_in[:1, :].astype(jnp.float32)
    high = pooled_rows(TOK_DEV - EDGE, EDGE, ATOMS_DEV - 256, ATOMS_DEV, me, token, hid, flags)
    outer = finish(PARTS - 1, jnp.concatenate([low, high], axis=0))

    early_sends(PARTS - 1)

    def left_copy(source, to, index):
        return pltpu.make_async_remote_copy(
            src_ref=source, dst_ref=left_in, send_sem=left_send.at[index], recv_sem=left_recv,
            device_id=place(to), device_id_type=MESH,
        )

    def left_to(child, index):
        return left_copy(left_all.at[index] if index < ROWS else left_in, child, index // 8)

    def left_sent(count, index):
        rows = left_all.at[pl.ds(0, count)]
        return pltpu.make_async_remote_copy(
            src_ref=rows, dst_ref=rows, send_sem=left_send.at[index], recv_sem=left_recv,
            device_id=place(parent), device_id_type=MESH,
        ).wait_send()

    @pl.when(is_first)
    def _():
        first_rows = jnp.concatenate([outer[:EDGE], normed[0][: HALF - EDGE]], axis=0)
        left = dot_nt(first_rows, w_pair[: 2 * CZ, :])
        for r in range(ROWS):
            rows = left[8 * r : 8 * r + 8]
            left_all[r] = jnp.concatenate([rows[:, :CZ], rows[:, CZ:]], axis=0).astype(jnp.bfloat16)
        left_in[...] = left_all[0]

    each_leader(lambda to, index: left_to(to, index).start())

    @pl.when(is_leader)
    def _():
        left_copy(left_in, parent, 0).wait_recv()

    each_head(lambda to, index: left_to(to, index).start())

    @pl.when(late_target)
    def _():
        pl.semaphore_wait(far_ready, 1)
        for part in range(PARTS):
            first_sends(part)

    @pl.when(is_head & jnp.logical_not(is_leader))
    def _():
        left_copy(left_in, parent, 0).wait_recv()

    @pl.when(is_head)
    def _():
        pl.semaphore_wait(left_ready, children)

    each_child(lambda to, index: left_to(to, index).start())
    @pl.when(row < ROWS - 1)
    def _():
        pl.semaphore_wait(pass_ready, ROWS - 1 - row)

    for part in range(PARTS):
        pass_on(part)

    @pl.when(child)
    def _():
        left_copy(left_in, parent, 0).wait_recv()

    mix_left(left_in, w_outer, base)
    left = left_in[:8, :].astype(jnp.float32)

    for part in range(PARTS):
        pass_all(part).wait_recv()
        pair_part(gathered[part], part, base, left, result)

    @pl.when(is_first)
    def _():
        left_sent(8, 0)

    @pl.when(is_leader)
    def _():
        left_sent(3, 1)

    @pl.when(is_head & (me != 1))
    def _():
        left_sent(7, 2)

    @pl.when(me == 1)
    def _():
        left_sent(6, 2)

    @pl.when(jnp.logical_not(is_last))
    def _():
        to_after.wait_send()

    @pl.when(jnp.logical_not(is_first))
    def _():
        for copy in to_before:
            copy.wait_send()

    for part in range(PARTS):
        pass_all(part).wait_send()

        @pl.when(jnp.logical_not(keeps))
        def _():
            first_copy(part).wait_send()


def mix_left(left_in, w_outer, base):
    outer = left_in[8:, :CO]
    spread = lax.broadcasted_iota(jnp.int32, (CO, CO * CO), 1) // CO
    spread = jnp.where(spread == lax.broadcasted_iota(jnp.int32, (CO, CO * CO), 0), 1.0, 0.0)
    wide = dot(outer, spread.astype(jnp.bfloat16))
    n = lax.broadcasted_iota(jnp.int32, (CO, CO * CO), 0)
    mine = lax.rem(lax.broadcasted_iota(jnp.int32, (CO, CO * CO), 1), CO) == n
    expanded = [jnp.where(mine, wide[i : i + 1], 0.0).astype(jnp.bfloat16) for i in range(8)]
    mixing = dot(jnp.concatenate(expanded, axis=0), w_outer[...]).astype(jnp.bfloat16)
    for i in range(8):
        for k in range(4):
            base[CZ + CO * k : CZ + CO * k + CO, CZ * i : CZ * i + CZ] = mixing[CO * i : CO * i + CO]


def packed_rows(tokens):
    return 16 * -(-tokens // 64)


def pair_part(gathered, part, base, left, result):
    tokens = TOKENS[part]
    lane = lax.broadcasted_iota(jnp.int32, (16, CZ), 1)
    pieces = []
    for k in range(ROWS):
        packed = gathered[k, tokens:, :].astype(jnp.float32)
        outer = [
            jnp.where(lane // CO == m % 4, packed[16 * (m // 4) : 16 * (m // 4) + 16], 0.0)
            for m in range(tokens // 16)
        ]
        outer = jnp.concatenate(outer, axis=0).astype(jnp.bfloat16)
        pieces.append(jnp.concatenate([gathered[k, :tokens, :], outer], axis=1))
    rows = jnp.concatenate(pieces, axis=0)
    for i in range(0, 8, 2):
        grid = dot(rows, base[:, CZ * i : CZ * i + 2 * CZ])
        for j in range(2):
            total = (grid[:, CZ * j : CZ * j + CZ] + left[i + j : i + j + 1]).astype(jnp.bfloat16)
            for k in range(ROWS):
                for first, to, size in SPANS[part]:
                    to += TOK_DEV * k
                    first += tokens * k
                    result[i + j, to : to + size, :] = total[first : first + size]


def body(
    atoms, window_offsets, atom_token, w_query, w_key, w_value, w_out, w_token, gain_token, w_pair, w_outer
):
    hbm = pl.BlockSpec(memory_space=pltpu.HBM)
    dma = pltpu.SemaphoreType.DMA
    bf16 = jnp.bfloat16
    return pl.pallas_call(
        embed_kernel,
        out_shape=pltpu.VMEM((8, ROWS * TOK_DEV, CZ), bf16),
        in_specs=[hbm] * 11,
        out_specs=pl.BlockSpec(memory_space=pltpu.VMEM),
        scratch_shapes=[
            pltpu.SMEM((ATOMS_DEV // QB,), jnp.int32),
            pltpu.VMEM((ATOMS_DEV,), jnp.int32),
            pltpu.VMEM((AW, AW), bf16),
            pltpu.VMEM((AW, AW), bf16),
            pltpu.VMEM((AW, AW), bf16),
            pltpu.VMEM((AW, AW), bf16),
            pltpu.VMEM((AW, TW), bf16),
            pltpu.VMEM((TW,), bf16),
            pltpu.VMEM((2 * CZ + 2 * CO, TW), bf16),
            pltpu.VMEM((CO * CO, CZ), bf16),
            *[pltpu.VMEM((ROWS, tokens + packed_rows(tokens), CZ), bf16) for tokens in TOKENS],
            pltpu.VMEM((2 * CZ, 8 * CZ), bf16),
            pltpu.VMEM((EXT, AW), bf16),
            pltpu.VMEM((EXT, AW), bf16),
            pltpu.VMEM((AW, WIDTH), bf16),
            pltpu.VMEM((2, AW + 16, WIDTH + GROUP), bf16),
            pltpu.VMEM((AW, WIDTH), bf16),
            pltpu.VMEM((WIDE, WIDTH), bf16),
            pltpu.VMEM((AW, WIDTH), bf16),
            pltpu.VMEM((AW, AW), bf16),
            pltpu.VMEM((TW, AW), bf16),
            pltpu.VMEM((2 * CZ, TW), bf16),
            pltpu.VMEM((16, NEXT), bf16),
            pltpu.VMEM((16, NEXT), bf16),
            *[pltpu.VMEM((tokens + packed_rows(tokens), CZ), bf16) for tokens in TOKENS],
            pltpu.VMEM((ROWS, 16, CZ), bf16),
            pltpu.VMEM((16, CZ), bf16),
            dma((3,)), dma((10,)), dma((3,)), dma((3,)),
            dma((PARTS,)), dma((PARTS,)), dma((PARTS,)), dma((PARTS,)), dma((PARTS,)), dma((3,)), dma,
            *[pltpu.SemaphoreType.REGULAR] * 3,
        ],
        compiler_params=pltpu.CompilerParams(
            collective_id=0, has_side_effects=True, vmem_limit_bytes=60 * 1024 * 1024
        ),
        name="embed",
    )(
        atoms, window_offsets, atom_token, w_query, w_key, w_value, w_out, w_token, gain_token, w_pair.T,
        w_outer,
    )


def solution(mesh):
    split = P(("row", "col"))
    placed = (P(("row", "col"), None), split, split) + (P(),) * 8
    return jax.shard_map(
        body, mesh=mesh, in_specs=placed, out_specs=P("row", "col", None), check_vma=False
    )
```
